256 devices in a mesh: gx: 2 (over x_hi), gy: 64 (over z, y, x_lo), gz: 2 (over core).
Axes of the slice: x: 4 (x_hi: 2, x_lo: 2; x = x_hi * 2 + x_lo), y: 4, z: 8, core: 2. Of those that a mesh axis runs over, the one named last changes fastest.
Arguments:
- adjoint_load: float32 [3, 16, 512, 256], P(None, 'gx', 'gy', 'gz'), may hold values from -6 to 6
- levels: int32 [8, 256, 128], P('gx', 'gy', 'gz'), may hold values from 0 to 15
- fine_stiffness: float32 [81, 81], replicated, may hold values from -0.025 to 2, as said below
- coarse_stiffness: float32 [24, 24], replicated, may hold values from -0.14 to 3.2, as said below
Outputs:
- preconditioned: float32 [3, 16, 512, 256], P(None, 'gx', 'gy', 'gz')
The draws below stay inside these ranges and needn't reach their ends.
Inputs may be any that keep to these rules, and one draw needn't show every extreme that they name: `fine_stiffness`: symmetric; off-diagonal entries are at most zero; each diagonal entry exceeds the sum of the magnitudes of the other entries of its row by a positive margin. `coarse_stiffness`: symmetric; off-diagonal entries are at most zero; each diagonal entry exceeds the sum of the magnitudes of the other entries of its row by a positive margin.
All inputs are finite; a program needn't handle non-finite values.
Results may differ from the reference program's by a relative error of at most 0.0003.
Values sent between devices are 32-bit elements; how exact they have to be, the bound alone decides.
No kernel may reach another device: no remote copies, remote signals or barrier semaphores. Data moves between devices by JAX's collectives and lax.ppermute only.
A program may use at most 64 MiB of HBM per device.

```python
import jax
import jax.numpy as jnp
from jax import lax

EX = 4
DEG = 4
DENSITY_LEVELS = 16
EDOF = 81
CDOF = 24
SPAN_ELEMENTS = 8
WIDTH_ELEMENTS = 256
DEPTH_ELEMENTS = 128
NX = 16
NY = 512
NZ = 256


def coupled_from(weights_raw, width_count):
    raw_weights = weights_raw / (width_count - 1)
    weights = 0.5 * (raw_weights + raw_weights.T)
    weights = weights * (1.0 - jnp.eye(width_count, dtype=jnp.float32))
    row_totals = jnp.sum(weights, axis=1)
    return jnp.diag(row_totals + 0.01) - weights


def coupled_block(key, width_count, low_bound, high_bound):
    raw_weights = jax.random.uniform(key, (width_count, width_count), jnp.float32, low_bound, high_bound)
    return coupled_from(raw_weights, width_count)


def draw_fine_stiffness(key, part):
    key = jax.random.fold_in(key, 11)
    return coupled_block(key, EDOF, 0.5, 1.5)


def draw_coarse_stiffness(key, part):
    key = jax.random.fold_in(key, 12)
    uniform_part = jax.random.uniform(key, (CDOF, CDOF), jnp.float32, 0.0, 1.0)
    return coupled_from(3.0 * uniform_part * uniform_part, CDOF)


def touch_ends(values, key, least, largest):
    dims = values.shape
    spot = [jax.random.randint(jax.random.fold_in(key, axis), (), 0, dims[axis]) for axis in range(len(dims))]
    values = values.at[tuple(spot)].set(least)
    longest = dims.index(max(dims))
    spot[longest] = (spot[longest] + 1) % dims[longest]
    return values.at[tuple(spot)].set(largest)


def steps_of(rng, shape, cuts, smallest, high):
    def one(position, blocks):
        draws = jax.random.uniform(jax.random.fold_in(jax.random.fold_in(rng, 6), position), (blocks,), jnp.float32, smallest / len(cuts), high / len(cuts))
        return jnp.repeat(jnp.exp(draws), shape[position] // blocks).reshape((-1,) + (1,) * (len(shape) - position - 1))

    loudness = one(*cuts[0])
    for cut in cuts[1:]:
        loudness = loudness * one(*cut)
    return loudness


def noise(stream_key, shape, width, reach, shards=(), held_as=jnp.bfloat16):
    values = width * jax.random.normal(stream_key, shape, jnp.float32)
    if shards:
        values = values * steps_of(stream_key, shape, shards, -0.22, 0.18)
    return jnp.clip(values, -reach, reach).astype(held_as)


def setup_inputs(seed: int = 0) -> dict:
    seeds = jax.random.split(jax.random.key(seed), 5)
    adjoint_load = noise(seeds[0], (3, NX, NY, NZ), 1.0, 6.0, ((1, 2), (2, 64), (3, 2)), jnp.float32)
    levels = touch_ends(jax.random.randint(seeds[1], (SPAN_ELEMENTS, WIDTH_ELEMENTS, DEPTH_ELEMENTS), 0, DENSITY_LEVELS), jax.random.fold_in(seeds[1], 1), 0, DENSITY_LEVELS - 1).astype(jnp.int32)
    fine_stiffness = draw_fine_stiffness(jax.random.fold_in(seeds[4], 71), 0)
    coarse_stiffness = draw_coarse_stiffness(jax.random.fold_in(seeds[4], 71), 0)
    return {"adjoint_load": adjoint_load, "levels": levels, "fine_stiffness": fine_stiffness, "coarse_stiffness": coarse_stiffness}


SPECTRUM_MID = 1.125
SPECTRUM_HALF = 0.875


def densities(levels):
    ratio = levels.astype(jnp.float32) / (DENSITY_LEVELS - 1)
    return 0.05 + 0.95 * ratio * ratio * ratio


def pad_axis(values, dimension, in_front, behind):
    config = [(0, 0)] * values.ndim
    config[dimension] = (in_front, behind)
    return jnp.pad(values, config)


def pad_upper(values):
    return jnp.pad(values, ((0, 0), (0, 1), (0, 1), (0, 1)))


def spread_axis(values, spacing):
    pieces = [values[:, offset] for offset in range(spacing + 1)]
    extent = pieces[0].shape[3]
    if spacing == 1:
        return pad_axis(pieces[0], 3, 0, 1) + pad_axis(pieces[1], 3, 1, 0)
    even_nodes = pad_axis(pieces[0], 3, 0, 1) + pad_axis(pieces[2], 3, 1, 0)
    woven_rows = jnp.stack([even_nodes[:, :, :, :extent], pieces[1]], axis=4)
    shape_out = list(even_nodes.shape)
    shape_out[3] = 2 * extent
    woven_rows = woven_rows.reshape(shape_out)
    return jnp.concatenate([woven_rows, even_nodes[:, :, :, extent:]], axis=3)


def assemble(products, spacing, moduli):
    span_cells, width_cells, depth_cells = moduli.shape
    corners = spacing + 1
    values = products.reshape(3, corners, corners, corners, span_cells, width_cells, depth_cells)
    for sweep_axis in range(3):
        values = spread_axis(values, spacing)
    return values


def element_vectors(nodal, spacing, moduli):
    span_cells, width_cells, depth_cells = moduli.shape
    gathered = []
    for lag_span in range(spacing + 1):
        for lag_width in range(spacing + 1):
            for lag_depth in range(spacing + 1):
                gathered.append(nodal[:, lag_span:lag_span + spacing * span_cells:spacing,
                                      lag_width:lag_width + spacing * width_cells:spacing,
                                      lag_depth:lag_depth + spacing * depth_cells:spacing])
    stacked = jnp.stack(gathered, axis=1)
    return stacked.reshape(3 * (spacing + 1) ** 3, span_cells * width_cells * depth_cells)


def element_apply(extended, moduli, stiffness, spacing):
    element_local = element_vectors(extended, spacing, moduli)
    products = jnp.dot(stiffness, element_local, precision=lax.Precision.HIGHEST,
                       preferred_element_type=jnp.float32)
    return assemble(products * moduli.reshape(1, -1), spacing, moduli)


def element_diagonal(stiffness, moduli, spacing):
    products = jnp.diagonal(stiffness).reshape(-1, 1) * moduli.reshape(1, -1)
    return assemble(products, spacing, moduli)


def by_slabs(operator_maker, moduli, spacing):
    slab_count = moduli.shape[0] // EX
    slab_nodes = spacing * EX

    def one_slab(slab_index):
        leading_row = (slab_index * EX).astype(jnp.int32)
        part_moduli = lax.dynamic_slice_in_dim(moduli, leading_row, EX, 0)
        return operator_maker(leading_row, part_moduli)

    results = lax.map(one_slab, jnp.arange(slab_count, dtype=jnp.int32))
    interior = results[:, :, :slab_nodes]
    carried = results[:, :, slab_nodes]
    interior = interior.at[1:, :, 0].add(carried[:-1])
    interior = jnp.moveaxis(interior, 0, 1)
    shape_in = interior.shape
    joined = interior.reshape(shape_in[0], shape_in[1] * shape_in[2], shape_in[3], shape_in[4])
    return joined[:, :, :-1, :-1]


def global_apply(nodal, moduli, stiffness, spacing):
    extended = pad_upper(nodal)

    def operator_maker(leading_row, part_moduli):
        window = lax.dynamic_slice_in_dim(extended, (leading_row * spacing).astype(jnp.int32),
                                          spacing * EX + 1, 1)
        return element_apply(window, part_moduli, stiffness, spacing)

    return by_slabs(operator_maker, moduli, spacing)


def global_diagonal(stiffness, moduli, spacing):
    def operator_maker(leading_row, part_moduli):
        return element_diagonal(stiffness, part_moduli, spacing)

    return by_slabs(operator_maker, moduli, spacing)


def restrict_axis(values, dimension):
    length_now = values.shape[dimension]
    even_nodes = lax.slice_in_dim(values, 0, length_now, 2, dimension)
    odd_nodes = lax.slice_in_dim(values, 1, length_now, 2, dimension)
    return even_nodes + 0.5 * pad_axis(odd_nodes, dimension, 0, 1) + 0.5 * pad_axis(odd_nodes, dimension, 1, 0)


def interpolate_axis(values, dimension):
    length_now = values.shape[dimension] - 1
    left_nodes = lax.slice_in_dim(values, 0, length_now, 1, dimension)
    right_nodes = lax.slice_in_dim(values, 1, length_now + 1, 1, dimension)
    woven_rows = jnp.stack([left_nodes, 0.5 * (left_nodes + right_nodes)], axis=dimension + 1)
    shape_out = list(left_nodes.shape)
    shape_out[dimension] = 2 * length_now
    return woven_rows.reshape(shape_out)


def restrict(extended):
    for dimension in (1, 2, 3):
        extended = restrict_axis(extended, dimension)
    return extended


def prolong(extended):
    for dimension in (1, 2, 3):
        extended = interpolate_axis(extended, dimension)
    return extended


def chebyshev(operator, diagonal, residual, keep_last):
    sigma_ratio = SPECTRUM_MID / SPECTRUM_HALF
    rho_now = 1.0 / sigma_ratio
    inverse = 1.0 / diagonal
    direction = inverse * residual / SPECTRUM_MID
    solution = jnp.zeros_like(residual)
    for sweep_index in range(DEG):
        solution = solution + direction
        if sweep_index < DEG - 1 or keep_last:
            residual = residual - operator(direction)
        if sweep_index < DEG - 1:
            rho_next = 1.0 / (2.0 * sigma_ratio - rho_now)
            direction = (rho_next * rho_now) * direction + (2.0 * rho_next / SPECTRUM_HALF) * (inverse * residual)
            rho_now = rho_next
    return solution, residual


def reference(adjoint_load, levels, fine_stiffness, coarse_stiffness):
    moduli = densities(levels)
    diag_fine = global_diagonal(fine_stiffness, moduli, 2)
    diag_coarse = global_diagonal(coarse_stiffness, moduli, 1)

    def fine_operator(nodal):
        return global_apply(nodal, moduli, fine_stiffness, 2)

    def coarse_operator(nodal):
        return global_apply(nodal, moduli, coarse_stiffness, 1)

    smoothed_field, leftover = chebyshev(fine_operator, diag_fine, adjoint_load, True)
    coarse_load = restrict(pad_upper(leftover))[:, :-1, :-1, :-1]
    coarse_fix, unused = chebyshev(coarse_operator, diag_coarse, coarse_load, False)
    corrected = smoothed_field + prolong(pad_upper(coarse_fix))
    post_fix, unused = chebyshev(fine_operator, diag_fine, adjoint_load - fine_operator(corrected), False)
    return corrected + post_fix
```

```python
import functools

import jax
import jax.numpy as jnp
import numpy as np
from jax import lax
from jax.experimental import pallas as pl
from jax.experimental.pallas import tpu as pltpu
from jax.sharding import PartitionSpec as P

DEG = 4
DENSITY_LEVELS = 16
MID = 1.125
HALF = 0.875

F32 = jnp.float32
BF16 = jnp.bfloat16
EXACT = lax.Precision.HIGHEST

OWN = 4
REACH = 12
ROWS = OWN + 2 * REACH
LANES = 1024
WIDE = LANES + 128
PACK = 104


def node_row(group, row):
    px, py = ((0, 0), (1, 0), (0, 1))[group]
    if row < 6:
        return row % 3, px, py, row // 3
    return group, 1, 1, row - 6


FINE_IN = [(g, sx, sy) for sx, sy, groups in ((0, 0, (0, 1, 2)), (1, 0, (0, 2)), (0, 1, (0, 1)), (1, 1, (0,))) for g in groups]
SHIFTS = [(0, 0), (1, 0), (0, 1), (1, 1)]


def fine_place(group, row, sx, sy, sz):
    p, px, py, pz = node_row(group, row)
    if (sx and px) or (sy and py) or (sz and pz):
        return None
    return 27 * p + 9 * (px + 2 * sx) + 3 * (py + 2 * sy) + pz + 2 * sz


def coarse_place(row, sx, sy, sz):
    return 8 * row + 4 * sx + 2 * sy + sz if row < 3 else None


def fine_selectors():
    out_rows = np.zeros((128, 81), np.float32)
    in_rows = np.zeros((256, 81), np.float32)
    at = 0
    for sz in (0, 1):
        for g, sx, sy in FINE_IN:
            for row in range(8):
                place = fine_place(g, row, sx, sy, sz)
                if place is not None:
                    out_rows[at + row, place] = 1.0
            at += 8
    at = 0
    for g, sx, sy in FINE_IN:
        for sz in (0, 1):
            for row in range(8):
                place = fine_place(g, row, sx, sy, sz)
                if place is not None:
                    in_rows[at + row, place] = 1.0
                    in_rows[at + 8 + row, place] = 1.0
            at += 16
    return out_rows, in_rows


def coarse_selectors():
    out_rows = np.zeros((64, 24), np.float32)
    in_rows = np.zeros((128, 24), np.float32)
    at = 0
    for sz in (0, 1):
        for sx, sy in SHIFTS:
            for row in range(3):
                out_rows[at + row, coarse_place(row, sx, sy, sz)] = 1.0
            at += 8
    at = 0
    for sx, sy in SHIFTS:
        for sz in (0, 1):
            for row in range(3):
                in_rows[at + row, coarse_place(row, sx, sy, sz)] = 1.0
                in_rows[at + 8 + row, coarse_place(row, sx, sy, sz)] = 1.0
            at += 16
    return out_rows, in_rows


def weight_along(parity, shift):
    if parity == 0:
        return 1.0 if shift == 0 else 0.0
    return 0.5


def prolong_weights():
    weights = np.zeros((24, 128), np.float32)
    at = 0
    for sx, sy in SHIFTS:
        for sz in (0, 1):
            for g in range(3):
                for row in range(8):
                    p, px, py, pz = node_row(g, row)
                    w = weight_along(px, sx) * weight_along(py, sy) * weight_along(pz, sz)
                    weights[8 * g + row, at + p] = w
                    weights[8 * g + row, at + 8 + p] = w
            at += 16
    return weights


def restrict_weights():
    weights = np.zeros((64, 48), np.float32)
    at = 0
    for sz in (0, 1):
        for sx, sy in SHIFTS:
            for g in range(3):
                for row in range(8):
                    p, px, py, pz = node_row(g, row)
                    w = weight_along(px, sx) * weight_along(py, sy) * weight_along(pz, sz)
                    weights[at + p, 16 * g + row] = w
                    weights[at + p, 16 * g + 8 + row] = w
            at += 8
    return weights


def row_shuffle():
    shuffle = np.zeros((96, 96), np.float32)
    for y in range(4):
        for g in range(3):
            for row in range(8):
                p, px, py, pz = node_row(g, row)
                shuffle[24 * y + 8 * g + row, pz * 48 + p * 16 + px * 8 + 2 * y + py] = 1.0
    return shuffle


def exact_dot(a, b):
    return jnp.dot(a, b, precision=EXACT, preferred_element_type=F32)


def pack_kernel(place_ref, load_ref, load_other_ref, levels_ref, levels_other_ref, shuffle_ref, out_ref):
    gz = place_ref[2]

    def spread(half):
        row = lax.broadcasted_iota(jnp.int32, (128, 256), 0)
        col = lax.broadcasted_iota(jnp.int32, (128, 256), 1)
        source = 2 * (col % 128) + col // 128
        return (source == row + 128 * half).astype(F32)

    def widen(half):
        row = lax.broadcasted_iota(jnp.int32, (64, 128), 0)
        col = lax.broadcasted_iota(jnp.int32, (64, 128), 1)
        return (col == row + 64 * half).astype(F32)

    own_spread, other_spread = spread(gz), spread(1 - gz)
    own_widen, other_widen = widen(gz), widen(1 - gz)
    for x in range(4):
        lanes = slice(128 * x, 128 * x + 128)
        own = load_ref[:, 2 * x : 2 * x + 2].reshape(48, 128)
        other = load_other_ref[:, 2 * x : 2 * x + 2].reshape(48, 128)
        parted = exact_dot(own, own_spread) + exact_dot(other, other_spread)
        stacked = jnp.concatenate([parted[:, :128], parted[:, 128:]], axis=0)
        out_ref[0:96, lanes] = exact_dot(shuffle_ref[...], stacked)
        level = exact_dot(levels_ref[x].astype(F32), own_widen) + exact_dot(
            levels_other_ref[x].astype(F32), other_widen
        )
        ratio = level / (DENSITY_LEVELS - 1)
        out_ref[96:100, lanes] = 0.05 + 0.95 * ratio * ratio * ratio
        out_ref[100:104, lanes] = jnp.zeros((4, 128), F32)


def split(values):
    high = values.astype(BF16).astype(F32)
    return jnp.concatenate([high, values - high], axis=0).astype(BF16)


def roll_tiles(values, step):
    tiles = []
    for t in range(values.shape[1] // 128):
        tile = values[:, 128 * t : 128 * t + 128]
        lane = lax.broadcasted_iota(jnp.int32, tile.shape, 1)
        if step == 1:
            tiles.append(jnp.where(lane < 127, pltpu.roll(tile, 127, 1), 0.0))
        else:
            tiles.append(jnp.where(lane > 0, pltpu.roll(tile, 1, 1), 0.0))
    return tiles[0] if len(tiles) == 1 else jnp.concatenate(tiles, axis=1)


def hi_lo_weights(weights):
    high = weights.astype(BF16).astype(F32)
    col = lax.broadcasted_iota(jnp.int32, weights.shape, 1)
    low = jnp.where(col % 16 < 8, weights - high, 0.0)
    return jnp.concatenate([high, low], axis=0).astype(BF16)


def scaled(values, moduli):
    rows, lanes = values.shape
    return (values.reshape(rows // 8, 8, lanes) * moduli[None]).reshape(rows, lanes)


def cycle_kernel(place_ref, *refs):
    blocks = refs[:14]
    (fine_ref, coarse_ref, fine_diag_ref, coarse_diag_ref, prolong_ref, restrict_ref, shuffle_ref) = refs[14:21]
    out_ref = refs[21]
    (load, moduli, inverse, res, step, total, fine_x, carry,
     fine_w, coarse_w, c_inverse, c_res, c_step, c_total, coarse_x, c_carry) = refs[22:]
    gx, gy, gz = place_ref[0], place_ref[1], place_ref[2]
    y_first = gy * OWN - REACH
    y_count = lax.mul(place_ref[3], OWN)

    def valid(y):
        at = y_first + y
        return jnp.where((at >= 0) & (at < y_count), 1.0, 0.0).astype(F32)

    own, own_x = blocks[0], blocks[1]
    side = 1 - 2 * gz
    spots = [(own, 0, gx), (own_x, 0, 1 - gx)]
    for s in (1, 2, 3):
        a, ax, za, zax = blocks[4 * s - 2 : 4 * s + 2]
        spots += [(a, -s * side, gx), (ax, -s * side, 1 - gx), (za, s * side, gx), (zax, s * side, 1 - gx)]
    for ref, offset, half in spots:
        first = REACH + OWN * offset
        lanes = pl.ds(pl.multiple_of(half * 512, 512), 512)
        for y in range(OWN):
            load[first + y, :, lanes] = ref[24 * y : 24 * y + 24, :]
            moduli[first + y, :, lanes] = jnp.broadcast_to(ref[96 + y : 97 + y, :], (8, 512))

    fine_w[...] = hi_lo_weights(fine_ref[...])
    coarse_w[...] = hi_lo_weights(coarse_ref[...])

    def clear_tail(y, _):
        fine_x[y, :, LANES:] = jnp.zeros((96, 128), BF16)
        coarse_x[y, :, LANES:] = jnp.zeros((32, 128), BF16)
        return 0

    lax.fori_loop(0, ROWS, clear_tail, 0)

    def store_fine(y, lanes, values):
        for g in range(3):
            part = values[8 * g : 8 * g + 8]
            fine_x[y, 32 * g : 32 * g + 16, lanes] = split(part)
            fine_x[y, 32 * g + 16 : 32 * g + 32, lanes] = split(roll_tiles(part, 1))

    def store_coarse(y, lanes, values):
        coarse_x[y, 0:16, lanes] = split(values)
        coarse_x[y, 16:32, lanes] = split(roll_tiles(values, 1))

    def fine_products(y, low):
        here, there = slice(low, low + 256), slice(low + 128, low + 384)
        operand = jnp.concatenate(
            [
                fine_x[y, :, here],
                fine_x[y, 0:32, there],
                fine_x[y, 64:96, there],
                fine_x[y + 1, 0:64, here],
                fine_x[y + 1, 0:32, there],
            ],
            axis=0,
        )
        products = jnp.dot(fine_w[...], operand, preferred_element_type=F32)
        return products[:128] + products[128:]

    def coarse_products(y, low):
        here, there = slice(low, low + 256), slice(low + 128, low + 384)
        operand = jnp.concatenate(
            [coarse_x[y, :, here], coarse_x[y, :, there], coarse_x[y + 1, :, here], coarse_x[y + 1, :, there]],
            axis=0,
        )
        return operand

    def pushed(before, values):
        return jnp.concatenate([before, values[:, :128]], axis=1)

    def fine_sweep(first, last, products_of, finish):
        carry[...] = jnp.zeros_like(carry)

        def row(y, _):
            before = [(jnp.zeros((16, 128), F32), jnp.zeros((8, 128), F32))] * 2
            for n in range(4):
                lanes = slice(256 * n, 256 * n + 256)
                values = scaled(products_of(y, 256 * n), moduli[y, :, lanes])
                sums = []
                for z in range(2):
                    v = values[64 * z : 64 * z + 64]
                    old = carry[16 * z : 16 * z + 16, lanes]
                    along_x = pushed(before[z][0], v[24:40])
                    along_xy = pushed(before[z][1], v[56:64])
                    before[z] = (v[24:40, 128:], v[56:64, 128:])
                    sums.append(
                        jnp.concatenate(
                            [v[0:8] + along_x[0:8] + old[0:8], v[8:16] + old[8:16], v[16:24] + along_x[8:16]], axis=0
                        )
                    )
                    carry[16 * z : 16 * z + 16, lanes] = jnp.concatenate([v[40:48] + along_xy, v[48:56]], axis=0)
                finish(y, lanes, sums[0] + roll_tiles(sums[1], -1))
            return 0

        lax.fori_loop(first, last, row, 0)

    def coarse_sweep(first, last, products_of, scale, finish):
        c_carry[...] = jnp.zeros_like(c_carry)

        def row(y, _):
            before = [(jnp.zeros((8, 128), F32), jnp.zeros((8, 128), F32))] * 2
            for n in range(4):
                lanes = slice(256 * n, 256 * n + 256)
                values = products_of(y, 256 * n)
                if scale:
                    values = scaled(values, moduli[y, :, lanes])
                sums = []
                for z in range(2):
                    v = values[32 * z : 32 * z + 32]
                    old = c_carry[8 * z : 8 * z + 8, lanes]
                    sums.append(v[0:8] + pushed(before[z][0], v[8:16]) + old)
                    c_carry[8 * z : 8 * z + 8, lanes] = v[16:24] + pushed(before[z][1], v[24:32])
                    before[z] = (v[8:16, 128:], v[24:32, 128:])
                finish(y, lanes, sums[0] + roll_tiles(sums[1], -1))
            return 0

        lax.fori_loop(first, last, row, 0)

    def over_moduli(diag_ref):
        def products_of(y, low):
            diag = diag_ref[...]
            return jnp.concatenate([diag, diag], axis=1)

        return products_of

    def start_fine(y, lanes, diag):
        ok = valid(y)
        inv = ok / jnp.where(ok > 0, diag, 1.0)
        inverse[y, :, lanes] = inv
        r = load[y, :, lanes]
        d = inv * r * (1.0 / MID)
        res[y, :, lanes] = r
        step[y, :, lanes] = d
        total[y, :, lanes] = d
        store_fine(y, lanes, d)

    o = REACH
    fine_sweep(o - 12, o + 15, over_moduli(fine_diag_ref), start_fine)

    sigma = MID / HALF
    rhos = [1.0 / sigma]
    for _ in range(DEG - 1):
        rhos.append(1.0 / (2.0 * sigma - rhos[-1]))
    factors = [(rhos[s + 1] * rhos[s], 2.0 * rhos[s + 1] / HALF) for s in range(DEG - 1)]

    def smooth_fine(keep, gain, with_operand):
        def finish(y, lanes, sums):
            r = res[y, :, lanes] - sums
            d = keep * step[y, :, lanes] + gain * (inverse[y, :, lanes] * r)
            res[y, :, lanes] = r
            step[y, :, lanes] = d
            total[y, :, lanes] = total[y, :, lanes] + d
            if with_operand:
                store_fine(y, lanes, d)

        return finish

    for s in range(DEG - 1):
        fine_sweep(o - 11 + s, o + 14 - s, fine_products, smooth_fine(*factors[s], True))

    def leave(y, lanes, sums):
        left = (res[y, :, lanes] - sums) * valid(y)
        for g in range(3):
            fine_x[y, 16 * g : 16 * g + 16, lanes] = split(left[8 * g : 8 * g + 8])

    fine_sweep(o - 8, o + 11, fine_products, leave)

    def restricted(y, low):
        return jnp.dot(restrict_ref[...], fine_x[y, 0:48, low : low + 256], preferred_element_type=F32)

    def keep_load(y, lanes, sums):
        c_res[y, :, lanes] = sums

    coarse_sweep(o - 8, o + 11, restricted, False, keep_load)

    def start_coarse(y, lanes, diag):
        ok = valid(y)
        used = (lax.broadcasted_iota(jnp.int32, diag.shape, 0) < 3) & (ok > 0)
        inv = jnp.where(used, 1.0 / jnp.where(used, diag, 1.0), 0.0)
        c_inverse[y, :, lanes] = inv
        d = inv * c_res[y, :, lanes] * (1.0 / MID)
        c_step[y, :, lanes] = d
        c_total[y, :, lanes] = d
        store_coarse(y, lanes, d)

    coarse_sweep(o - 8, o + 11, over_moduli(coarse_diag_ref), True, start_coarse)

    def coarse_product(y, low):
        products = jnp.dot(coarse_w[...], coarse_products(y, low), preferred_element_type=F32)
        return products[:64] + products[64:]

    def smooth_coarse(keep, gain, last):
        def finish(y, lanes, sums):
            r = c_res[y, :, lanes] - sums
            d = keep * c_step[y, :, lanes] + gain * (c_inverse[y, :, lanes] * r)
            t = c_total[y, :, lanes] + d
            c_res[y, :, lanes] = r
            c_step[y, :, lanes] = d
            c_total[y, :, lanes] = t
            store_coarse(y, lanes, t if last else d)

        return finish

    for s in range(DEG - 1):
        coarse_sweep(o - 7 + s, o + 10 - s, coarse_product, True, smooth_coarse(*factors[s], s == DEG - 2))

    def correct(y, _):
        for n in range(4):
            lanes = slice(256 * n, 256 * n + 256)
            t = total[y, :, lanes] + jnp.dot(prolong_ref[...], coarse_products(y, 256 * n), preferred_element_type=F32)
            total[y, :, lanes] = t
            store_fine(y, lanes, t)
        return 0

    lax.fori_loop(o - 4, o + 8, correct, 0)

    def restart(y, lanes, sums):
        r = load[y, :, lanes] - sums
        d = inverse[y, :, lanes] * r * (1.0 / MID)
        res[y, :, lanes] = r
        step[y, :, lanes] = d
        total[y, :, lanes] = total[y, :, lanes] + d
        store_fine(y, lanes, d)

    fine_sweep(o - 4, o + 7, fine_products, restart)
    for s in range(DEG - 1):
        fine_sweep(o - 3 + s, o + 6 - s, fine_products, smooth_fine(*factors[s], s < DEG - 2))

    row = lax.broadcasted_iota(jnp.int32, (128, 128), 0)
    col = lax.broadcasted_iota(jnp.int32, (128, 128), 1)
    mine = row == 64 * gz + col // 2
    weave = [(mine & (col % 2 == pz)).astype(F32) for pz in (0, 1)]
    for x in range(4):
        lanes = pl.ds(pl.multiple_of(gx * 512 + 128 * x, 128), 128)
        rows = total[REACH : REACH + OWN, :, lanes].reshape(96, 128)
        back = lax.dot_general(
            shuffle_ref[...], rows, (((0,), (0,)), ((), ())), precision=EXACT, preferred_element_type=F32
        )
        woven = exact_dot(back[0:48], weave[0]) + exact_dot(back[48:96], weave[1])
        out_ref[:, 2 * x : 2 * x + 2] = woven.reshape(3, 2, 8, 128)


def per_device(adjoint_load, levels, fine_stiffness, coarse_stiffness):
    count = lax.axis_size("gy")
    place = jnp.stack(
        [lax.axis_index("gx"), lax.axis_index("gy"), lax.axis_index("gz"), jnp.int32(count)]
    ).astype(jnp.int32)

    def swap(value, axis):
        return lax.ppermute(value, axis, [(0, 1), (1, 0)])

    def sided(value, steps):
        pairs = [(2 * i, 2 * (i + steps)) for i in range(count - steps)]
        pairs += [(2 * (i + steps) + 1, 2 * i + 1) for i in range(count - steps)]
        return lax.ppermute(value, ("gy", "gz"), pairs)

    whole = pl.BlockSpec(memory_space=pltpu.VMEM)
    scalars = pl.BlockSpec(memory_space=pltpu.SMEM)
    shuffle = jnp.asarray(row_shuffle())
    own = pl.pallas_call(
        pack_kernel,
        out_shape=jax.ShapeDtypeStruct((PACK, 512), F32),
        in_specs=[scalars] + [whole] * 5,
        out_specs=whole,
        name="pack",
    )(place, adjoint_load, swap(adjoint_load, "gz"), levels, swap(levels, "gz"), shuffle)

    blocks = [own, swap(own, "gx")]
    for s in (1, 2, 3):
        a = sided(own, s)
        ax = swap(a, "gx")
        blocks += [a, ax, swap(a, "gz"), swap(ax, "gz")]

    fine_out, fine_in = fine_selectors()
    coarse_out, coarse_in = coarse_selectors()
    fine = exact_dot(exact_dot(jnp.asarray(fine_out), fine_stiffness), jnp.asarray(fine_in.T))
    coarse = exact_dot(exact_dot(jnp.asarray(coarse_out), coarse_stiffness), jnp.asarray(coarse_in.T))
    fine_diag = exact_dot(jnp.asarray(fine_out), jnp.broadcast_to(jnp.diagonal(fine_stiffness)[:, None], (81, 128)))
    coarse_diag = exact_dot(
        jnp.asarray(coarse_out), jnp.broadcast_to(jnp.diagonal(coarse_stiffness)[:, None], (24, 128))
    )

    scratch = [
        pltpu.VMEM((ROWS, 24, LANES), F32),
        pltpu.VMEM((ROWS, 8, LANES), F32),
        pltpu.VMEM((ROWS, 24, LANES), F32),
        pltpu.VMEM((ROWS, 24, LANES), F32),
        pltpu.VMEM((ROWS, 24, LANES), F32),
        pltpu.VMEM((ROWS, 24, LANES), F32),
        pltpu.VMEM((ROWS, 96, WIDE), BF16),
        pltpu.VMEM((32, LANES), F32),
        pltpu.VMEM((256, 256), BF16),
        pltpu.VMEM((128, 128), BF16),
        pltpu.VMEM((ROWS, 8, LANES), F32),
        pltpu.VMEM((ROWS, 8, LANES), F32),
        pltpu.VMEM((ROWS, 8, LANES), F32),
        pltpu.VMEM((ROWS, 8, LANES), F32),
        pltpu.VMEM((ROWS, 32, WIDE), BF16),
        pltpu.VMEM((16, LANES), F32),
    ]
    return pl.pallas_call(
        cycle_kernel,
        out_shape=jax.ShapeDtypeStruct(adjoint_load.shape, F32),
        in_specs=[scalars] + [whole] * 21,
        out_specs=whole,
        scratch_shapes=scratch,
        compiler_params=pltpu.CompilerParams(vmem_limit_bytes=56 * 1024 * 1024),
        name="cycle",
    )(
        place,
        *blocks,
        fine,
        coarse,
        fine_diag,
        coarse_diag,
        jnp.asarray(prolong_weights(), dtype=BF16),
        jnp.asarray(restrict_weights(), dtype=BF16),
        shuffle,
    )


def solution(mesh):
    return jax.shard_map(
        per_device,
        mesh=mesh,
        in_specs=(P(None, "gx", "gy", "gz"), P("gx", "gy", "gz"), P(), P()),
        out_specs=P(None, "gx", "gy", "gz"),
        check_vma=False,
    )
```

```python
import jax
import jax.numpy as jnp
import numpy as np
from jax import lax
from jax.experimental import pallas as pl
from jax.experimental.pallas import tpu as pltpu
from jax.sharding import PartitionSpec as P

DEG = 4
DENSITY_LEVELS = 16
MID = 1.125
HALF = 0.875

F32 = jnp.float32
BF16 = jnp.bfloat16
EXACT = lax.Precision.HIGHEST

OWN = 4
SIDE = 4
FAR = 8
ROWS = OWN + 2 * SIDE
C_ROWS = OWN + 2 * FAR
LANES = 1024
WIDE = LANES + 128
AHEAD = 2
PACK = 104
NOTE = 24


def node_row(group, row):
    px, py = ((0, 0), (1, 0), (0, 1))[group]
    if row < 6:
        return row % 3, px, py, row // 3
    return group, 1, 1, row - 6


FINE_IN = [(g, sx, sy) for sx, sy, groups in ((0, 0, (0, 1, 2)), (1, 0, (0, 2)), (0, 1, (0, 1)), (1, 1, (0,))) for g in groups]
SHIFTS = [(0, 0), (1, 0), (0, 1), (1, 1)]


def fine_place(group, row, sx, sy, sz):
    p, px, py, pz = node_row(group, row)
    if (sx and px) or (sy and py) or (sz and pz):
        return None
    return 27 * p + 9 * (px + 2 * sx) + 3 * (py + 2 * sy) + pz + 2 * sz


def coarse_place(row, sx, sy, sz):
    return 8 * row + 4 * sx + 2 * sy + sz if row < 3 else None


def fine_selectors():
    out_rows = np.zeros((128, 81), np.float32)
    in_rows = np.zeros((256, 81), np.float32)
    at = 0
    for sz in (0, 1):
        for g, sx, sy in FINE_IN:
            for row in range(8):
                place = fine_place(g, row, sx, sy, sz)
                if place is not None:
                    out_rows[at + row, place] = 1.0
            at += 8
    at = 0
    for g, sx, sy in FINE_IN:
        for sz in (0, 1):
            for row in range(8):
                place = fine_place(g, row, sx, sy, sz)
                if place is not None:
                    in_rows[at + row, place] = 1.0
                    in_rows[at + 8 + row, place] = 1.0
            at += 16
    return out_rows, in_rows


def coarse_selectors():
    out_rows = np.zeros((64, 24), np.float32)
    in_rows = np.zeros((128, 24), np.float32)
    at = 0
    for sz in (0, 1):
        for sx, sy in SHIFTS:
            for row in range(3):
                out_rows[at + row, coarse_place(row, sx, sy, sz)] = 1.0
            at += 8
    at = 0
    for sx, sy in SHIFTS:
        for sz in (0, 1):
            for row in range(3):
                in_rows[at + row, coarse_place(row, sx, sy, sz)] = 1.0
                in_rows[at + 8 + row, coarse_place(row, sx, sy, sz)] = 1.0
            at += 16
    return out_rows, in_rows


def weight_along(parity, shift):
    if parity == 0:
        return 1.0 if shift == 0 else 0.0
    return 0.5


def prolong_weights():
    weights = np.zeros((24, 128), np.float32)
    at = 0
    for sx, sy in SHIFTS:
        for sz in (0, 1):
            for g in range(3):
                for row in range(8):
                    p, px, py, pz = node_row(g, row)
                    w = weight_along(px, sx) * weight_along(py, sy) * weight_along(pz, sz)
                    weights[8 * g + row, at + p] = w
                    weights[8 * g + row, at + 8 + p] = w
            at += 16
    return weights


def restrict_weights():
    weights = np.zeros((64, 48), np.float32)
    at = 0
    for sz in (0, 1):
        for sx, sy in SHIFTS:
            for g in range(3):
                for row in range(8):
                    p, px, py, pz = node_row(g, row)
                    w = weight_along(px, sx) * weight_along(py, sy) * weight_along(pz, sz)
                    weights[at + p, 16 * g + row] = w
                    weights[at + p, 16 * g + 8 + row] = w
            at += 8
    return weights


def row_shuffle():
    shuffle = np.zeros((96, 96), np.float32)
    for y in range(4):
        for g in range(3):
            for row in range(8):
                p, px, py, pz = node_row(g, row)
                shuffle[24 * y + 8 * g + row, pz * 48 + p * 16 + px * 8 + 2 * y + py] = 1.0
    return shuffle


def diag_selectors():
    fine = np.zeros((32, 16, 81), np.float32)
    coarse = np.zeros((32, 16, 24), np.float32)
    for at in range(8):
        sy, sx, sz = at // 4, at // 2 % 2, at % 2
        for half in (0, 8):
            for g in range(3):
                for row in range(8):
                    place = fine_place(g, row, sx, sy, sz)
                    if place is not None:
                        fine[8 * g + row, half + at, place] = 1.0
            for row in range(3):
                coarse[24 + row, half + at, coarse_place(row, sx, sy, sz)] = 1.0
    return fine.reshape(512, 81), coarse.reshape(512, 24)


def exact_dot(a, b):
    return jnp.dot(a, b, precision=EXACT, preferred_element_type=F32)


def pack_kernel(place_ref, load_ref, load_other_ref, levels_ref, levels_other_ref, shuffle_ref, out_ref):
    gz = place_ref[2]

    def spread(half):
        row = lax.broadcasted_iota(jnp.int32, (128, 256), 0)
        col = lax.broadcasted_iota(jnp.int32, (128, 256), 1)
        source = 2 * (col % 128) + col // 128
        return (source == row + 128 * half).astype(F32)

    def widen(half):
        row = lax.broadcasted_iota(jnp.int32, (64, 128), 0)
        col = lax.broadcasted_iota(jnp.int32, (64, 128), 1)
        return (col == row + 64 * half).astype(F32)

    own_spread, other_spread = spread(gz), spread(1 - gz)
    own_widen, other_widen = widen(gz), widen(1 - gz)
    for x in range(4):
        lanes = slice(128 * x, 128 * x + 128)
        own = load_ref[:, 2 * x : 2 * x + 2].reshape(48, 128)
        other = load_other_ref[:, 2 * x : 2 * x + 2].reshape(48, 128)
        parted = exact_dot(own, own_spread) + exact_dot(other, other_spread)
        stacked = jnp.concatenate([parted[:, :128], parted[:, 128:]], axis=0)
        out_ref[0:96, lanes] = exact_dot(shuffle_ref[...], stacked)
        level = exact_dot(levels_ref[x].astype(F32), own_widen) + exact_dot(
            levels_other_ref[x].astype(F32), other_widen
        )
        ratio = level / (DENSITY_LEVELS - 1)
        out_ref[96:100, lanes] = 0.05 + 0.95 * ratio * ratio * ratio
        out_ref[100:104, lanes] = jnp.zeros((4, 128), F32)


def split(values):
    high = values.astype(BF16).astype(F32)
    return jnp.concatenate([high, values - high], axis=0).astype(BF16)


def roll_tiles(values, step):
    tiles = []
    for t in range(values.shape[1] // 128):
        tile = values[:, 128 * t : 128 * t + 128]
        lane = lax.broadcasted_iota(jnp.int32, tile.shape, 1)
        if step == 1:
            tiles.append(jnp.where(lane < 127, pltpu.roll(tile, 127, 1), 0.0))
        else:
            tiles.append(jnp.where(lane > 0, pltpu.roll(tile, 1, 1), 0.0))
    return tiles[0] if len(tiles) == 1 else jnp.concatenate(tiles, axis=1)


def hi_lo_weights(weights):
    high = weights.astype(BF16).astype(F32)
    col = lax.broadcasted_iota(jnp.int32, weights.shape, 1)
    low = jnp.where(col % 16 < 8, weights - high, 0.0)
    return jnp.concatenate([high, low], axis=0).astype(BF16)


def scaled(values, moduli):
    rows, lanes = values.shape
    return (values.reshape(rows // 8, 8, lanes) * moduli[None]).reshape(rows, lanes)


def joined(sweeps):
    rows, factors = [], []
    for first, last, keep, gain, flag in sweeps:
        rows += list(range(first, last))
        factors += [(keep, gain, flag)] * (last - first)
    return rows, factors


def schedules():
    sigma = MID / HALF
    rhos = [1.0 / sigma]
    for _ in range(DEG - 1):
        rhos.append(1.0 / (2.0 * sigma - rhos[-1]))
    smooth = [(rhos[s + 1] * rhos[s], 2.0 * rhos[s + 1] / HALF) for s in range(DEG - 1)]
    o, c = SIDE, FAR
    runs = {
        "start": (joined([(0, ROWS, 0.0, 0.0, 0.0)]), 3),
        "before": (joined([(o - 3 + s, o + 7 - s, *smooth[s], 0.0) for s in range(DEG - 1)]), 6),
        "leave": (joined([(o, o + 4, 0.0, 0.0, 0.0)]), 4),
        "coarse_start": (joined([(c - 7, c + 11, 0.0, 0.0, 0.0)]), 3),
        "coarse": (joined([(c - 7 + s, c + 10 - s, *smooth[s], float(s == DEG - 2)) for s in range(DEG - 1)]), 9),
        "correct": (joined([(o - 4, o + 8, 0.0, 0.0, 0.0)]), 3),
        "after": (
            joined(
                [(o - 4, o + 7, 0.0, 1.0 / MID, 0.0)]
                + [(o - 3 + s, o + 6 - s + (s == DEG - 2), *smooth[s], 0.0) for s in range(DEG - 1)]
            ),
            3,
        ),
    }
    rows, factors, at = [], [], {}
    for name, ((run_rows, run_factors), together) in runs.items():
        assert len(run_rows) % together == 0
        assert together % (AHEAD + 1) == 0 or len(run_rows) == together
        at[name] = (len(rows), len(run_rows), together)
        rows += run_rows + [o] * AHEAD
        factors += run_factors + [(0.0, 0.0, 0.0)] * AHEAD
    return np.asarray(rows, np.int32), np.asarray(factors, np.float32).reshape(-1), at


CHUNKS = [(256 * n, slice(256 * n, 256 * n + 256)) for n in range(4)]


def pushed(before, values):
    return jnp.concatenate([before, values[:, :128]], axis=1)


def store_fine(fine_x, y, lanes, values):
    for g in range(3):
        part = values[8 * g : 8 * g + 8]
        fine_x[y, 32 * g : 32 * g + 16, lanes] = split(part)
        fine_x[y, 32 * g + 16 : 32 * g + 32, lanes] = split(roll_tiles(part, 1))


def store_coarse(coarse_x, y, lanes, values):
    coarse_x[y, 0:16, lanes] = split(values)
    coarse_x[y, 16:32, lanes] = split(roll_tiles(values, 1))


def pipeline(rows_ref, prods, name, issue, finish):
    first, count, together = schedules()[2][name]
    for u in range(AHEAD):
        issue(rows_ref[first + u], prods[u])

    def some(i, _):
        t = first + together * i
        for u in range(together):
            issue(rows_ref[t + u + AHEAD], prods[(u + AHEAD) % len(prods)])
            finish(t + u, rows_ref[t + u], prods[u % len(prods)])
        return 0

    lax.fori_loop(0, count // together, some, 0)


def fine_issue(fine_w, fine_x):
    def issue(y, prod):
        for low, lanes in CHUNKS:
            there = slice(low + 128, low + 384)
            operand = jnp.concatenate(
                [
                    fine_x[y, :, lanes],
                    fine_x[y, 0:32, there],
                    fine_x[y, 64:96, there],
                    fine_x[y + 1, 0:64, lanes],
                    fine_x[y + 1, 0:32, there],
                ],
                axis=0,
            )
            products = jnp.dot(fine_w[...], operand, preferred_element_type=F32)
            prod[:, lanes] = products[:128] + products[128:]

    return issue


def fine_finish(moduli, offset, carry, use):
    def finish(t, y, prod):
        before = [(jnp.zeros((16, 128), F32), jnp.zeros((8, 128), F32))] * 2
        for low, lanes in CHUNKS:
            m = moduli[y + offset, :, lanes]
            sums = []
            for z in range(2):
                v = scaled(prod[64 * z : 64 * z + 64, lanes], m)
                old = carry[16 * z : 16 * z + 16, lanes]
                along_x = pushed(before[z][0], v[24:40])
                along_xy = pushed(before[z][1], v[56:64])
                before[z] = (v[24:40, 128:], v[56:64, 128:])
                sums.append(
                    jnp.concatenate(
                        [v[0:8] + along_x[0:8] + old[0:8], v[8:16] + old[8:16], v[16:24] + along_x[8:16]], axis=0
                    )
                )
                carry[16 * z : 16 * z + 16, lanes] = jnp.concatenate([v[40:48] + along_xy, v[48:56]], axis=0)
            use(t, y, lanes, sums[0] + roll_tiles(sums[1], -1))

    return finish


def coarse_finish(moduli, carry, use):
    def finish(t, y, prod):
        before = [(jnp.zeros((8, 128), F32), jnp.zeros((8, 128), F32))] * 2
        for low, lanes in CHUNKS:
            sums = []
            for z in range(2):
                v = prod[32 * z : 32 * z + 32, lanes]
                if moduli is not None:
                    v = scaled(v, moduli[y, :, lanes])
                old = carry[8 * z : 8 * z + 8, lanes]
                sums.append(v[0:8] + pushed(before[z][0], v[8:16]) + old)
                carry[8 * z : 8 * z + 8, lanes] = v[16:24] + pushed(before[z][1], v[24:32])
                before[z] = (v[8:16, 128:], v[24:32, 128:])
            use(t, y, lanes, sums[0] + roll_tiles(sums[1], -1))

    return finish


def smooth_fine(factors_ref, inverse, res, step, total, fine_x):
    def use(t, y, lanes, sums):
        keep, gain = factors_ref[3 * t], factors_ref[3 * t + 1]
        r = res[y, :, lanes] - sums
        d = keep * step[y, :, lanes] + gain * (inverse[y, :, lanes] * r)
        res[y, :, lanes] = r
        step[y, :, lanes] = d
        total[y, :, lanes] = total[y, :, lanes] + d
        store_fine(fine_x, y, lanes, d)

    return use


def diag_issue(diag_w, moduli, count):
    def issue(y, prod):
        spot = lax.broadcasted_iota(jnp.int32, (8, 256), 0)
        before = jnp.zeros((8, 128), F32)
        for low, lanes in CHUNKS:
            near = jnp.where(spot < 4, moduli[y, :, lanes], moduli[jnp.maximum(y - 1, 0), :, lanes])
            moved = pushed(before, near)
            before = near[:, 128:]
            around = jnp.where(spot % 4 < 2, near, moved)
            around = jnp.where(spot % 2 < 1, around, roll_tiles(around, -1))
            products = jnp.dot(diag_w[...], split(around), preferred_element_type=F32)
            prod[0:count, lanes] = products[:count] + products[count:]

    return issue


def clear_tail(ref, rows):
    def clear(y, _):
        ref[y, :, LANES:] = jnp.zeros((ref.shape[1], 128), BF16)
        return 0

    lax.fori_loop(0, rows, clear, 0)


def validity(place_ref, ahead):
    first, count = place_ref[1] * OWN - ahead, place_ref[3] * OWN

    def valid(y):
        return jnp.where((first + y >= 0) & (first + y < count), 1.0, 0.0).astype(F32)

    return valid


def before_kernel(place_ref, rows_ref, factors_ref, *refs):
    blocks = refs[:6]
    fine_ref, diag_ref, restrict_ref = refs[6:9]
    load, moduli, inverse, smoothed, note = refs[9:14]
    res, step, total, fine_x, carry, fine_w, diag_w, c_carry, *prods = refs[14:]
    gx, gz = place_ref[0], place_ref[2]
    valid = validity(place_ref, SIDE)
    o = SIDE

    own, own_x, a, ax, za, zax = blocks
    side = 1 - 2 * gz
    for ref, offset, half in [
        (own, 0, gx), (own_x, 0, 1 - gx), (a, -side, gx), (ax, -side, 1 - gx), (za, side, gx), (zax, side, 1 - gx)
    ]:
        first = o + OWN * offset
        lanes = pl.ds(pl.multiple_of(half * 512, 512), 512)
        for y in range(OWN):
            load[first + y, :, lanes] = ref[24 * y : 24 * y + 24, :]
            moduli[first + y, :, lanes] = jnp.broadcast_to(ref[96 + y : 97 + y, :], (8, 512))

    fine_w[...] = hi_lo_weights(fine_ref[...])
    diag_w[...] = hi_lo_weights(diag_ref[0:24, :])
    clear_tail(fine_x, ROWS)
    carry[...] = jnp.zeros_like(carry)

    def start(t, y, prod):
        ok = valid(y)
        for low, lanes in CHUNKS:
            inv = ok / (prod[0:24, lanes] + (1.0 - ok))
            r = load[y, :, lanes]
            d = inv * r * (1.0 / MID)
            inverse[y, :, lanes] = inv
            res[y, :, lanes] = r
            step[y, :, lanes] = d
            total[y, :, lanes] = d
            store_fine(fine_x, y, lanes, d)

    pipeline(rows_ref, prods, "start", diag_issue(diag_w, moduli, 24), start)
    issue = fine_issue(fine_w, fine_x)
    use = smooth_fine(factors_ref, inverse, res, step, total, fine_x)
    pipeline(rows_ref, prods, "before", issue, fine_finish(moduli, 0, carry, use))
    for y in range(OWN):
        smoothed[24 * y : 24 * y + 24, :] = total[o + y]

    carry[...] = jnp.zeros_like(carry)

    def store_left(y, lanes, left):
        for g in range(3):
            fine_x[y, 16 * g : 16 * g + 16, lanes] = split(left[8 * g : 8 * g + 8])

    def leave(t, y, lanes, sums):
        store_left(y, lanes, res[y, :, lanes] - sums)

    pipeline(rows_ref, prods, "leave", issue, fine_finish(moduli, 0, carry, leave))
    for low, lanes in CHUNKS:
        last = carry[0:16, lanes] + roll_tiles(carry[16:32, lanes], -1)
        last = jnp.concatenate([last, jnp.zeros((8, 256), F32)], axis=0)
        store_left(o + OWN, lanes, -last * valid(o + OWN))

    c_carry[...] = jnp.zeros_like(c_carry)
    for j in range(OWN + 1):
        prod = prods[j % len(prods)]
        for low, lanes in CHUNKS:
            prod[0:64, lanes] = jnp.dot(
                restrict_ref[...], fine_x[o + j, 0:48, lanes], preferred_element_type=F32
            )

        def keep(t, y, lanes, sums, j=j):
            note[3 * j : 3 * j + 3, lanes] = sums[0:3]

        coarse_finish(None, c_carry, keep)(0, o + j, prod)
    for y in range(OWN):
        note[16 + y : 17 + y, :] = moduli[o + y, 0:1, :]


def after_kernel(place_ref, rows_ref, factors_ref, *refs):
    note, m1, zm1, m2, zm2, s0, s1, zs1, load, near_moduli, inverse = refs[:11]
    fine_ref, coarse_ref, diag_ref, prolong_ref, shuffle_ref = refs[11:16]
    out_ref = refs[16]
    (res, step, total, fine_x, carry, fine_w, moduli, coarse_w, diag_w,
     c_inverse, c_res, c_step, c_total, coarse_x, c_carry, *prods) = refs[17:]
    gx, gz = place_ref[0], place_ref[2]
    o, c = SIDE, FAR
    valid = validity(place_ref, FAR)
    side = 1 - 2 * gz

    for y in range(ROWS):
        moduli[c - o + y] = near_moduli[y]
    c_res[...] = jnp.zeros_like(c_res)
    for ref, offset in [(m2, -2 * side), (zm2, 2 * side)]:
        first = c + OWN * offset
        for y in range(OWN):
            moduli[first + y] = jnp.broadcast_to(ref[16 + y : 17 + y, :], (8, LANES))
    for ref, offset in [(note, 0), (m1, -side), (zm1, side), (m2, -2 * side), (zm2, 2 * side)]:
        first = c + OWN * offset
        for y in range(OWN + 1):
            at = jnp.minimum(first + y, C_ROWS)
            c_res[at, 0:3, :] = c_res[at, 0:3, :] + ref[3 * y : 3 * y + 3, :]
    for ref, offset in [(s0, 0), (s1, -side), (zs1, side)]:
        for y in range(OWN):
            total[o + OWN * offset + y] = ref[24 * y : 24 * y + 24, :]

    fine_w[...] = hi_lo_weights(fine_ref[...])
    coarse_w[...] = hi_lo_weights(coarse_ref[...])
    diag_w[...] = hi_lo_weights(diag_ref[24:32, :])
    clear_tail(fine_x, ROWS)
    clear_tail(coarse_x, C_ROWS)
    carry[...] = jnp.zeros_like(carry)
    c_carry[...] = jnp.zeros_like(c_carry)

    def start(t, y, prod):
        ok = valid(y)
        for low, lanes in CHUNKS:
            used = lax.broadcasted_iota(jnp.int32, (8, 256), 0) < 3
            inv = jnp.where(used, ok / (prod[0:8, lanes] + (1.0 - ok)), 0.0)
            d = inv * c_res[y, :, lanes] * (1.0 / MID)
            c_inverse[y, :, lanes] = inv
            c_step[y, :, lanes] = d
            c_total[y, :, lanes] = d
            store_coarse(coarse_x, y, lanes, d)

    pipeline(rows_ref, prods, "coarse_start", diag_issue(diag_w, moduli, 8), start)

    def coarse_operand(y, low, lanes):
        there = slice(low + 128, low + 384)
        return jnp.concatenate(
            [coarse_x[y, :, lanes], coarse_x[y, :, there], coarse_x[y + 1, :, lanes], coarse_x[y + 1, :, there]],
            axis=0,
        )

    def coarse_issue(y, prod):
        for low, lanes in CHUNKS:
            products = jnp.dot(coarse_w[...], coarse_operand(y, low, lanes), preferred_element_type=F32)
            prod[0:64, lanes] = products[:64] + products[64:]

    def smooth_coarse(t, y, lanes, sums):
        keep, gain, last = factors_ref[3 * t], factors_ref[3 * t + 1], factors_ref[3 * t + 2]
        r = c_res[y, :, lanes] - sums
        d = keep * c_step[y, :, lanes] + gain * (c_inverse[y, :, lanes] * r)
        so_far = c_total[y, :, lanes]
        c_res[y, :, lanes] = r
        c_step[y, :, lanes] = d
        c_total[y, :, lanes] = so_far + d
        store_coarse(coarse_x, y, lanes, d + last * so_far)

    pipeline(rows_ref, prods, "coarse", coarse_issue, coarse_finish(moduli, c_carry, smooth_coarse))

    def correct_issue(y, prod):
        for low, lanes in CHUNKS:
            prod[0:24, lanes] = jnp.dot(
                prolong_ref[...], coarse_operand(y + (c - o), low, lanes), preferred_element_type=F32
            )

    def correct(t, y, prod):
        for low, lanes in CHUNKS:
            corrected = total[y, :, lanes] + prod[0:24, lanes]
            total[y, :, lanes] = corrected
            res[y, :, lanes] = load[y, :, lanes]
            step[y, :, lanes] = jnp.zeros((24, 256), F32)
            store_fine(fine_x, y, lanes, corrected)

    pipeline(rows_ref, prods, "correct", correct_issue, correct)
    use = smooth_fine(factors_ref, inverse, res, step, total, fine_x)
    pipeline(rows_ref, prods, "after", fine_issue(fine_w, fine_x), fine_finish(moduli, c - o, carry, use))

    row = lax.broadcasted_iota(jnp.int32, (128, 128), 0)
    col = lax.broadcasted_iota(jnp.int32, (128, 128), 1)
    mine = row == 64 * gz + col // 2
    weave = [(mine & (col % 2 == pz)).astype(F32) for pz in (0, 1)]
    for x in range(4):
        lanes = pl.ds(pl.multiple_of(gx * 512 + 128 * x, 128), 128)
        rows = total[o : o + OWN, :, lanes].reshape(96, 128)
        back = lax.dot_general(
            shuffle_ref[...], rows, (((0,), (0,)), ((), ())), precision=EXACT, preferred_element_type=F32
        )
        woven = exact_dot(back[0:48], weave[0]) + exact_dot(back[48:96], weave[1])
        out_ref[:, 2 * x : 2 * x + 2] = woven.reshape(3, 2, 8, 128)


def per_device(adjoint_load, levels, fine_stiffness, coarse_stiffness):
    count = lax.axis_size("gy")
    place = jnp.stack(
        [lax.axis_index("gx"), lax.axis_index("gy"), lax.axis_index("gz"), jnp.int32(count)]
    ).astype(jnp.int32)

    def swap(value, axis):
        return lax.ppermute(value, axis, [(0, 1), (1, 0)])

    def sided(value, steps):
        pairs = [(2 * i, 2 * (i + steps)) for i in range(count - steps)]
        pairs += [(2 * (i + steps) + 1, 2 * i + 1) for i in range(count - steps)]
        return lax.ppermute(value, ("gy", "gz"), pairs)

    whole = pl.BlockSpec(memory_space=pltpu.VMEM)
    scalars = pl.BlockSpec(memory_space=pltpu.SMEM)
    shuffle = jnp.asarray(row_shuffle())
    own = pl.pallas_call(
        pack_kernel,
        out_shape=jax.ShapeDtypeStruct((PACK, 512), F32),
        in_specs=[scalars] + [whole] * 5,
        out_specs=whole,
        name="pack",
    )(place, adjoint_load, swap(adjoint_load, "gz"), levels, swap(levels, "gz"), shuffle)

    a = sided(own, 1)
    own_x = swap(own, "gx")
    ax = swap(a, "gx")
    blocks = [own, own_x, a, ax, swap(a, "gz"), swap(ax, "gz")]

    fine_out, fine_in = fine_selectors()
    coarse_out, coarse_in = coarse_selectors()
    fine = exact_dot(exact_dot(jnp.asarray(fine_out), fine_stiffness), jnp.asarray(fine_in.T))
    coarse = exact_dot(exact_dot(jnp.asarray(coarse_out), coarse_stiffness), jnp.asarray(coarse_in.T))
    fine_at, coarse_at = diag_selectors()
    diag = jnp.sum(jnp.asarray(fine_at) * jnp.diagonal(fine_stiffness), axis=1)
    diag = diag + jnp.sum(jnp.asarray(coarse_at) * jnp.diagonal(coarse_stiffness), axis=1)
    rows, factors, _ = schedules()

    rows, factors = jnp.asarray(rows), jnp.asarray(factors)
    diag = diag.reshape(32, 16)

    def held(count, height=24):
        return pltpu.VMEM((count, height, LANES), F32)

    fine_scratch = [
        held(ROWS),
        held(ROWS),
        held(ROWS),
        pltpu.VMEM((ROWS + 1, 96, WIDE), BF16),
        pltpu.VMEM((32, LANES), F32),
        pltpu.VMEM((256, 256), BF16),
    ]
    prods = [pltpu.VMEM((128, LANES), F32)] * (AHEAD + 1)
    limit = pltpu.CompilerParams(vmem_limit_bytes=56 * 1024 * 1024)
    load, moduli, inverse, smoothed, note = pl.pallas_call(
        before_kernel,
        out_shape=[
            jax.ShapeDtypeStruct(shape, F32)
            for shape in [(ROWS, 24, LANES), (ROWS, 8, LANES), (ROWS, 24, LANES), (24 * OWN, LANES), (NOTE, LANES)]
        ],
        in_specs=[scalars] * 3 + [whole] * 9,
        out_specs=[whole] * 5,
        scratch_shapes=fine_scratch
        + [
            pltpu.VMEM((48, 16), BF16),
            pltpu.VMEM((16, LANES), F32),
            *prods,
        ],
        compiler_params=limit,
        name="before",
    )(place, rows, factors, *blocks, fine, diag, jnp.asarray(restrict_weights(), dtype=BF16))

    m1, m2 = sided(note, 1), sided(note, 2)
    s1 = sided(smoothed, 1)
    notes = [note, m1, swap(m1, "gz"), m2, swap(m2, "gz")]
    return pl.pallas_call(
        after_kernel,
        out_shape=jax.ShapeDtypeStruct(adjoint_load.shape, F32),
        in_specs=[scalars] * 3 + [whole] * 16,
        out_specs=whole,
        scratch_shapes=fine_scratch
        + [
            held(C_ROWS, 8),
            pltpu.VMEM((128, 128), BF16),
            pltpu.VMEM((16, 16), BF16),
            held(C_ROWS, 8),
            held(C_ROWS + 1, 8),
            held(C_ROWS, 8),
            held(C_ROWS, 8),
            pltpu.VMEM((C_ROWS + 1, 32, WIDE), BF16),
            pltpu.VMEM((16, LANES), F32),
            *prods,
        ],
        compiler_params=limit,
        name="after",
    )(
        place,
        rows,
        factors,
        *notes,
        smoothed,
        s1,
        swap(s1, "gz"),
        load,
        moduli,
        inverse,
        fine,
        coarse,
        diag,
        jnp.asarray(prolong_weights(), dtype=BF16),
        shuffle,
    )


def solution(mesh):
    return jax.shard_map(
        per_device,
        mesh=mesh,
        in_specs=(P(None, "gx", "gy", "gz"), P("gx", "gy", "gz"), P(), P()),
        out_specs=P(None, "gx", "gy", "gz"),
        check_vma=False,
    )
```

```python
import jax
import jax.numpy as jnp
import numpy as np
from jax import lax
from jax.experimental import pallas as pl
from jax.experimental.pallas import tpu as pltpu
from jax.sharding import PartitionSpec as P

DEG = 4
DENSITY_LEVELS = 16
MID = 1.125
HALF = 0.875

F32 = jnp.float32
BF16 = jnp.bfloat16

OWN = 4
SIDE = 4
FAR = 8
ROWS = OWN + 2 * SIDE
C_ROWS = OWN + 2 * FAR
LANES = 1024
WIDE = LANES + 128
AHEAD = 2
PART = 56
PACK = 104
NOTE = 24


def node_row(group, row):
    px, py = ((0, 0), (1, 0), (0, 1))[group]
    if row < 6:
        return row % 3, px, py, row // 3
    return group, 1, 1, row - 6


FINE_IN = [(g, sx, sy) for sx, sy, groups in ((0, 0, (0, 1, 2)), (1, 0, (0, 2)), (0, 1, (0, 1)), (1, 1, (0,))) for g in groups]
SHIFTS = [(0, 0), (1, 0), (0, 1), (1, 1)]


def fine_place(group, row, sx, sy, sz):
    p, px, py, pz = node_row(group, row)
    if (sx and px) or (sy and py) or (sz and pz):
        return None
    return 27 * p + 9 * (px + 2 * sx) + 3 * (py + 2 * sy) + pz + 2 * sz


def coarse_place(row, sx, sy, sz):
    return 8 * row + 4 * sx + 2 * sy + sz if row < 3 else None


def fine_selectors():
    out_rows = np.zeros((128, 81), np.float32)
    in_rows = np.zeros((256, 81), np.float32)
    at = 0
    for sz in (0, 1):
        for g, sx, sy in FINE_IN:
            for row in range(8):
                place = fine_place(g, row, sx, sy, sz)
                if place is not None:
                    out_rows[at + row, place] = 1.0
            at += 8
    at = 0
    for g, sx, sy in FINE_IN:
        for sz in (0, 1):
            for row in range(8):
                place = fine_place(g, row, sx, sy, sz)
                if place is not None:
                    in_rows[at + row, place] = 1.0
                    in_rows[at + 8 + row, place] = 1.0
            at += 16
    return out_rows, in_rows


def coarse_selectors():
    out_rows = np.zeros((32, 24), np.float32)
    in_rows = np.zeros((64, 24), np.float32)
    for at, (sx, sy) in enumerate(SHIFTS):
        for sz in (0, 1):
            for row in range(3):
                place = coarse_place(row, sx, sy, sz)
                out_rows[8 * at + 3 * sz + row, place] = 1.0
                in_rows[[16 * at + 3 * sz + row, 16 * at + 8 + 3 * sz + row], place] = 1.0
    return out_rows, in_rows


def weight_along(parity, shift):
    if parity == 0:
        return 1.0 if shift == 0 else 0.0
    return 0.5


def transfer_weights():
    prolong = np.zeros((24, 64), np.float32)
    restrict = np.zeros((32, 48), np.float32)
    for at, (sx, sy) in enumerate(SHIFTS):
        for sz in (0, 1):
            for g in range(3):
                for row in range(8):
                    p, px, py, pz = node_row(g, row)
                    w = weight_along(px, sx) * weight_along(py, sy) * weight_along(pz, sz)
                    prolong[8 * g + row, [16 * at + 3 * sz + p, 16 * at + 8 + 3 * sz + p]] = w
                    restrict[8 * at + 3 * sz + p, [16 * g + row, 16 * g + 8 + row]] = w
    return prolong, restrict


def row_shuffle():
    shuffle = np.zeros((96, 96), np.float32)
    for y in range(4):
        for g in range(3):
            for row in range(8):
                p, px, py, pz = node_row(g, row)
                shuffle[24 * y + 8 * g + row, pz * 48 + p * 16 + px * 8 + 2 * y + py] = 1.0
    return np.concatenate([shuffle, shuffle], axis=1)


def diag_selectors():
    fine_rows, fine_at = np.zeros((24, 81), np.float32), np.zeros((81, 16), np.float32)
    coarse_rows, coarse_at = np.zeros((8, 24), np.float32), np.zeros((24, 16), np.float32)
    for at in range(8):
        sy, sx, sz = at // 4, at // 2 % 2, at % 2
        for g in range(3):
            for row in range(8):
                place = fine_place(g, row, sx, sy, sz)
                if place is not None:
                    fine_rows[8 * g + row, place] = 1.0
                    fine_at[place, [at, at + 8]] = 1.0
        for row in range(3):
            place = coarse_place(row, sx, sy, sz)
            coarse_rows[row, place] = 1.0
            coarse_at[place, [at, at + 8]] = 1.0
    return fine_rows, fine_at, coarse_rows, coarse_at


def laid_out(parts):
    places, at = {}, 0
    for name, (rows, columns) in parts.items():
        places[name] = (at, rows, columns)
        at += -(-rows // 16) * 16
    return places, at


def constants():
    fine_out, fine_in = fine_selectors()
    coarse_out, coarse_in = coarse_selectors()
    fine_rows, fine_at, coarse_rows, coarse_at = diag_selectors()
    prolong, restrict = transfer_weights()
    return {
        "fine_out": fine_out, "fine_in": fine_in.T, "fine_rows": fine_rows, "fine_at": fine_at,
        "coarse_out": coarse_out, "coarse_in": coarse_in.T, "coarse_rows": coarse_rows, "coarse_at": coarse_at,
        "restrict": restrict, "prolong": prolong, "shuffle": row_shuffle(),
    }


CARDS, CARD_ROWS = laid_out({name: value.shape for name, value in constants().items()})
BOOKS = [
    laid_out({"fine": (256, 256), "fine_diag": (48, 16), "restrict": (32, 48)}),
    laid_out({"coarse": (64, 64), "coarse_diag": (16, 16)}),
    laid_out({"fine": (256, 256), "prolong": (24, 64), "shuffle": (96, 192)}),
]


def cards():
    sheet = np.zeros((CARD_ROWS, 256), np.float32)
    for name, value in constants().items():
        first, rows, columns = CARDS[name]
        sheet[first : first + rows, :columns] = value
    return jnp.asarray(sheet, dtype=BF16)


class Part:
    def __init__(self, ref, places, name):
        first, rows, columns = places[name]
        self.ref, self.at = ref, (slice(first, first + rows), slice(0, columns))

    def __getitem__(self, _):
        return self.ref[self.at]

    def __setitem__(self, _, values):
        self.ref[self.at] = values


def halves(values):
    high = values.astype(BF16).astype(F32)
    return high, (values - high).astype(BF16).astype(F32)


def fetched(copies, sems, first=0):
    started = [pltpu.make_async_copy(a, b, sems.at[first + i]) for i, (a, b) in enumerate(copies)]
    for copy in started:
        copy.start()
    return started


def wait_for(started):
    for copy in started:
        copy.wait()


def pack_kernel(place_ref, raw_sent, other_sent, out_ref, half_ref, raw, other, sems):
    gz = place_ref[2]
    copies = fetched([(raw_sent, raw), (other_sent, other)], sems)

    row = lax.broadcasted_iota(jnp.int32, (256, 256), 0)
    col = lax.broadcasted_iota(jnp.int32, (256, 256), 1)
    parter = jnp.where(2 * (col & 127) + (col >> 7) == ((row + 128 * gz) & 255), 1.0, 0.0).astype(BF16)
    row = lax.broadcasted_iota(jnp.int32, (256, 128), 0)
    col = lax.broadcasted_iota(jnp.int32, (256, 128), 1)
    half = jnp.where(row < 128, gz, 1 - gz)
    widen = jnp.where(((row & 127) < 64) & (col == (row & 127) + 64 * half), 1.0, 0.0).astype(BF16)

    row = lax.broadcasted_iota(jnp.int32, (96, 192), 0)
    col = lax.broadcasted_iota(jnp.int32, (96, 192), 1)
    y = sum(jnp.where(row >= 24 * i, 1, 0) for i in (1, 2, 3))
    group, at = (row >> 3) - 3 * y, row & 7
    back = jnp.where(at >= 3, 1, 0)
    corner = at >= 6
    component = jnp.where(corner, group, at - 3 * back)
    pz = jnp.where(corner, at - 6, back)
    px = jnp.where(corner | (group == 1), 1, 0)
    py = jnp.where(corner | (group == 2), 1, 0)
    source = 48 * pz + 16 * component + 8 * px + 2 * y + py
    shuffle = jnp.where(jnp.where(col >= 96, col - 96, col) == source, 1.0, 0.0).astype(BF16)

    wait_for(copies)
    high, low = halves(jnp.concatenate([raw[0:3].reshape(192, 128), other[0:3].reshape(192, 128)], axis=1))
    parted = jnp.dot(jnp.concatenate([high, low], axis=0).astype(BF16), parter, preferred_element_type=F32)
    parted = parted.reshape(2, 3, 8, 8, 256)
    pieces = []
    for x in range(4):
        near = parted[:, :, 2 * x : 2 * x + 2].reshape(2, 48, 256)
        pieces.append(
            jnp.concatenate([near[0, :, :128], near[0, :, 128:], near[1, :, :128], near[1, :, 128:]], axis=0)
        )
    stacked = jnp.concatenate(pieces, axis=1).astype(BF16)
    out_ref[0:96, :] = jnp.dot(shuffle, stacked, preferred_element_type=F32)

    levels = jnp.concatenate([raw[3, 0:4].reshape(32, 128), other[3, 0:4].reshape(32, 128)], axis=1)
    ratio = jnp.dot(levels.astype(BF16), widen, preferred_element_type=F32) / (DENSITY_LEVELS - 1)
    moduli = 0.05 + 0.95 * ratio * ratio * ratio
    for x in range(4):
        out_ref[96:104, 128 * x : 128 * x + 128] = moduli[8 * x : 8 * x + 8]
    half_ref[...] = out_ref[pl.ds(pl.multiple_of((PACK - PART) * gz, 8), PART), :]


def split(values):
    high = values.astype(BF16).astype(F32)
    return jnp.concatenate([high, values - high], axis=0).astype(BF16)


def roll_tiles(values, step):
    tiles = []
    for t in range(values.shape[1] // 128):
        tile = values[:, 128 * t : 128 * t + 128]
        lane = lax.broadcasted_iota(jnp.int32, tile.shape, 1)
        if step == 1:
            tiles.append(jnp.where(lane < 127, pltpu.roll(tile, 127, 1), 0.0))
        else:
            tiles.append(jnp.where(lane > 0, pltpu.roll(tile, 1, 1), 0.0))
    return tiles[0] if len(tiles) == 1 else jnp.concatenate(tiles, axis=1)


def hi_lo_weights(matrix, left, right):
    high, low = halves(matrix)
    col = lax.broadcasted_iota(jnp.int32, right.shape, 1)
    right_high = jnp.where(col % 16 < 8, right.astype(F32), 0.0).astype(BF16)
    rows = [
        jnp.dot(jnp.dot(left, part.astype(BF16), preferred_element_type=F32).astype(BF16), to, preferred_element_type=F32)
        for part, to in ((high, right), (low, right_high))
    ]
    return jnp.concatenate(rows, axis=0).astype(BF16)


def weights_kernel(fine_ref, coarse_ref, cards_ref, *book_refs):
    def card(name):
        return Part(cards_ref, CARDS, name)[...]

    matrices = {name: card(name) for name in ("restrict", "prolong", "shuffle")}
    for name, ref in (("fine", fine_ref), ("coarse", coarse_ref)):
        matrix = ref[...]
        row = lax.broadcasted_iota(jnp.int32, matrix.shape, 0)
        col = lax.broadcasted_iota(jnp.int32, matrix.shape, 1)
        diagonal = jnp.where(row == col, matrix, 0.0)
        matrices[name] = hi_lo_weights(matrix, card(name + "_out"), card(name + "_in"))
        matrices[name + "_diag"] = hi_lo_weights(diagonal, card(name + "_rows"), card(name + "_at"))
    for (places, _), book_ref in zip(BOOKS, book_refs, strict=True):
        for name in places:
            Part(book_ref, places, name)[...] = matrices[name]


def scaled(values, moduli):
    rows, lanes = values.shape
    return (values.reshape(rows // 8, 8, lanes) * moduli[None]).reshape(rows, lanes)


def schedules():
    sigma = MID / HALF
    rhos = [1.0 / sigma]
    for _ in range(DEG - 1):
        rhos.append(1.0 / (2.0 * sigma - rhos[-1]))
    smooth = [(rhos[s + 1] * rhos[s], 2.0 * rhos[s + 1] / HALF) for s in range(DEG - 1)]
    o, c = SIDE, FAR
    return {
        "start": ([(0, ROWS, 0.0, 0.0, 0.0)], 3),
        "before": ([(o - 3 + s, o + 7 - s, *smooth[s], 0.0) for s in range(DEG - 1)], 6),
        "leave": ([(o, o + 4, 0.0, 0.0, 0.0)], 4),
        "coarse_start": ([(c - 7, c + 11, 0.0, 0.0, 0.0)], 3),
        "coarse": ([(c - 7 + s, c + 10 - s, *smooth[s], float(s == DEG - 2)) for s in range(DEG - 1)], 9),
        "correct": ([(o - 4, o + 8, 0.0, 0.0, 0.0)], 3),
        "after": (
            [(o - 4, o + 7, 0.0, 1.0 / MID, 0.0)]
            + [(o - 3 + s, o + 6 - s + (s == DEG - 2), *smooth[s], 0.0) for s in range(DEG - 1)],
            3,
        ),
    }


def row_at(name, t):
    at, row = 0, None
    for first, last, *_ in schedules()[name][0]:
        here = t + (first - at)
        row = here if row is None else jnp.where(t >= at, here, row)
        at += last - first
    return jnp.where(t >= at, SIDE, row).astype(jnp.int32)


def factor_at(name, t, which):
    at, factor = 0, None
    for first, last, *factors in schedules()[name][0]:
        here = jnp.float32(factors[which])
        factor = here if factor is None else jnp.where(t >= at, here, factor)
        at += last - first
    return factor


CHUNKS = [(256 * n, slice(256 * n, 256 * n + 256)) for n in range(4)]


def pushed(before, values):
    return jnp.concatenate([before, values[:, :128]], axis=1)


def store_fine(fine_x, y, lanes, values):
    for g in range(3):
        part = values[8 * g : 8 * g + 8]
        fine_x[y, 32 * g : 32 * g + 16, lanes] = split(part)
        fine_x[y, 32 * g + 16 : 32 * g + 32, lanes] = split(roll_tiles(part, 1))


def store_coarse(coarse_x, y, lanes, values):
    row = lax.broadcasted_iota(jnp.int32, values.shape, 0)
    further = pltpu.roll(roll_tiles(values, 1), 3, 0)
    coarse_x[y, :, lanes] = split(jnp.where(row < 3, values, jnp.where(row < 6, further, 0.0)))


def pipeline(prods, name, issue, finish):
    sweeps, together = schedules()[name]
    count = sum(last - first for first, last, *_ in sweeps)
    assert count % together == 0
    assert together % (AHEAD + 1) == 0 or count == together
    for u in range(AHEAD):
        issue(row_at(name, jnp.int32(u)), prods[u])

    def some(i, _):
        t = together * i
        for u in range(together):
            issue(row_at(name, t + u + AHEAD), prods[(u + AHEAD) % len(prods)])
            finish(t + u, row_at(name, t + u), prods[u % len(prods)])
        return 0

    lax.fori_loop(0, count // together, some, 0)


def fine_issue(fine_w, fine_x):
    def issue(y, prod):
        for low, lanes in CHUNKS:
            there = slice(low + 128, low + 384)
            operand = jnp.concatenate(
                [
                    fine_x[y, :, lanes],
                    fine_x[y, 0:32, there],
                    fine_x[y, 64:96, there],
                    fine_x[y + 1, 0:64, lanes],
                    fine_x[y + 1, 0:32, there],
                ],
                axis=0,
            )
            products = jnp.dot(fine_w[...], operand, preferred_element_type=F32)
            prod[:, lanes] = products[:128] + products[128:]

    return issue


def fine_finish(moduli, carry, use):
    def finish(t, y, prod):
        before = [(jnp.zeros((16, 128), F32), jnp.zeros((8, 128), F32))] * 2
        for low, lanes in CHUNKS:
            m = moduli[y, :, lanes]
            sums = []
            for z in range(2):
                v = scaled(prod[64 * z : 64 * z + 64, lanes], m)
                old = carry[16 * z : 16 * z + 16, lanes]
                along_x = pushed(before[z][0], v[24:40])
                along_xy = pushed(before[z][1], v[56:64])
                before[z] = (v[24:40, 128:], v[56:64, 128:])
                sums.append(
                    jnp.concatenate(
                        [v[0:8] + along_x[0:8] + old[0:8], v[8:16] + old[8:16], v[16:24] + along_x[8:16]], axis=0
                    )
                )
                carry[16 * z : 16 * z + 16, lanes] = jnp.concatenate([v[40:48] + along_xy, v[48:56]], axis=0)
            use(t, y, lanes, sums[0] + roll_tiles(sums[1], -1))

    return finish


def coarse_finish(moduli, carry, use):
    def finish(t, y, prod):
        before = (jnp.zeros((8, 128), F32), jnp.zeros((8, 128), F32))
        for low, lanes in CHUNKS:
            v = prod[0:32, lanes]
            if moduli is not None:
                v = scaled(v, moduli[y, :, lanes])
            sums = v[0:8] + pushed(before[0], v[8:16]) + carry[:, lanes]
            carry[:, lanes] = v[16:24] + pushed(before[1], v[24:32])
            before = (v[8:16, 128:], v[24:32, 128:])
            use(t, y, lanes, sums + roll_tiles(pltpu.roll(sums, 5, 0), -1))

    return finish


def smooth_fine(name, inverse, res, step, total, fine_x):
    def use(t, y, lanes, sums):
        keep, gain = factor_at(name, t, 0), factor_at(name, t, 1)
        r = res[y, :, lanes] - sums
        d = keep * step[y, :, lanes] + gain * (inverse[y, :, lanes] * r)
        res[y, :, lanes] = r
        step[y, :, lanes] = d
        total[y, :, lanes] = total[y, :, lanes] + d
        store_fine(fine_x, y, lanes, d)

    return use


def diag_issue(diag_w, moduli, count):
    def issue(y, prod):
        spot = lax.broadcasted_iota(jnp.int32, (8, 256), 0)
        before = jnp.zeros((8, 128), F32)
        for low, lanes in CHUNKS:
            near = jnp.where(spot < 4, moduli[y, :, lanes], moduli[jnp.maximum(y - 1, 0), :, lanes])
            moved = pushed(before, near)
            before = near[:, 128:]
            around = jnp.where(spot % 4 < 2, near, moved)
            around = jnp.where(spot % 2 < 1, around, roll_tiles(around, -1))
            products = jnp.dot(diag_w[...], split(around), preferred_element_type=F32)
            prod[0:count, lanes] = products[:count] + products[count:]

    return issue


def clear_tail(ref, rows):
    def clear(y, _):
        ref[y, :, LANES:] = jnp.zeros((ref.shape[1], 128), BF16)
        return 0

    lax.fori_loop(0, rows, clear, 0)


def validity(place_ref, ahead):
    first, count = place_ref[1] * OWN - ahead, place_ref[3] * OWN

    def valid(y):
        return jnp.where((first + y >= 0) & (first + y < count), 1.0, 0.0).astype(F32)

    return valid


def before_kernel(place_ref, *refs):
    blocks = refs[:7]
    book_ref, outs = refs[7], refs[8:13]
    (book, res, step, total, fine_x, carry, load, moduli, inverse, note, moduli_rows, c_carry, sems, out_sems, *prods) = refs[13:]
    gx, gz = place_ref[0], place_ref[2]
    valid = validity(place_ref, SIDE)
    o = SIDE

    own, a, ax, za, zax, half, half_other = blocks
    lanes_of = [pl.ds(pl.multiple_of(x * 512, 512), 512) for x in (gx, 1 - gx)]
    side = 1 - 2 * gz
    spots = [(own, 0, 0), (a, -side, 0), (ax, -side, 1), (za, side, 0), (zax, side, 1)]
    fine_w, diag_w, restrict_w = [Part(book, BOOKS[0][0], name) for name in BOOKS[0][0]]
    copies = [(book_ref, book)]
    for i, (ref, offset, across) in enumerate(spots):
        copies.append((ref.at[96:104, :], moduli_rows.at[i]))
        for y in range(OWN):
            copies.append((ref.at[24 * y : 24 * y + 24, :], load.at[o + OWN * offset + y, :, lanes_of[across]]))
    for i, (ref, core) in enumerate([(half, gz), (half_other, 1 - gz)]):
        copies.append((ref.at[PART - 8 : PART, :], moduli_rows.at[5 + i]))
        for y in range(2):
            first = pl.multiple_of(24 * y + (PACK - PART - 48) * core, 8)
            copies.append((ref.at[pl.ds(first, 24), :], load.at[o + 2 * core + y, :, lanes_of[1]]))
    copies = fetched(copies, sems)
    clear_tail(fine_x, ROWS)
    carry[...] = jnp.zeros_like(carry)
    wait_for(copies)
    own_rows = jnp.where(jnp.full((8, 512), gz) == 1, moduli_rows[5], moduli_rows[6])
    for rows, offset, across in [(moduli_rows[i], *spot[1:]) for i, spot in enumerate(spots)] + [(own_rows, 0, 1)]:
        for y in range(OWN):
            moduli[o + OWN * offset + y, :, lanes_of[across]] = jnp.broadcast_to(rows[y : y + 1], (8, 512))
    leaving = fetched([(load, outs[0]), (moduli, outs[1])], out_sems)

    def start(t, y, prod):
        ok = valid(y)
        for low, lanes in CHUNKS:
            inv = ok / (prod[0:24, lanes] + (1.0 - ok))
            r = load[y, :, lanes]
            d = inv * r * (1.0 / MID)
            inverse[y, :, lanes] = inv
            res[y, :, lanes] = r
            step[y, :, lanes] = d
            total[y, :, lanes] = d
            store_fine(fine_x, y, lanes, d)

    pipeline(prods, "start", diag_issue(diag_w, moduli, 24), start)
    leaving += fetched([(inverse, outs[2])], out_sems, len(leaving))
    issue = fine_issue(fine_w, fine_x)
    use = smooth_fine("before", inverse, res, step, total, fine_x)
    pipeline(prods, "before", issue, fine_finish(moduli, carry, use))
    rows = [(total.at[o + y], outs[3].at[24 * y : 24 * y + 24, :]) for y in range(OWN)]
    leaving += fetched(rows, out_sems, len(leaving))

    carry[...] = jnp.zeros_like(carry)

    def store_left(y, lanes, left):
        for g in range(3):
            fine_x[y, 16 * g : 16 * g + 16, lanes] = split(left[8 * g : 8 * g + 8])

    def leave(t, y, lanes, sums):
        store_left(y, lanes, res[y, :, lanes] - sums)

    pipeline(prods, "leave", issue, fine_finish(moduli, carry, leave))
    for low, lanes in CHUNKS:
        last = carry[0:16, lanes] + roll_tiles(carry[16:32, lanes], -1)
        last = jnp.concatenate([last, jnp.zeros((8, 256), F32)], axis=0)
        store_left(o + OWN, lanes, -last * valid(o + OWN))

    c_carry[...] = jnp.zeros_like(c_carry)
    for j in range(OWN + 1):
        prod = prods[j % len(prods)]
        for low, lanes in CHUNKS:
            prod[0:32, lanes] = jnp.dot(restrict_w[...], fine_x[o + j, 0:48, lanes], preferred_element_type=F32)

        def keep(t, y, lanes, sums, j=j):
            note[3 * j : 3 * j + 3, lanes] = sums[0:3]

        coarse_finish(None, c_carry, keep)(0, o + j, prod)
    for y in range(OWN):
        note[16 + y : 17 + y, :] = moduli[o + y, 0:1, :]
    leaving += fetched([(note, outs[4])], out_sems, len(leaving))
    wait_for(leaving)


def coarse_operand(coarse_x, y, low, lanes):
    there = slice(low + 128, low + 384)
    return jnp.concatenate(
        [coarse_x[y, :, lanes], coarse_x[y, :, there], coarse_x[y + 1, :, lanes], coarse_x[y + 1, :, there]], axis=0
    )


def coarse_kernel(place_ref, *refs):
    note, m1, zm1, m2, zm2, near_moduli, book_ref, fix = refs[:8]
    book, moduli, notes, c_inverse, c_res, c_step, c_total, coarse_x, c_carry, sems, *prods = refs[8:]
    gz = place_ref[2]
    o, c = SIDE, FAR
    valid = validity(place_ref, FAR)
    side = 1 - 2 * gz

    spots = [(note, 0), (m1, -side), (zm1, side), (m2, -2 * side), (zm2, 2 * side)]
    copies = [(ref, notes.at[i]) for i, (ref, _) in enumerate(spots)]
    copies.append((near_moduli, moduli.at[c - o : c - o + ROWS]))
    copies.append((book_ref, book))
    coarse_w, diag_w = [Part(book, BOOKS[1][0], name) for name in BOOKS[1][0]]
    copies = fetched(copies, sems)
    clear_tail(coarse_x, C_ROWS)
    c_carry[...] = jnp.zeros_like(c_carry)
    c_res[...] = jnp.zeros_like(c_res)
    wait_for(copies)
    for i, (_, offset) in enumerate(spots):
        at = c + OWN * offset
        if i >= 3:
            for y in range(OWN):
                moduli[at + y] = jnp.broadcast_to(notes[i, 16 + y : 17 + y, :], (8, LANES))
        for y in range(OWN + 1):
            c_res[at + y, 0:3, :] = c_res[at + y, 0:3, :] + notes[i, 3 * y : 3 * y + 3, :]

    def start(t, y, prod):
        ok = valid(y)
        for low, lanes in CHUNKS:
            used = lax.broadcasted_iota(jnp.int32, (8, 256), 0) < 3
            inv = jnp.where(used, ok / (prod[0:8, lanes] + (1.0 - ok)), 0.0)
            d = inv * c_res[y, :, lanes] * (1.0 / MID)
            c_inverse[y, :, lanes] = inv
            c_step[y, :, lanes] = d
            c_total[y, :, lanes] = d
            store_coarse(coarse_x, y, lanes, d)

    pipeline(prods, "coarse_start", diag_issue(diag_w, moduli, 8), start)

    def issue(y, prod):
        for low, lanes in CHUNKS:
            products = jnp.dot(coarse_w[...], coarse_operand(coarse_x, y, low, lanes), preferred_element_type=F32)
            prod[0:32, lanes] = products[:32] + products[32:]

    def smooth(t, y, lanes, sums):
        keep, gain, last = [factor_at("coarse", t, which) for which in range(3)]
        r = c_res[y, :, lanes] - sums
        d = keep * c_step[y, :, lanes] + gain * (c_inverse[y, :, lanes] * r)
        so_far = c_total[y, :, lanes]
        c_res[y, :, lanes] = r
        c_step[y, :, lanes] = d
        c_total[y, :, lanes] = so_far + d
        store_coarse(coarse_x, y, lanes, d + last * so_far)

    pipeline(prods, "coarse", issue, coarse_finish(moduli, c_carry, smooth))
    wait_for(fetched([(coarse_x.at[c - o : c - o + ROWS + 1], fix)], sems))


def after_kernel(place_ref, *refs):
    fix_sent, s0, s1, zs1, load_sent, moduli_sent, inverse_sent, book_ref, out_ref = refs[:9]
    (book, res, step, total, fine_x, carry, load, moduli, inverse, fix, sems, *prods) = refs[9:]
    gx, gz = place_ref[0], place_ref[2]
    o = SIDE
    side = 1 - 2 * gz

    fine_w, prolong_w, shuffle = [Part(book, BOOKS[2][0], name) for name in BOOKS[2][0]]
    copies = [(fix_sent, fix), (load_sent, load), (book_ref, book)]
    for ref, offset in [(s0, 0), (s1, -side), (zs1, side)]:
        for y in range(OWN):
            copies.append((ref.at[24 * y : 24 * y + 24, :], total.at[o + OWN * offset + y]))
    first = fetched(copies, sems)
    second = fetched([(inverse_sent, inverse), (moduli_sent, moduli)], sems, len(first))
    clear_tail(fine_x, ROWS)
    carry[...] = jnp.zeros_like(carry)
    wait_for(first)

    def correct_issue(y, prod):
        for low, lanes in CHUNKS:
            prod[0:24, lanes] = jnp.dot(
                prolong_w[...], coarse_operand(fix, y, low, lanes), preferred_element_type=F32
            )

    def correct(t, y, prod):
        for low, lanes in CHUNKS:
            corrected = total[y, :, lanes] + prod[0:24, lanes]
            total[y, :, lanes] = corrected
            res[y, :, lanes] = load[y, :, lanes]
            step[y, :, lanes] = jnp.zeros((24, 256), F32)
            store_fine(fine_x, y, lanes, corrected)

    pipeline(prods, "correct", correct_issue, correct)
    wait_for(second)
    use = smooth_fine("after", inverse, res, step, total, fine_x)
    pipeline(prods, "after", fine_issue(fine_w, fine_x), fine_finish(moduli, carry, use))

    row = lax.broadcasted_iota(jnp.int32, (256, 128), 0)
    col = lax.broadcasted_iota(jnp.int32, (256, 128), 1)
    weave = (row == 128 * (col % 2) + 64 * gz + col // 2).astype(F32).astype(BF16)
    lanes = pl.ds(pl.multiple_of(gx * 512, 512), 512)
    high, low = halves(total[o : o + OWN, :, lanes].reshape(96, 512))
    pieces = []
    for part in (high, low):
        back = lax.dot_general(
            shuffle[...][:, 0:96], part.astype(BF16), (((0,), (0,)), ((), ())), preferred_element_type=F32
        )
        for x in range(4):
            near = back[:, 128 * x : 128 * x + 128]
            pieces.append(jnp.concatenate([near[0:48], near[48:96]], axis=1))
    woven = jnp.dot(jnp.concatenate(pieces, axis=0).astype(BF16), weave, preferred_element_type=F32)
    woven = woven[:192] + woven[192:]
    for x in range(4):
        out_ref[:, 2 * x : 2 * x + 2] = woven[48 * x : 48 * x + 48].reshape(3, 2, 8, 128)


def per_device(adjoint_load, levels, fine_stiffness, coarse_stiffness):
    count = lax.axis_size("gy")
    place = jnp.stack(
        [lax.axis_index("gx"), lax.axis_index("gy"), lax.axis_index("gz"), jnp.int32(count)]
    ).astype(jnp.int32)

    def swap(value, axis):
        return lax.ppermute(value, axis, [(0, 1), (1, 0)])

    def sided(value, steps, across=False):
        pairs = []
        for gx in range(2):
            for i in range(count - steps):
                low, high = 2 * (gx * count + i), 2 * (gx * count + i + steps)
                other = 2 * count * (1 - 2 * gx) if across else 0
                pairs += [(low, high + other), (high + 1, low + other + 1)]
        return lax.ppermute(value, ("gx", "gy", "gz"), pairs)

    whole = pl.BlockSpec(memory_space=pltpu.VMEM)
    there = pl.BlockSpec(memory_space=pl.ANY)
    scalars = pl.BlockSpec(memory_space=pltpu.SMEM)

    def pack(raw, other):
        return pl.pallas_call(
            pack_kernel,
            out_shape=[jax.ShapeDtypeStruct((rows, 512), F32) for rows in (PACK, PART)],
            in_specs=[scalars, there, there],
            out_specs=[whole] * 2,
            scratch_shapes=[pltpu.VMEM(raw.shape, F32)] * 2 + [pltpu.SemaphoreType.DMA((2,))],
            compiler_params=pltpu.CompilerParams(vmem_limit_bytes=8 * 1024 * 1024),
            name="pack",
        )(place, raw, other)

    book, coarse_book, after_book = pl.pallas_call(
        weights_kernel,
        out_shape=[jax.ShapeDtypeStruct((rows, 256), BF16) for _, rows in BOOKS],
        in_specs=[whole] * 3,
        out_specs=[whole] * 3,
        compiler_params=pltpu.CompilerParams(vmem_limit_bytes=8 * 1024 * 1024),
        name="weights",
    )(fine_stiffness, coarse_stiffness, cards())

    _, x_nodes, y_nodes, z_nodes = adjoint_load.shape
    room = [(0, whole_size - size) for whole_size, size in zip((x_nodes, y_nodes, z_nodes), levels.shape, strict=True)]
    raw = jnp.concatenate([adjoint_load, jnp.pad(levels, room).astype(F32)[None]], axis=0)
    own, half = pack(raw, swap(raw, "gz"))
    a, ax = sided(own, 1), sided(own, 1, True)
    half_x = swap(half, "gx")
    blocks = [own, a, ax, swap(lax.optimization_barrier((a, book))[0], "gz"), swap(ax, "gz"), half_x, swap(half_x, "gz")]

    def held(count, height=24):
        return pltpu.VMEM((count, height, LANES), F32)

    fine_scratch = [
        held(ROWS),
        held(ROWS),
        held(ROWS),
        pltpu.VMEM((ROWS + 1, 96, WIDE), BF16),
        pltpu.VMEM((32, LANES), F32),
        held(ROWS),
    ]
    prods = [pltpu.VMEM((128, LANES), F32)] * (AHEAD + 1)
    limit = pltpu.CompilerParams(vmem_limit_bytes=24 * 1024 * 1024)
    load, moduli, inverse, smoothed, note = pl.pallas_call(
        before_kernel,
        out_shape=[
            jax.ShapeDtypeStruct(shape, F32)
            for shape in [(ROWS, 24, LANES), (ROWS, 8, LANES), (ROWS, 24, LANES), (24 * OWN, LANES), (NOTE, LANES)]
        ],
        in_specs=[scalars] + [there] * 8,
        out_specs=[there] * 5,
        scratch_shapes=[pltpu.VMEM(book.shape, BF16), *fine_scratch]
        + [
            held(ROWS, 8),
            held(ROWS),
            pltpu.VMEM((NOTE, LANES), F32),
            pltpu.VMEM((7, 8, 512), F32),
            pltpu.VMEM((8, LANES), F32),
            pltpu.SemaphoreType.DMA((5 * (OWN + 1) + 7,)),
            pltpu.SemaphoreType.DMA((OWN + 4,)),
            *prods,
        ],
        compiler_params=limit,
        name="before",
    )(place, *blocks, book)

    m1, m2 = sided(note, 1), sided(note, 2)
    s1 = sided(smoothed, 1)
    fix = pl.pallas_call(
        coarse_kernel,
        out_shape=jax.ShapeDtypeStruct((ROWS + 1, 16, WIDE), BF16),
        in_specs=[scalars] + [there] * 7,
        out_specs=there,
        scratch_shapes=[
            pltpu.VMEM(coarse_book.shape, BF16),
            held(C_ROWS, 8),
            pltpu.VMEM((5, NOTE, LANES), F32),
            held(C_ROWS, 8),
            held(C_ROWS + 1, 8),
            held(C_ROWS, 8),
            held(C_ROWS, 8),
            pltpu.VMEM((C_ROWS + 1, 16, WIDE), BF16),
            pltpu.VMEM((8, LANES), F32),
            pltpu.SemaphoreType.DMA((7,)),
            *prods,
        ],
        compiler_params=limit,
        cost_estimate=pl.CostEstimate(flops=4 * 10**9, bytes_accessed=4 * 10**7, transcendentals=0),
        name="coarse",
    )(place, note, m1, swap(m1, "gz"), m2, swap(m2, "gz"), moduli, coarse_book)
    return pl.pallas_call(
        after_kernel,
        out_shape=jax.ShapeDtypeStruct(adjoint_load.shape, F32),
        in_specs=[scalars] + [there] * 8,
        out_specs=whole,
        scratch_shapes=[
            pltpu.VMEM(after_book.shape, BF16),
            *fine_scratch,
            held(ROWS, 8),
            held(ROWS),
            pltpu.VMEM((ROWS + 1, 16, WIDE), BF16),
            pltpu.SemaphoreType.DMA((3 * OWN + 5,)),
            *prods,
        ],
        compiler_params=limit,
        name="after",
    )(place, fix, smoothed, s1, swap(s1, "gz"), load, moduli, inverse, after_book)


def solution(mesh):
    return jax.shard_map(
        per_device,
        mesh=mesh,
        in_specs=(P(None, "gx", "gy", "gz"), P("gx", "gy", "gz"), P(), P()),
        out_specs=P(None, "gx", "gy", "gz"),
        check_vma=False,
    )
```

```python
from typing import NamedTuple

import jax
import jax.numpy as jnp
import numpy as np
from jax import lax
from jax.experimental import pallas as pl
from jax.experimental.pallas import tpu as pltpu
from jax.sharding import PartitionSpec as P

DEG = 4
DENSITY_LEVELS = 16
MID = 1.125
HALF = 0.875

F32 = jnp.float32
BF16 = jnp.bfloat16

OWN = 4
SIDE = 4
FAR = 8
ROWS = OWN + 2 * SIDE
C_ROWS = OWN + 2 * FAR
LANES = 1024
WIDE = LANES + 128
AHEAD = 2
PART = 56
PACK = 104
NOTE = 24


def node_row(group, row):
    px, py = ((0, 0), (1, 0), (0, 1))[group]
    if row < 6:
        return row % 3, px, py, row // 3
    return group, 1, 1, row - 6


FINE_IN = [(g, sx, sy) for sx, sy, groups in ((0, 0, (0, 1, 2)), (1, 0, (0, 2)), (0, 1, (0, 1)), (1, 1, (0,))) for g in groups]
SHIFTS = [(0, 0), (1, 0), (0, 1), (1, 1)]


def fine_place(group, row, sx, sy, sz):
    p, px, py, pz = node_row(group, row)
    if (sx and px) or (sy and py) or (sz and pz):
        return None
    return 27 * p + 9 * (px + 2 * sx) + 3 * (py + 2 * sy) + pz + 2 * sz


def coarse_place(row, sx, sy, sz):
    return 8 * row + 4 * sx + 2 * sy + sz if row < 3 else None


def fine_selectors():
    out_rows = np.zeros((128, 81), np.float32)
    in_rows = np.zeros((256, 81), np.float32)
    at = 0
    for sz in (0, 1):
        for g, sx, sy in FINE_IN:
            for row in range(8):
                place = fine_place(g, row, sx, sy, sz)
                if place is not None:
                    out_rows[at + row, place] = 1.0
            at += 8
    at = 0
    for g, sx, sy in FINE_IN:
        for sz in (0, 1):
            for row in range(8):
                place = fine_place(g, row, sx, sy, sz)
                if place is not None:
                    in_rows[at + row, place] = 1.0
                    in_rows[at + 8 + row, place] = 1.0
            at += 16
    return out_rows, in_rows


def coarse_selectors():
    out_rows = np.zeros((32, 24), np.float32)
    in_rows = np.zeros((64, 24), np.float32)
    for at, (sx, sy) in enumerate(SHIFTS):
        for sz in (0, 1):
            for row in range(3):
                place = coarse_place(row, sx, sy, sz)
                out_rows[8 * at + 3 * sz + row, place] = 1.0
                in_rows[[16 * at + 3 * sz + row, 16 * at + 8 + 3 * sz + row], place] = 1.0
    return out_rows, in_rows


def weight_along(parity, shift):
    if parity == 0:
        return 1.0 if shift == 0 else 0.0
    return 0.5


def transfer_weights():
    prolong = np.zeros((24, 64), np.float32)
    restrict = np.zeros((32, 48), np.float32)
    for at, (sx, sy) in enumerate(SHIFTS):
        for sz in (0, 1):
            for g in range(3):
                for row in range(8):
                    p, px, py, pz = node_row(g, row)
                    w = weight_along(px, sx) * weight_along(py, sy) * weight_along(pz, sz)
                    prolong[8 * g + row, [16 * at + 3 * sz + p, 16 * at + 8 + 3 * sz + p]] = w
                    restrict[8 * at + 3 * sz + p, [16 * g + row, 16 * g + 8 + row]] = w
    return prolong, restrict


def row_shuffle():
    shuffle = np.zeros((96, 96), np.float32)
    for y in range(4):
        for g in range(3):
            for row in range(8):
                p, px, py, pz = node_row(g, row)
                shuffle[24 * y + 8 * g + row, pz * 48 + p * 16 + px * 8 + 2 * y + py] = 1.0
    return np.concatenate([shuffle, shuffle], axis=1)


def diag_selectors():
    fine_rows, fine_at = np.zeros((24, 81), np.float32), np.zeros((81, 16), np.float32)
    coarse_rows, coarse_at = np.zeros((8, 24), np.float32), np.zeros((24, 16), np.float32)
    for at in range(8):
        sy, sx, sz = at // 4, at // 2 % 2, at % 2
        for g in range(3):
            for row in range(8):
                place = fine_place(g, row, sx, sy, sz)
                if place is not None:
                    fine_rows[8 * g + row, place] = 1.0
                    fine_at[place, [at, at + 8]] = 1.0
        for row in range(3):
            place = coarse_place(row, sx, sy, sz)
            coarse_rows[row, place] = 1.0
            coarse_at[place, [at, at + 8]] = 1.0
    return fine_rows, fine_at, coarse_rows, coarse_at


def laid_out(parts):
    places, at = {}, 0
    for name, (rows, columns) in parts.items():
        places[name] = (at, rows, columns)
        at += -(-rows // 16) * 16
    return places, at


def constants():
    fine_out, fine_in = fine_selectors()
    coarse_out, coarse_in = coarse_selectors()
    fine_rows, fine_at, coarse_rows, coarse_at = diag_selectors()
    prolong, restrict = transfer_weights()
    return {
        "fine_out": fine_out, "fine_in": fine_in.T, "fine_rows": fine_rows, "fine_at": fine_at,
        "coarse_out": coarse_out, "coarse_in": coarse_in.T, "coarse_rows": coarse_rows, "coarse_at": coarse_at,
        "restrict": restrict, "prolong": prolong, "shuffle": row_shuffle(),
    }


CARDS, CARD_ROWS = laid_out({name: value.shape for name, value in constants().items()})
BOOKS = [
    laid_out({"fine": (256, 256), "fine_diag": (48, 16), "restrict": (32, 48)}),
    laid_out({"coarse": (64, 64), "coarse_diag": (16, 16)}),
    laid_out({"fine": (256, 256), "prolong": (24, 64), "shuffle": (96, 192)}),
]


def cards():
    sheet = np.zeros((CARD_ROWS, 256), np.float32)
    for name, value in constants().items():
        first, rows, columns = CARDS[name]
        sheet[first : first + rows, :columns] = value
    return jnp.asarray(sheet, dtype=BF16)


class Part:
    def __init__(self, ref, places, name):
        first, rows, columns = places[name]
        self.ref, self.at = ref, (slice(first, first + rows), slice(0, columns))

    def __getitem__(self, _):
        return self.ref[self.at]

    def __setitem__(self, _, values):
        self.ref[self.at] = values


def halves(values):
    high = values.astype(BF16).astype(F32)
    return high, (values - high).astype(BF16).astype(F32)


def fetched(copies, sems, first=0):
    started = [pltpu.make_async_copy(a, b, sems.at[first + i]) for i, (a, b) in enumerate(copies)]
    for copy in started:
        copy.start()
    return started


def wait_for(started):
    for copy in started:
        copy.wait()


def pack_kernel(place_ref, raw_sent, other_sent, out_ref, half_ref, raw, other, sems):
    gz = place_ref[2]
    copies = fetched([(raw_sent, raw), (other_sent, other)], sems)

    row = lax.broadcasted_iota(jnp.int32, (256, 256), 0)
    col = lax.broadcasted_iota(jnp.int32, (256, 256), 1)
    parter = jnp.where(2 * (col & 127) + (col >> 7) == ((row + 128 * gz) & 255), 1.0, 0.0).astype(BF16)
    row = lax.broadcasted_iota(jnp.int32, (256, 128), 0)
    col = lax.broadcasted_iota(jnp.int32, (256, 128), 1)
    half = jnp.where(row < 128, gz, 1 - gz)
    widen = jnp.where(((row & 127) < 64) & (col == (row & 127) + 64 * half), 1.0, 0.0).astype(BF16)

    row = lax.broadcasted_iota(jnp.int32, (96, 192), 0)
    col = lax.broadcasted_iota(jnp.int32, (96, 192), 1)
    y = sum(jnp.where(row >= 24 * i, 1, 0) for i in (1, 2, 3))
    group, at = (row >> 3) - 3 * y, row & 7
    back = jnp.where(at >= 3, 1, 0)
    corner = at >= 6
    component = jnp.where(corner, group, at - 3 * back)
    pz = jnp.where(corner, at - 6, back)
    px = jnp.where(corner | (group == 1), 1, 0)
    py = jnp.where(corner | (group == 2), 1, 0)
    source = 48 * pz + 16 * component + 8 * px + 2 * y + py
    shuffle = jnp.where(jnp.where(col >= 96, col - 96, col) == source, 1.0, 0.0).astype(BF16)

    wait_for(copies)
    high, low = halves(jnp.concatenate([raw[0:3].reshape(192, 128), other[0:3].reshape(192, 128)], axis=1))
    parted = jnp.dot(jnp.concatenate([high, low], axis=0).astype(BF16), parter, preferred_element_type=F32)
    parted = parted.reshape(2, 3, 8, 8, 256)
    pieces = []
    for x in range(4):
        near = parted[:, :, 2 * x : 2 * x + 2].reshape(2, 48, 256)
        pieces.append(
            jnp.concatenate([near[0, :, :128], near[0, :, 128:], near[1, :, :128], near[1, :, 128:]], axis=0)
        )
    stacked = jnp.concatenate(pieces, axis=1).astype(BF16)
    out_ref[0:96, :] = jnp.dot(shuffle, stacked, preferred_element_type=F32)

    levels = jnp.concatenate([raw[3, 0:4].reshape(32, 128), other[3, 0:4].reshape(32, 128)], axis=1)
    ratio = jnp.dot(levels.astype(BF16), widen, preferred_element_type=F32) / (DENSITY_LEVELS - 1)
    moduli = 0.05 + 0.95 * ratio * ratio * ratio
    for x in range(4):
        out_ref[96:104, 128 * x : 128 * x + 128] = moduli[8 * x : 8 * x + 8]
    half_ref[...] = out_ref[pl.ds(pl.multiple_of((PACK - PART) * gz, 8), PART), :]


def split(values):
    high = values.astype(BF16).astype(F32)
    return jnp.concatenate([high, values - high], axis=0).astype(BF16)


def roll_tiles(values, step):
    tiles = []
    for t in range(values.shape[1] // 128):
        tile = values[:, 128 * t : 128 * t + 128]
        lane = lax.broadcasted_iota(jnp.int32, tile.shape, 1)
        if step == 1:
            tiles.append(jnp.where(lane < 127, pltpu.roll(tile, 127, 1), 0.0))
        else:
            tiles.append(jnp.where(lane > 0, pltpu.roll(tile, 1, 1), 0.0))
    return tiles[0] if len(tiles) == 1 else jnp.concatenate(tiles, axis=1)


def hi_lo_weights(matrix, left, right):
    high, low = halves(matrix)
    col = lax.broadcasted_iota(jnp.int32, right.shape, 1)
    right_high = jnp.where(col % 16 < 8, right.astype(F32), 0.0).astype(BF16)
    rows = [
        jnp.dot(jnp.dot(left, part.astype(BF16), preferred_element_type=F32).astype(BF16), to, preferred_element_type=F32)
        for part, to in ((high, right), (low, right_high))
    ]
    return jnp.concatenate(rows, axis=0).astype(BF16)


def weights_kernel(fine_ref, coarse_ref, cards_ref, *book_refs):
    def card(name):
        return Part(cards_ref, CARDS, name)[...]

    matrices = {name: card(name) for name in ("restrict", "prolong", "shuffle")}
    for name, ref in (("fine", fine_ref), ("coarse", coarse_ref)):
        matrix = ref[...]
        row = lax.broadcasted_iota(jnp.int32, matrix.shape, 0)
        col = lax.broadcasted_iota(jnp.int32, matrix.shape, 1)
        diagonal = jnp.where(row == col, matrix, 0.0)
        matrices[name] = hi_lo_weights(matrix, card(name + "_out"), card(name + "_in"))
        matrices[name + "_diag"] = hi_lo_weights(diagonal, card(name + "_rows"), card(name + "_at"))
    for (places, _), book_ref in zip(BOOKS, book_refs, strict=True):
        for name in places:
            Part(book_ref, places, name)[...] = matrices[name]


def scaled(values, moduli):
    rows, lanes = values.shape
    return (values.reshape(rows // 8, 8, lanes) * moduli[None]).reshape(rows, lanes)


class Step(NamedTuple):
    row: int
    keep: float = 0.0
    gain: float = 0.0
    last: bool = False
    lead: bool = False
    tail: bool = False
    operand: bool = True
    residual: bool = True


def schedules():
    sigma = MID / HALF
    rhos = [1.0 / sigma]
    for _ in range(DEG - 1):
        rhos.append(1.0 / (2.0 * sigma - rhos[-1]))
    smooth = [(rhos[s + 1] * rhos[s], 2.0 * rhos[s + 1] / HALF) for s in range(DEG - 1)]
    o, c = SIDE, FAR

    def smoothing(sweeps, operand, residual):
        steps = []
        for at, (first, last, keep, gain) in enumerate(sweeps):
            final = at == len(sweeps) - 1
            reads = operand if final else range(sweeps[at + 1][0], sweeps[at + 1][1] + 1)
            sums = residual if final else range(sweeps[at + 1][0] + 1, sweeps[at + 1][1])
            for row in range(first, last):
                steps.append(Step(row, keep, gain, final, row == first, row == last - 1, row in reads, row in sums))
        return steps

    return {
        "start": [Step(row) for row in range(o - 3, o + 8)],
        "before": smoothing(
            [(o - 3 + s, o + 7 - s, *smooth[s]) for s in range(DEG - 1)], range(o, o + 5), range(o, o + 4)
        ),
        "leave": [Step(row) for row in range(o, o + 4)],
        "coarse_start": [Step(row) for row in range(c - 7, c + 11)],
        "coarse": smoothing(
            [(c - 7 + s, c + 10 - s, *smooth[s]) for s in range(DEG - 1)], range(c - 4, c + 8), range(0)
        ),
        "correct": [Step(row) for row in range(o - 4, o + 8)],
        "after": smoothing(
            [(o - 4, o + 7, 0.0, 1.0 / MID)] + [(o - 3 + s, o + 6 - s, *smooth[s]) for s in range(DEG - 1)],
            range(0),
            range(0),
        ),
    }


OWN_ROWS = range(SIDE, SIDE + OWN)


CHUNKS = [(256 * n, slice(256 * n, 256 * n + 256)) for n in range(4)]


def pushed(before, values):
    return jnp.concatenate([before, values[:, :128]], axis=1)


def store_fine(fine_x, y, lanes, values):
    for g in range(3):
        part = values[8 * g : 8 * g + 8]
        fine_x[y, 32 * g : 32 * g + 16, lanes] = split(part)
        fine_x[y, 32 * g + 16 : 32 * g + 32, lanes] = split(roll_tiles(part, 1))


def store_coarse(coarse_x, y, lanes, values):
    row = lax.broadcasted_iota(jnp.int32, values.shape, 0)
    further = pltpu.roll(roll_tiles(values, 1), 3, 0)
    coarse_x[y, :, lanes] = split(jnp.where(row < 3, values, jnp.where(row < 6, further, 0.0)))


def pipeline(prods, name, issue, finish):
    steps = schedules()[name]
    for t in range(len(steps) + AHEAD):
        if t < len(steps):
            issue(steps[t].row, prods[t % len(prods)])
        if t >= AHEAD:
            finish(steps[t - AHEAD], prods[(t - AHEAD) % len(prods)])


def fine_issue(fine_w, fine_x):
    def issue(y, prod):
        for low, lanes in CHUNKS:
            there = slice(low + 128, low + 384)
            operand = jnp.concatenate(
                [
                    fine_x[y, :, lanes],
                    fine_x[y, 0:32, there],
                    fine_x[y, 64:96, there],
                    fine_x[y + 1, 0:64, lanes],
                    fine_x[y + 1, 0:32, there],
                ],
                axis=0,
            )
            products = jnp.dot(fine_w[...], operand, preferred_element_type=F32)
            prod[:, lanes] = products[:128] + products[128:]

    return issue


def fine_finish(moduli, carry, use):
    def finish(now, prod):
        y = now.row
        before = [(jnp.zeros((16, 128), F32), jnp.zeros((8, 128), F32))] * 2
        for low, lanes in CHUNKS:
            m = moduli[y, :, lanes]
            sums = []
            for z in range(2):
                v = scaled(prod[64 * z : 64 * z + 64, lanes], m)
                if not now.lead:
                    old = carry[16 * z : 16 * z + 16, lanes]
                    along_x = pushed(before[z][0], v[24:40])
                    sums.append(
                        jnp.concatenate(
                            [v[0:8] + along_x[0:8] + old[0:8], v[8:16] + old[8:16], v[16:24] + along_x[8:16]], axis=0
                        )
                    )
                if not now.tail:
                    along_xy = pushed(before[z][1], v[56:64])
                    carry[16 * z : 16 * z + 16, lanes] = jnp.concatenate([v[40:48] + along_xy, v[48:56]], axis=0)
                before[z] = (v[24:40, 128:], v[56:64, 128:])
            if not now.lead:
                use(now, y, lanes, sums[0] + roll_tiles(sums[1], -1))

    return finish


def coarse_finish(moduli, carry, use):
    def finish(now, prod):
        y = now.row
        before = (jnp.zeros((8, 128), F32), jnp.zeros((8, 128), F32))
        for low, lanes in CHUNKS:
            v = prod[0:32, lanes]
            if moduli is not None:
                v = scaled(v, moduli[y, :, lanes])
            if not now.lead:
                sums = v[0:8] + pushed(before[0], v[8:16]) + carry[:, lanes]
            if not now.tail:
                carry[:, lanes] = v[16:24] + pushed(before[1], v[24:32])
            before = (v[8:16, 128:], v[24:32, 128:])
            if not now.lead:
                use(now, y, lanes, sums + roll_tiles(pltpu.roll(sums, 5, 0), -1))

    return finish


def smooth_fine(inverse, res, step, total, fine_x):
    def use(now, y, lanes, sums):
        if not (now.operand or now.residual or y in OWN_ROWS):
            return
        r = res[y, :, lanes] - sums
        d = now.gain * (inverse[y, :, lanes] * r)
        if now.keep:
            d = now.keep * step[y, :, lanes] + d
        if now.residual:
            res[y, :, lanes] = r
            step[y, :, lanes] = d
        if y in OWN_ROWS:
            total[y, :, lanes] = total[y, :, lanes] + d
        if now.operand:
            store_fine(fine_x, y, lanes, d)

    return use


def diag_issue(diag_w, moduli, count):
    def issue(y, prod):
        spot = lax.broadcasted_iota(jnp.int32, (8, 256), 0)
        before = jnp.zeros((8, 128), F32)
        for low, lanes in CHUNKS:
            near = jnp.where(spot < 4, moduli[y, :, lanes], moduli[max(y - 1, 0), :, lanes])
            moved = pushed(before, near)
            before = near[:, 128:]
            around = jnp.where(spot % 4 < 2, near, moved)
            around = jnp.where(spot % 2 < 1, around, roll_tiles(around, -1))
            products = jnp.dot(diag_w[...], split(around), preferred_element_type=F32)
            prod[0:count, lanes] = products[:count] + products[count:]

    return issue


def clear_tail(ref, rows):
    def clear(y, _):
        ref[y, :, LANES:] = jnp.zeros((ref.shape[1], 128), BF16)
        return 0

    lax.fori_loop(0, rows, clear, 0)


def validity(place_ref, ahead):
    first, count = place_ref[1] * OWN - ahead, place_ref[3] * OWN

    def valid(y):
        return jnp.where((first + y >= 0) & (first + y < count), 1.0, 0.0).astype(F32)

    return valid


def before_kernel(place_ref, *refs):
    blocks = refs[:7]
    book_ref, outs = refs[7], refs[8:13]
    (book, res, step, total, fine_x, carry, load, moduli, inverse, note, moduli_rows, c_carry, sems, out_sems, *prods) = refs[13:]
    gx, gz = place_ref[0], place_ref[2]
    valid = validity(place_ref, SIDE)
    o = SIDE

    own, a, ax, za, zax, half, half_other = blocks
    lanes_of = [pl.ds(pl.multiple_of(x * 512, 512), 512) for x in (gx, 1 - gx)]
    side = 1 - 2 * gz
    spots = [(own, 0, 0), (a, -side, 0), (ax, -side, 1), (za, side, 0), (zax, side, 1)]
    fine_w, diag_w, restrict_w = [Part(book, BOOKS[0][0], name) for name in BOOKS[0][0]]
    copies = [(book_ref, book)]
    for i, (ref, offset, across) in enumerate(spots):
        copies.append((ref.at[96:104, :], moduli_rows.at[i]))
        for y in range(OWN):
            copies.append((ref.at[24 * y : 24 * y + 24, :], load.at[o + OWN * offset + y, :, lanes_of[across]]))
    for i, (ref, core) in enumerate([(half, gz), (half_other, 1 - gz)]):
        copies.append((ref.at[PART - 8 : PART, :], moduli_rows.at[5 + i]))
        for y in range(2):
            first = pl.multiple_of(24 * y + (PACK - PART - 48) * core, 8)
            copies.append((ref.at[pl.ds(first, 24), :], load.at[o + 2 * core + y, :, lanes_of[1]]))
    copies = fetched(copies, sems)
    clear_tail(fine_x, ROWS)
    carry[...] = jnp.zeros_like(carry)
    wait_for(copies)
    own_rows = jnp.where(jnp.full((8, 512), gz) == 1, moduli_rows[5], moduli_rows[6])
    for rows, offset, across in [(moduli_rows[i], *spot[1:]) for i, spot in enumerate(spots)] + [(own_rows, 0, 1)]:
        for y in range(OWN):
            moduli[o + OWN * offset + y, :, lanes_of[across]] = jnp.broadcast_to(rows[y : y + 1], (8, 512))
    leaving = fetched([(load, outs[0]), (moduli, outs[1])], out_sems)

    def start(now, prod):
        y = now.row
        ok = valid(y)
        for low, lanes in CHUNKS:
            inv = ok / (prod[0:24, lanes] + (1.0 - ok))
            r = load[y, :, lanes]
            d = inv * r * (1.0 / MID)
            inverse[y, :, lanes] = inv
            res[y, :, lanes] = r
            step[y, :, lanes] = d
            if y in OWN_ROWS:
                total[y, :, lanes] = d
            store_fine(fine_x, y, lanes, d)

    pipeline(prods, "start", diag_issue(diag_w, moduli, 24), start)
    leaving += fetched([(inverse, outs[2])], out_sems, len(leaving))
    issue = fine_issue(fine_w, fine_x)
    use = smooth_fine(inverse, res, step, total, fine_x)
    pipeline(prods, "before", issue, fine_finish(moduli, carry, use))
    rows = [(total.at[o + y], outs[3].at[24 * y : 24 * y + 24, :]) for y in range(OWN)]
    leaving += fetched(rows, out_sems, len(leaving))

    carry[...] = jnp.zeros_like(carry)

    def store_left(y, lanes, left):
        for g in range(3):
            fine_x[y, 16 * g : 16 * g + 16, lanes] = split(left[8 * g : 8 * g + 8])

    def leave(now, y, lanes, sums):
        store_left(y, lanes, res[y, :, lanes] - sums)

    pipeline(prods, "leave", issue, fine_finish(moduli, carry, leave))
    for low, lanes in CHUNKS:
        last = carry[0:16, lanes] + roll_tiles(carry[16:32, lanes], -1)
        last = jnp.concatenate([last, jnp.zeros((8, 256), F32)], axis=0)
        store_left(o + OWN, lanes, -last * valid(o + OWN))

    c_carry[...] = jnp.zeros_like(c_carry)
    for j in range(OWN + 1):
        prod = prods[j % len(prods)]
        for low, lanes in CHUNKS:
            prod[0:32, lanes] = jnp.dot(restrict_w[...], fine_x[o + j, 0:48, lanes], preferred_element_type=F32)

        def keep(now, y, lanes, sums, j=j):
            note[3 * j : 3 * j + 3, lanes] = sums[0:3]

        coarse_finish(None, c_carry, keep)(Step(o + j), prod)
    for y in range(OWN):
        note[16 + y : 17 + y, :] = moduli[o + y, 0:1, :]
    leaving += fetched([(note, outs[4])], out_sems, len(leaving))
    wait_for(leaving)


def coarse_operand(coarse_x, y, low, lanes):
    there = slice(low + 128, low + 384)
    return jnp.concatenate(
        [coarse_x[y, :, lanes], coarse_x[y, :, there], coarse_x[y + 1, :, lanes], coarse_x[y + 1, :, there]], axis=0
    )


def coarse_kernel(place_ref, *refs):
    note, m1, zm1, m2, zm2, near_moduli, book_ref, fix = refs[:8]
    book, moduli, notes, c_inverse, c_res, c_step, c_total, coarse_x, c_carry, sems, *prods = refs[8:]
    gz = place_ref[2]
    o, c = SIDE, FAR
    valid = validity(place_ref, FAR)
    side = 1 - 2 * gz

    spots = [(note, 0), (m1, -side), (zm1, side), (m2, -2 * side), (zm2, 2 * side)]
    copies = [(ref, notes.at[i]) for i, (ref, _) in enumerate(spots)]
    copies.append((near_moduli, moduli.at[c - o : c - o + ROWS]))
    copies.append((book_ref, book))
    coarse_w, diag_w = [Part(book, BOOKS[1][0], name) for name in BOOKS[1][0]]
    copies = fetched(copies, sems)
    clear_tail(coarse_x, C_ROWS)
    c_carry[...] = jnp.zeros_like(c_carry)
    c_res[...] = jnp.zeros_like(c_res)
    wait_for(copies)
    for i, (_, offset) in enumerate(spots):
        at = c + OWN * offset
        if i >= 3:
            for y in range(OWN):
                moduli[at + y] = jnp.broadcast_to(notes[i, 16 + y : 17 + y, :], (8, LANES))
        for y in range(OWN + 1):
            c_res[at + y, 0:3, :] = c_res[at + y, 0:3, :] + notes[i, 3 * y : 3 * y + 3, :]

    def start(now, prod):
        y = now.row
        ok = valid(y)
        for low, lanes in CHUNKS:
            used = lax.broadcasted_iota(jnp.int32, (8, 256), 0) < 3
            inv = jnp.where(used, ok / (prod[0:8, lanes] + (1.0 - ok)), 0.0)
            d = inv * c_res[y, :, lanes] * (1.0 / MID)
            c_inverse[y, :, lanes] = inv
            c_step[y, :, lanes] = d
            c_total[y, :, lanes] = d
            store_coarse(coarse_x, y, lanes, d)

    pipeline(prods, "coarse_start", diag_issue(diag_w, moduli, 8), start)

    def issue(y, prod):
        for low, lanes in CHUNKS:
            products = jnp.dot(coarse_w[...], coarse_operand(coarse_x, y, low, lanes), preferred_element_type=F32)
            prod[0:32, lanes] = products[:32] + products[32:]

    def smooth(now, y, lanes, sums):
        if not (now.operand or now.residual):
            return
        r = c_res[y, :, lanes] - sums
        d = now.keep * c_step[y, :, lanes] + now.gain * (c_inverse[y, :, lanes] * r)
        so_far = c_total[y, :, lanes] + d
        if now.residual:
            c_res[y, :, lanes] = r
            c_step[y, :, lanes] = d
            c_total[y, :, lanes] = so_far
        store_coarse(coarse_x, y, lanes, so_far if now.last else d)

    pipeline(prods, "coarse", issue, coarse_finish(moduli, c_carry, smooth))
    wait_for(fetched([(coarse_x.at[c - o : c - o + ROWS + 1], fix)], sems))


def after_kernel(place_ref, *refs):
    fix_sent, s0, s1, zs1, load_sent, moduli_sent, inverse_sent, book_ref, out_ref = refs[:9]
    (book, res, step, total, fine_x, carry, moduli, inverse, fix, sems, *prods) = refs[9:]
    gx, gz = place_ref[0], place_ref[2]
    o = SIDE
    side = 1 - 2 * gz

    fine_w, prolong_w, shuffle = [Part(book, BOOKS[2][0], name) for name in BOOKS[2][0]]
    copies = [(fix_sent, fix), (load_sent, res), (book_ref, book)]
    for ref, offset in [(s0, 0), (s1, -side), (zs1, side)]:
        for y in range(OWN):
            copies.append((ref.at[24 * y : 24 * y + 24, :], total.at[o + OWN * offset + y]))
    first = fetched(copies, sems)
    second = fetched([(inverse_sent, inverse), (moduli_sent, moduli)], sems, len(first))
    clear_tail(fine_x, ROWS)
    carry[...] = jnp.zeros_like(carry)
    wait_for(first)

    def correct_issue(y, prod):
        for low, lanes in CHUNKS:
            prod[0:24, lanes] = jnp.dot(
                prolong_w[...], coarse_operand(fix, y, low, lanes), preferred_element_type=F32
            )

    def correct(now, prod):
        y = now.row
        for low, lanes in CHUNKS:
            corrected = total[y, :, lanes] + prod[0:24, lanes]
            if y in OWN_ROWS:
                total[y, :, lanes] = corrected
            store_fine(fine_x, y, lanes, corrected)

    pipeline(prods, "correct", correct_issue, correct)
    wait_for(second)
    use = smooth_fine(inverse, res, step, total, fine_x)
    pipeline(prods, "after", fine_issue(fine_w, fine_x), fine_finish(moduli, carry, use))

    row = lax.broadcasted_iota(jnp.int32, (256, 128), 0)
    col = lax.broadcasted_iota(jnp.int32, (256, 128), 1)
    weave = (row == 128 * (col % 2) + 64 * gz + col // 2).astype(F32).astype(BF16)
    lanes = pl.ds(pl.multiple_of(gx * 512, 512), 512)
    high, low = halves(total[o : o + OWN, :, lanes].reshape(96, 512))
    pieces = []
    for part in (high, low):
        back = lax.dot_general(
            shuffle[...][:, 0:96], part.astype(BF16), (((0,), (0,)), ((), ())), preferred_element_type=F32
        )
        for x in range(4):
            near = back[:, 128 * x : 128 * x + 128]
            pieces.append(jnp.concatenate([near[0:48], near[48:96]], axis=1))
    woven = jnp.dot(jnp.concatenate(pieces, axis=0).astype(BF16), weave, preferred_element_type=F32)
    woven = woven[:192] + woven[192:]
    for x in range(4):
        out_ref[:, 2 * x : 2 * x + 2] = woven[48 * x : 48 * x + 48].reshape(3, 2, 8, 128)


def per_device(adjoint_load, levels, fine_stiffness, coarse_stiffness):
    count = lax.axis_size("gy")
    place = jnp.stack(
        [lax.axis_index("gx"), lax.axis_index("gy"), lax.axis_index("gz"), jnp.int32(count)]
    ).astype(jnp.int32)

    def swap(value, axis):
        return lax.ppermute(value, axis, [(0, 1), (1, 0)])

    def sided(value, steps, across=False):
        pairs = []
        for gx in range(2):
            for i in range(count - steps):
                low, high = 2 * (gx * count + i), 2 * (gx * count + i + steps)
                other = 2 * count * (1 - 2 * gx) if across else 0
                pairs += [(low, high + other), (high + 1, low + other + 1)]
        return lax.ppermute(value, ("gx", "gy", "gz"), pairs)

    whole = pl.BlockSpec(memory_space=pltpu.VMEM)
    there = pl.BlockSpec(memory_space=pl.ANY)
    scalars = pl.BlockSpec(memory_space=pltpu.SMEM)

    def pack(raw, other):
        return pl.pallas_call(
            pack_kernel,
            out_shape=[jax.ShapeDtypeStruct((rows, 512), F32) for rows in (PACK, PART)],
            in_specs=[scalars, there, there],
            out_specs=[whole] * 2,
            scratch_shapes=[pltpu.VMEM(raw.shape, F32)] * 2 + [pltpu.SemaphoreType.DMA((2,))],
            compiler_params=pltpu.CompilerParams(vmem_limit_bytes=8 * 1024 * 1024),
            name="pack",
        )(place, raw, other)

    book, coarse_book, after_book = pl.pallas_call(
        weights_kernel,
        out_shape=[jax.ShapeDtypeStruct((rows, 256), BF16) for _, rows in BOOKS],
        in_specs=[whole] * 3,
        out_specs=[whole] * 3,
        compiler_params=pltpu.CompilerParams(vmem_limit_bytes=8 * 1024 * 1024),
        name="weights",
    )(fine_stiffness, coarse_stiffness, cards())

    _, x_nodes, y_nodes, z_nodes = adjoint_load.shape
    room = [(0, whole_size - size) for whole_size, size in zip((x_nodes, y_nodes, z_nodes), levels.shape, strict=True)]
    raw = jnp.concatenate([adjoint_load, jnp.pad(levels, room).astype(F32)[None]], axis=0)
    own, half = pack(raw, swap(raw, "gz"))
    a, ax = sided(own, 1), sided(own, 1, True)
    half_x = swap(half, "gx")
    blocks = [own, a, ax, swap(lax.optimization_barrier((a, book))[0], "gz"), swap(ax, "gz"), half_x, swap(half_x, "gz")]

    def held(count, height=24):
        return pltpu.VMEM((count, height, LANES), F32)

    fine_scratch = [
        held(ROWS),
        held(ROWS),
        held(ROWS),
        pltpu.VMEM((ROWS + 1, 96, WIDE), BF16),
        pltpu.VMEM((32, LANES), F32),
    ]
    prods = [pltpu.VMEM((128, LANES), F32)] * (AHEAD + 1)
    limit = pltpu.CompilerParams(vmem_limit_bytes=24 * 1024 * 1024)
    load, moduli, inverse, smoothed, note = pl.pallas_call(
        before_kernel,
        out_shape=[
            jax.ShapeDtypeStruct(shape, F32)
            for shape in [(ROWS, 24, LANES), (ROWS, 8, LANES), (ROWS, 24, LANES), (24 * OWN, LANES), (NOTE, LANES)]
        ],
        in_specs=[scalars] + [there] * 8,
        out_specs=[there] * 5,
        scratch_shapes=[pltpu.VMEM(book.shape, BF16), *fine_scratch]
        + [
            held(ROWS),
            held(ROWS, 8),
            held(ROWS),
            pltpu.VMEM((NOTE, LANES), F32),
            pltpu.VMEM((7, 8, 512), F32),
            pltpu.VMEM((8, LANES), F32),
            pltpu.SemaphoreType.DMA((5 * (OWN + 1) + 7,)),
            pltpu.SemaphoreType.DMA((OWN + 4,)),
            *prods,
        ],
        compiler_params=limit,
        name="before",
    )(place, *blocks, book)

    m1, m2 = sided(note, 1), sided(note, 2)
    s1 = sided(smoothed, 1)
    fix = pl.pallas_call(
        coarse_kernel,
        out_shape=jax.ShapeDtypeStruct((ROWS + 1, 16, WIDE), BF16),
        in_specs=[scalars] + [there] * 7,
        out_specs=there,
        scratch_shapes=[
            pltpu.VMEM(coarse_book.shape, BF16),
            held(C_ROWS, 8),
            pltpu.VMEM((5, NOTE, LANES), F32),
            held(C_ROWS, 8),
            held(C_ROWS + 1, 8),
            held(C_ROWS, 8),
            held(C_ROWS, 8),
            pltpu.VMEM((C_ROWS + 1, 16, WIDE), BF16),
            pltpu.VMEM((8, LANES), F32),
            pltpu.SemaphoreType.DMA((7,)),
            *prods,
        ],
        compiler_params=limit,
        cost_estimate=pl.CostEstimate(flops=4 * 10**9, bytes_accessed=4 * 10**7, transcendentals=0),
        name="coarse",
    )(place, note, m1, swap(m1, "gz"), m2, swap(m2, "gz"), moduli, coarse_book)
    return pl.pallas_call(
        after_kernel,
        out_shape=jax.ShapeDtypeStruct(adjoint_load.shape, F32),
        in_specs=[scalars] + [there] * 8,
        out_specs=whole,
        scratch_shapes=[
            pltpu.VMEM(after_book.shape, BF16),
            *fine_scratch,
            held(ROWS, 8),
            held(ROWS),
            pltpu.VMEM((ROWS + 1, 16, WIDE), BF16),
            pltpu.SemaphoreType.DMA((3 * OWN + 5,)),
            *prods,
        ],
        compiler_params=limit,
        name="after",
    )(place, fix, smoothed, s1, swap(s1, "gz"), load, moduli, inverse, after_book)


def solution(mesh):
    return jax.shard_map(
        per_device,
        mesh=mesh,
        in_specs=(P(None, "gx", "gy", "gz"), P("gx", "gy", "gz"), P(), P()),
        out_specs=P(None, "gx", "gy", "gz"),
        check_vma=False,
    )
```

```python
from typing import NamedTuple

import jax
import jax.numpy as jnp
import numpy as np
from jax import lax
from jax.experimental import pallas as pl
from jax.experimental.pallas import tpu as pltpu
from jax.sharding import PartitionSpec as P

DEG = 4
DENSITY_LEVELS = 16
MID = 1.125
HALF = 0.875

F32 = jnp.float32
BF16 = jnp.bfloat16

OWN = 4
SIDE = 4
FAR = 8
ROWS = OWN + 2 * SIDE
C_ROWS = OWN + 2 * FAR
LANES = 1024
WIDE = LANES + 128
AHEAD = 2
PART = 56
PACK = 104
NOTE = 24


def node_row(group, row):
    px, py = ((0, 0), (1, 0), (0, 1))[group]
    if row < 6:
        return row % 3, px, py, row // 3
    return group, 1, 1, row - 6


FINE_IN = [(g, sx, sy) for sx, sy, groups in ((0, 0, (0, 1, 2)), (1, 0, (0, 2)), (0, 1, (0, 1)), (1, 1, (0,))) for g in groups]
SHIFTS = [(0, 0), (1, 0), (0, 1), (1, 1)]


def fine_place(group, row, sx, sy, sz):
    p, px, py, pz = node_row(group, row)
    if (sx and px) or (sy and py) or (sz and pz):
        return None
    return 27 * p + 9 * (px + 2 * sx) + 3 * (py + 2 * sy) + pz + 2 * sz


def coarse_place(row, sx, sy, sz):
    return 8 * row + 4 * sx + 2 * sy + sz if row < 3 else None


def fine_selectors():
    out_rows = np.zeros((128, 81), np.float32)
    in_rows = np.zeros((256, 81), np.float32)
    at = 0
    for sz in (0, 1):
        for g, sx, sy in FINE_IN:
            for row in range(8):
                place = fine_place(g, row, sx, sy, sz)
                if place is not None:
                    out_rows[at + row, place] = 1.0
            at += 8
    at = 0
    for g, sx, sy in FINE_IN:
        for sz in (0, 1):
            for row in range(8):
                place = fine_place(g, row, sx, sy, sz)
                if place is not None:
                    in_rows[at + row, place] = 1.0
                    in_rows[at + 8 + row, place] = 1.0
            at += 16
    return out_rows, in_rows


def coarse_selectors():
    out_rows = np.zeros((32, 24), np.float32)
    in_rows = np.zeros((64, 24), np.float32)
    for at, (sx, sy) in enumerate(SHIFTS):
        for sz in (0, 1):
            for row in range(3):
                place = coarse_place(row, sx, sy, sz)
                out_rows[8 * at + 3 * sz + row, place] = 1.0
                in_rows[[16 * at + 3 * sz + row, 16 * at + 8 + 3 * sz + row], place] = 1.0
    return out_rows, in_rows


def weight_along(parity, shift):
    if parity == 0:
        return 1.0 if shift == 0 else 0.0
    return 0.5


def transfer_weights():
    prolong = np.zeros((24, 64), np.float32)
    restrict = np.zeros((32, 48), np.float32)
    for at, (sx, sy) in enumerate(SHIFTS):
        for sz in (0, 1):
            for g in range(3):
                for row in range(8):
                    p, px, py, pz = node_row(g, row)
                    w = weight_along(px, sx) * weight_along(py, sy) * weight_along(pz, sz)
                    prolong[8 * g + row, [16 * at + 3 * sz + p, 16 * at + 8 + 3 * sz + p]] = w
                    restrict[8 * at + 3 * sz + p, [16 * g + row, 16 * g + 8 + row]] = w
    return prolong, restrict


def row_shuffle():
    shuffle = np.zeros((96, 96), np.float32)
    for y in range(4):
        for g in range(3):
            for row in range(8):
                p, px, py, pz = node_row(g, row)
                shuffle[24 * y + 8 * g + row, pz * 48 + p * 16 + px * 8 + 2 * y + py] = 1.0
    return np.concatenate([shuffle, shuffle], axis=1)


def diag_selectors():
    fine_rows, fine_at = np.zeros((24, 81), np.float32), np.zeros((81, 16), np.float32)
    coarse_rows, coarse_at = np.zeros((8, 24), np.float32), np.zeros((24, 16), np.float32)
    for at in range(8):
        sy, sx, sz = at // 4, at // 2 % 2, at % 2
        for g in range(3):
            for row in range(8):
                place = fine_place(g, row, sx, sy, sz)
                if place is not None:
                    fine_rows[8 * g + row, place] = 1.0
                    fine_at[place, [at, at + 8]] = 1.0
        for row in range(3):
            place = coarse_place(row, sx, sy, sz)
            coarse_rows[row, place] = 1.0
            coarse_at[place, [at, at + 8]] = 1.0
    return fine_rows, fine_at, coarse_rows, coarse_at


def laid_out(parts):
    places, at = {}, 0
    for name, (rows, columns) in parts.items():
        places[name] = (at, rows, columns)
        at += -(-rows // 16) * 16
    return places, at


def constants():
    fine_out, fine_in = fine_selectors()
    coarse_out, coarse_in = coarse_selectors()
    fine_rows, fine_at, coarse_rows, coarse_at = diag_selectors()
    prolong, restrict = transfer_weights()
    return {
        "fine_out": fine_out, "fine_in": fine_in.T, "fine_rows": fine_rows, "fine_at": fine_at,
        "coarse_out": coarse_out, "coarse_in": coarse_in.T, "coarse_rows": coarse_rows, "coarse_at": coarse_at,
        "restrict": restrict, "prolong": prolong, "shuffle": row_shuffle(),
    }


CARDS, CARD_ROWS = laid_out({name: value.shape for name, value in constants().items()})
BOOKS = [
    laid_out({"fine": (256, 256), "fine_diag": (48, 16), "restrict": (32, 48)}),
    laid_out({"coarse": (64, 64), "coarse_diag": (16, 16)}),
    laid_out({"fine": (256, 256), "prolong": (24, 64), "shuffle": (96, 192)}),
]


def cards():
    sheet = np.zeros((CARD_ROWS, 256), np.float32)
    for name, value in constants().items():
        first, rows, columns = CARDS[name]
        sheet[first : first + rows, :columns] = value
    return jnp.asarray(sheet, dtype=BF16)


class Part:
    def __init__(self, ref, places, name):
        first, rows, columns = places[name]
        self.ref, self.at = ref, (slice(first, first + rows), slice(0, columns))

    def __getitem__(self, _):
        return self.ref[self.at]

    def __setitem__(self, _, values):
        self.ref[self.at] = values


def halves(values):
    high = values.astype(BF16).astype(F32)
    return high, (values - high).astype(BF16).astype(F32)


def fetched(copies, sems, first=0):
    started = [pltpu.make_async_copy(a, b, sems.at[first + i]) for i, (a, b) in enumerate(copies)]
    for copy in started:
        copy.start()
    return started


def wait_for(started):
    for copy in started:
        copy.wait()


def pack_kernel(place_ref, raw_sent, other_sent, out_ref, half_ref, raw, other, sems):
    gz = place_ref[2]
    copies = fetched([(raw_sent, raw), (other_sent, other)], sems)

    row = lax.broadcasted_iota(jnp.int32, (256, 256), 0)
    col = lax.broadcasted_iota(jnp.int32, (256, 256), 1)
    parter = jnp.where(2 * (col & 127) + (col >> 7) == ((row + 128 * gz) & 255), 1.0, 0.0).astype(BF16)
    row = lax.broadcasted_iota(jnp.int32, (256, 128), 0)
    col = lax.broadcasted_iota(jnp.int32, (256, 128), 1)
    half = jnp.where(row < 128, gz, 1 - gz)
    widen = jnp.where(((row & 127) < 64) & (col == (row & 127) + 64 * half), 1.0, 0.0).astype(BF16)

    row = lax.broadcasted_iota(jnp.int32, (96, 192), 0)
    col = lax.broadcasted_iota(jnp.int32, (96, 192), 1)
    y = sum(jnp.where(row >= 24 * i, 1, 0) for i in (1, 2, 3))
    group, at = (row >> 3) - 3 * y, row & 7
    back = jnp.where(at >= 3, 1, 0)
    corner = at >= 6
    component = jnp.where(corner, group, at - 3 * back)
    pz = jnp.where(corner, at - 6, back)
    px = jnp.where(corner | (group == 1), 1, 0)
    py = jnp.where(corner | (group == 2), 1, 0)
    source = 48 * pz + 16 * component + 8 * px + 2 * y + py
    shuffle = jnp.where(jnp.where(col >= 96, col - 96, col) == source, 1.0, 0.0).astype(BF16)

    wait_for(copies)
    high, low = halves(jnp.concatenate([raw[0:3].reshape(192, 128), other[0:3].reshape(192, 128)], axis=1))
    parted = jnp.dot(jnp.concatenate([high, low], axis=0).astype(BF16), parter, preferred_element_type=F32)
    parted = parted.reshape(2, 3, 8, 8, 256)
    pieces = []
    for x in range(4):
        near = parted[:, :, 2 * x : 2 * x + 2].reshape(2, 48, 256)
        pieces.append(
            jnp.concatenate([near[0, :, :128], near[0, :, 128:], near[1, :, :128], near[1, :, 128:]], axis=0)
        )
    stacked = jnp.concatenate(pieces, axis=1).astype(BF16)
    out_ref[0:96, :] = jnp.dot(shuffle, stacked, preferred_element_type=F32)

    levels = jnp.concatenate([raw[3, 0:4].reshape(32, 128), other[3, 0:4].reshape(32, 128)], axis=1)
    ratio = jnp.dot(levels.astype(BF16), widen, preferred_element_type=F32) / (DENSITY_LEVELS - 1)
    moduli = 0.05 + 0.95 * ratio * ratio * ratio
    for x in range(4):
        out_ref[96:104, 128 * x : 128 * x + 128] = moduli[8 * x : 8 * x + 8]
    half_ref[...] = out_ref[pl.ds(pl.multiple_of((PACK - PART) * gz, 8), PART), :]


def split(values):
    high = values.astype(BF16).astype(F32)
    return jnp.concatenate([high, values - high], axis=0).astype(BF16)


def roll_tiles(values, step):
    tiles = []
    for t in range(values.shape[1] // 128):
        tile = values[:, 128 * t : 128 * t + 128]
        lane = lax.broadcasted_iota(jnp.int32, tile.shape, 1)
        if step == 1:
            tiles.append(jnp.where(lane < 127, pltpu.roll(tile, 127, 1), 0.0))
        else:
            tiles.append(jnp.where(lane > 0, pltpu.roll(tile, 1, 1), 0.0))
    return tiles[0] if len(tiles) == 1 else jnp.concatenate(tiles, axis=1)


def hi_lo_weights(matrix, left, right):
    high, low = halves(matrix)
    col = lax.broadcasted_iota(jnp.int32, right.shape, 1)
    right_high = jnp.where(col % 16 < 8, right.astype(F32), 0.0).astype(BF16)
    rows = [
        jnp.dot(jnp.dot(left, part.astype(BF16), preferred_element_type=F32).astype(BF16), to, preferred_element_type=F32)
        for part, to in ((high, right), (low, right_high))
    ]
    return jnp.concatenate(rows, axis=0).astype(BF16)


def weights_kernel(fine_ref, coarse_ref, cards_ref, *book_refs):
    def card(name):
        return Part(cards_ref, CARDS, name)[...]

    matrices = {name: card(name) for name in ("restrict", "prolong", "shuffle")}
    for name, ref in (("fine", fine_ref), ("coarse", coarse_ref)):
        matrix = ref[...]
        row = lax.broadcasted_iota(jnp.int32, matrix.shape, 0)
        col = lax.broadcasted_iota(jnp.int32, matrix.shape, 1)
        diagonal = jnp.where(row == col, matrix, 0.0)
        matrices[name] = hi_lo_weights(matrix, card(name + "_out"), card(name + "_in"))
        matrices[name + "_diag"] = hi_lo_weights(diagonal, card(name + "_rows"), card(name + "_at"))
    for (places, _), book_ref in zip(BOOKS, book_refs, strict=True):
        for name in places:
            Part(book_ref, places, name)[...] = matrices[name]


def scaled(values, moduli):
    rows, lanes = values.shape
    return (values.reshape(rows // 8, 8, lanes) * moduli[None]).reshape(rows, lanes)


class Step(NamedTuple):
    row: int
    keep: float = 0.0
    gain: float = 0.0
    last: bool = False
    lead: bool = False
    tail: bool = False
    operand: bool = True
    residual: bool = True


def schedules():
    sigma = MID / HALF
    rhos = [1.0 / sigma]
    for _ in range(DEG - 1):
        rhos.append(1.0 / (2.0 * sigma - rhos[-1]))
    smooth = [(rhos[s + 1] * rhos[s], 2.0 * rhos[s + 1] / HALF) for s in range(DEG - 1)]
    o, c = SIDE, FAR

    def smoothing(sweeps, operand, residual):
        steps = []
        for at, (first, last, keep, gain) in enumerate(sweeps):
            final = at == len(sweeps) - 1
            reads = operand if final else range(sweeps[at + 1][0], sweeps[at + 1][1] + 1)
            sums = residual if final else range(sweeps[at + 1][0] + 1, sweeps[at + 1][1])
            for row in range(first, last):
                steps.append(Step(row, keep, gain, final, row == first, row == last - 1, row in reads, row in sums))
        return steps

    return {
        "start": [Step(row) for row in range(o - 3, o + 8)],
        "before": smoothing(
            [(o - 3 + s, o + 7 - s, *smooth[s]) for s in range(DEG - 1)], range(o, o + 5), range(o, o + 4)
        ),
        "leave": [Step(row) for row in range(o, o + 4)],
        "coarse_start": [Step(row) for row in range(c - 7, c + 11)],
        "coarse": smoothing(
            [(c - 7 + s, c + 10 - s, *smooth[s]) for s in range(DEG - 1)], range(c - 4, c + 8), range(0)
        ),
        "correct": [Step(row) for row in range(o - 4, o + 8)],
        "after": smoothing(
            [(o - 4, o + 7, 0.0, 1.0 / MID)] + [(o - 3 + s, o + 6 - s, *smooth[s]) for s in range(DEG - 1)],
            range(0),
            range(0),
        ),
    }


OWN_ROWS = range(SIDE, SIDE + OWN)


CHUNKS = [(256 * n, slice(256 * n, 256 * n + 256)) for n in range(4)]


def pushed(before, values):
    return jnp.concatenate([before, values[:, :128]], axis=1)


def store_fine(fine_x, y, lanes, values):
    for g in range(3):
        part = values[8 * g : 8 * g + 8]
        fine_x[y, 32 * g : 32 * g + 16, lanes] = split(part)
        fine_x[y, 32 * g + 16 : 32 * g + 32, lanes] = split(roll_tiles(part, 1))


def store_coarse(coarse_x, y, lanes, values):
    row = lax.broadcasted_iota(jnp.int32, values.shape, 0)
    further = pltpu.roll(roll_tiles(values, 1), 3, 0)
    coarse_x[y, :, lanes] = split(jnp.where(row < 3, values, jnp.where(row < 6, further, 0.0)))


def pipeline(prods, name, issue, finish):
    steps = schedules()[name]
    for t in range(len(steps) + AHEAD):
        if t < len(steps):
            issue(steps[t].row, prods[t % len(prods)])
        if t >= AHEAD:
            finish(steps[t - AHEAD], prods[(t - AHEAD) % len(prods)])


def fine_issue(fine_w, fine_x):
    def issue(y, prod):
        for low, lanes in CHUNKS:
            there = slice(low + 128, low + 384)
            operand = jnp.concatenate(
                [
                    fine_x[y, :, lanes],
                    fine_x[y, 0:32, there],
                    fine_x[y, 64:96, there],
                    fine_x[y + 1, 0:64, lanes],
                    fine_x[y + 1, 0:32, there],
                ],
                axis=0,
            )
            products = jnp.dot(fine_w[...], operand, preferred_element_type=F32)
            prod[:, lanes] = products[:128] + products[128:]

    return issue


def fine_finish(moduli, carry, use):
    def finish(now, prod):
        y = now.row
        before = [(jnp.zeros((16, 128), F32), jnp.zeros((8, 128), F32))] * 2
        for low, lanes in CHUNKS:
            m = moduli[y, :, lanes]
            sums = []
            for z in range(2):
                v = scaled(prod[64 * z : 64 * z + 64, lanes], m)
                if not now.lead:
                    old = carry[16 * z : 16 * z + 16, lanes]
                    along_x = pushed(before[z][0], v[24:40])
                    sums.append(
                        jnp.concatenate(
                            [v[0:8] + along_x[0:8] + old[0:8], v[8:16] + old[8:16], v[16:24] + along_x[8:16]], axis=0
                        )
                    )
                if not now.tail:
                    along_xy = pushed(before[z][1], v[56:64])
                    carry[16 * z : 16 * z + 16, lanes] = jnp.concatenate([v[40:48] + along_xy, v[48:56]], axis=0)
                before[z] = (v[24:40, 128:], v[56:64, 128:])
            if not now.lead:
                use(now, y, lanes, sums[0] + roll_tiles(sums[1], -1))

    return finish


def coarse_finish(moduli, carry, use):
    def finish(now, prod):
        y = now.row
        before = (jnp.zeros((8, 128), F32), jnp.zeros((8, 128), F32))
        for low, lanes in CHUNKS:
            v = prod[0:32, lanes]
            if moduli is not None:
                v = scaled(v, moduli[y, :, lanes])
            if not now.lead:
                sums = v[0:8] + pushed(before[0], v[8:16]) + carry[:, lanes]
            if not now.tail:
                carry[:, lanes] = v[16:24] + pushed(before[1], v[24:32])
            before = (v[8:16, 128:], v[24:32, 128:])
            if not now.lead:
                use(now, y, lanes, sums + roll_tiles(pltpu.roll(sums, 5, 0), -1))

    return finish


def smooth_fine(inverse, res, step, total, fine_x):
    def use(now, y, lanes, sums):
        if not (now.operand or now.residual or y in OWN_ROWS):
            return
        r = res[y, :, lanes] - sums
        d = now.gain * (inverse[y, :, lanes] * r)
        if now.keep:
            d = now.keep * step[y, :, lanes] + d
        if now.residual:
            res[y, :, lanes] = r
            step[y, :, lanes] = d
        if y in OWN_ROWS:
            total[y, :, lanes] = total[y, :, lanes] + d
        if now.operand:
            store_fine(fine_x, y, lanes, d)

    return use


def diag_issue(diag_w, moduli, count):
    def issue(y, prod):
        spot = lax.broadcasted_iota(jnp.int32, (8, 256), 0)
        before = jnp.zeros((8, 128), F32)
        for low, lanes in CHUNKS:
            near = jnp.where(spot < 4, moduli[y, :, lanes], moduli[max(y - 1, 0), :, lanes])
            moved = pushed(before, near)
            before = near[:, 128:]
            around = jnp.where(spot % 4 < 2, near, moved)
            around = jnp.where(spot % 2 < 1, around, roll_tiles(around, -1))
            products = jnp.dot(diag_w[...], split(around), preferred_element_type=F32)
            prod[0:count, lanes] = products[:count] + products[count:]

    return issue


def clear_tail(ref, rows):
    def clear(y, _):
        ref[y, :, LANES:] = jnp.zeros((ref.shape[1], 128), BF16)
        return 0

    lax.fori_loop(0, rows, clear, 0)


def validity(place_ref, ahead):
    first, count = place_ref[1] * OWN - ahead, place_ref[3] * OWN

    def valid(y):
        return jnp.where((first + y >= 0) & (first + y < count), 1.0, 0.0).astype(F32)

    return valid


def before_kernel(place_ref, *refs):
    blocks = refs[:7]
    book_ref, outs = refs[7], refs[8:13]
    (book, res, step, total, fine_x, carry, load, moduli, inverse, note, moduli_rows, c_carry, sems, out_sems, *prods) = refs[13:]
    gx, gz = place_ref[0], place_ref[2]
    valid = validity(place_ref, SIDE)
    o = SIDE

    own, a, ax, za, zax, half, half_other = blocks
    lanes_of = [pl.ds(pl.multiple_of(x * 512, 512), 512) for x in (gx, 1 - gx)]
    side = 1 - 2 * gz
    spots = [(own, 0, 0), (a, -side, 0), (ax, -side, 1), (za, side, 0), (zax, side, 1)]
    fine_w, diag_w, restrict_w = [Part(book, BOOKS[0][0], name) for name in BOOKS[0][0]]
    copies = [(book_ref, book)]
    for i, (ref, offset, across) in enumerate(spots):
        copies.append((ref.at[96:104, :], moduli_rows.at[i]))
        for y in range(OWN):
            copies.append((ref.at[24 * y : 24 * y + 24, :], load.at[o + OWN * offset + y, :, lanes_of[across]]))
    for i, (ref, core) in enumerate([(half, gz), (half_other, 1 - gz)]):
        copies.append((ref.at[PART - 8 : PART, :], moduli_rows.at[5 + i]))
        for y in range(2):
            first = pl.multiple_of(24 * y + (PACK - PART - 48) * core, 8)
            copies.append((ref.at[pl.ds(first, 24), :], load.at[o + 2 * core + y, :, lanes_of[1]]))
    copies = fetched(copies, sems)
    clear_tail(fine_x, ROWS)
    carry[...] = jnp.zeros_like(carry)
    wait_for(copies)
    own_rows = jnp.where(jnp.full((8, 512), gz) == 1, moduli_rows[5], moduli_rows[6])
    for rows, offset, across in [(moduli_rows[i], *spot[1:]) for i, spot in enumerate(spots)] + [(own_rows, 0, 1)]:
        for y in range(OWN):
            moduli[o + OWN * offset + y, :, lanes_of[across]] = jnp.broadcast_to(rows[y : y + 1], (8, 512))
    leaving = fetched([(load, outs[0]), (moduli, outs[1])], out_sems)

    def start(now, prod):
        y = now.row
        ok = valid(y)
        for low, lanes in CHUNKS:
            inv = ok / (prod[0:24, lanes] + (1.0 - ok))
            r = load[y, :, lanes]
            d = inv * r * (1.0 / MID)
            inverse[y, :, lanes] = inv
            res[y, :, lanes] = r
            step[y, :, lanes] = d
            if y in OWN_ROWS:
                total[y, :, lanes] = d
            store_fine(fine_x, y, lanes, d)

    pipeline(prods, "start", diag_issue(diag_w, moduli, 24), start)
    leaving += fetched([(inverse, outs[2])], out_sems, len(leaving))
    issue = fine_issue(fine_w, fine_x)
    use = smooth_fine(inverse, res, step, total, fine_x)
    pipeline(prods, "before", issue, fine_finish(moduli, carry, use))
    leaving += fetched([(total.at[o : o + OWN], outs[3])], out_sems, len(leaving))

    carry[...] = jnp.zeros_like(carry)

    def store_left(y, lanes, left):
        for g in range(3):
            fine_x[y, 16 * g : 16 * g + 16, lanes] = split(left[8 * g : 8 * g + 8])

    def leave(now, y, lanes, sums):
        store_left(y, lanes, res[y, :, lanes] - sums)

    pipeline(prods, "leave", issue, fine_finish(moduli, carry, leave))
    for low, lanes in CHUNKS:
        last = carry[0:16, lanes] + roll_tiles(carry[16:32, lanes], -1)
        last = jnp.concatenate([last, jnp.zeros((8, 256), F32)], axis=0)
        store_left(o + OWN, lanes, -last * valid(o + OWN))

    c_carry[...] = jnp.zeros_like(c_carry)
    for j in range(OWN + 1):
        prod = prods[j % len(prods)]
        for low, lanes in CHUNKS:
            prod[0:32, lanes] = jnp.dot(restrict_w[...], fine_x[o + j, 0:48, lanes], preferred_element_type=F32)

        def keep(now, y, lanes, sums, j=j):
            note[3 * j : 3 * j + 3, lanes] = sums[0:3]

        coarse_finish(None, c_carry, keep)(Step(o + j), prod)
    for y in range(OWN):
        note[16 + y : 17 + y, :] = moduli[o + y, 0:1, :]
    leaving += fetched([(note, outs[4])], out_sems, len(leaving))
    wait_for(leaving)


def coarse_operand(coarse_x, y, low, lanes):
    there = slice(low + 128, low + 384)
    return jnp.concatenate(
        [coarse_x[y, :, lanes], coarse_x[y, :, there], coarse_x[y + 1, :, lanes], coarse_x[y + 1, :, there]], axis=0
    )


def coarse_kernel(place_ref, *refs):
    note, m1, zm1, m2, zm2, near_moduli, book_ref, fix = refs[:8]
    book, moduli, notes, c_inverse, c_res, c_step, c_total, coarse_x, c_carry, sems, *prods = refs[8:]
    gz = place_ref[2]
    o, c = SIDE, FAR
    valid = validity(place_ref, FAR)
    side = 1 - 2 * gz

    spots = [(note, 0), (m1, -side), (zm1, side), (m2, -2 * side), (zm2, 2 * side)]
    copies = [(ref, notes.at[i]) for i, (ref, _) in enumerate(spots)]
    copies.append((near_moduli, moduli.at[c - o : c - o + ROWS]))
    copies.append((book_ref, book))
    coarse_w, diag_w = [Part(book, BOOKS[1][0], name) for name in BOOKS[1][0]]
    copies = fetched(copies, sems)
    clear_tail(coarse_x, C_ROWS)
    c_carry[...] = jnp.zeros_like(c_carry)
    c_res[...] = jnp.zeros_like(c_res)
    wait_for(copies)
    for i, (_, offset) in enumerate(spots):
        at = c + OWN * offset
        if i >= 3:
            for y in range(OWN):
                moduli[at + y] = jnp.broadcast_to(notes[i, 16 + y : 17 + y, :], (8, LANES))
        for y in range(OWN + 1):
            c_res[at + y, 0:3, :] = c_res[at + y, 0:3, :] + notes[i, 3 * y : 3 * y + 3, :]

    def start(now, prod):
        y = now.row
        ok = valid(y)
        for low, lanes in CHUNKS:
            used = lax.broadcasted_iota(jnp.int32, (8, 256), 0) < 3
            inv = jnp.where(used, ok / (prod[0:8, lanes] + (1.0 - ok)), 0.0)
            d = inv * c_res[y, :, lanes] * (1.0 / MID)
            c_inverse[y, :, lanes] = inv
            c_step[y, :, lanes] = d
            c_total[y, :, lanes] = d
            store_coarse(coarse_x, y, lanes, d)

    pipeline(prods, "coarse_start", diag_issue(diag_w, moduli, 8), start)

    def issue(y, prod):
        for low, lanes in CHUNKS:
            products = jnp.dot(coarse_w[...], coarse_operand(coarse_x, y, low, lanes), preferred_element_type=F32)
            prod[0:32, lanes] = products[:32] + products[32:]

    def smooth(now, y, lanes, sums):
        if not (now.operand or now.residual):
            return
        r = c_res[y, :, lanes] - sums
        d = now.keep * c_step[y, :, lanes] + now.gain * (c_inverse[y, :, lanes] * r)
        so_far = c_total[y, :, lanes] + d
        if now.residual:
            c_res[y, :, lanes] = r
            c_step[y, :, lanes] = d
            c_total[y, :, lanes] = so_far
        store_coarse(coarse_x, y, lanes, so_far if now.last else d)

    pipeline(prods, "coarse", issue, coarse_finish(moduli, c_carry, smooth))
    wait_for(fetched([(coarse_x.at[c - o : c - o + ROWS + 1], fix)], sems))


def after_kernel(place_ref, *refs):
    fix_sent, s0, s1, zs1, load_sent, moduli_sent, inverse_sent, book_ref, out_ref = refs[:9]
    (book, res, step, total, fine_x, carry, moduli, inverse, fix, sems, *prods) = refs[9:]
    gx, gz = place_ref[0], place_ref[2]
    o = SIDE
    side = 1 - 2 * gz

    fine_w, prolong_w, shuffle = [Part(book, BOOKS[2][0], name) for name in BOOKS[2][0]]
    copies = [(fix_sent, fix), (load_sent, res), (book_ref, book)]
    for ref, offset in [(s0, 0), (s1, -side), (zs1, side)]:
        copies.append((ref, total.at[pl.ds(o + OWN * offset, OWN)]))
    first = fetched(copies, sems)
    second = fetched([(inverse_sent, inverse), (moduli_sent, moduli)], sems, len(first))
    clear_tail(fine_x, ROWS)
    carry[...] = jnp.zeros_like(carry)
    wait_for(first)

    def correct_issue(y, prod):
        for low, lanes in CHUNKS:
            prod[0:24, lanes] = jnp.dot(
                prolong_w[...], coarse_operand(fix, y, low, lanes), preferred_element_type=F32
            )

    def correct(now, prod):
        y = now.row
        for low, lanes in CHUNKS:
            corrected = total[y, :, lanes] + prod[0:24, lanes]
            if y in OWN_ROWS:
                total[y, :, lanes] = corrected
            store_fine(fine_x, y, lanes, corrected)

    pipeline(prods, "correct", correct_issue, correct)
    wait_for(second)
    use = smooth_fine(inverse, res, step, total, fine_x)
    pipeline(prods, "after", fine_issue(fine_w, fine_x), fine_finish(moduli, carry, use))

    row = lax.broadcasted_iota(jnp.int32, (256, 128), 0)
    col = lax.broadcasted_iota(jnp.int32, (256, 128), 1)
    weave = (row == 128 * (col % 2) + 64 * gz + col // 2).astype(F32).astype(BF16)
    lanes = pl.ds(pl.multiple_of(gx * 512, 512), 512)
    high, low = halves(total[o : o + OWN, :, lanes].reshape(96, 512))
    pieces = []
    for part in (high, low):
        back = lax.dot_general(
            shuffle[...][:, 0:96], part.astype(BF16), (((0,), (0,)), ((), ())), preferred_element_type=F32
        )
        for x in range(4):
            near = back[:, 128 * x : 128 * x + 128]
            pieces.append(jnp.concatenate([near[0:48], near[48:96]], axis=1))
    woven = jnp.dot(jnp.concatenate(pieces, axis=0).astype(BF16), weave, preferred_element_type=F32)
    woven = woven[:192] + woven[192:]
    for x in range(4):
        out_ref[:, 2 * x : 2 * x + 2] = woven[48 * x : 48 * x + 48].reshape(3, 2, 8, 128)


def per_device(adjoint_load, levels, fine_stiffness, coarse_stiffness):
    count = lax.axis_size("gy")
    place = jnp.stack(
        [lax.axis_index("gx"), lax.axis_index("gy"), lax.axis_index("gz"), jnp.int32(count)]
    ).astype(jnp.int32)

    def swap(value, axis):
        return lax.ppermute(value, axis, [(0, 1), (1, 0)])

    def sided(value, steps, across=False):
        pairs = []
        for gx in range(2):
            for i in range(count - steps):
                low, high = 2 * (gx * count + i), 2 * (gx * count + i + steps)
                other = 2 * count * (1 - 2 * gx) if across else 0
                pairs += [(low, high + other), (high + 1, low + other + 1)]
        return lax.ppermute(value, ("gx", "gy", "gz"), pairs)

    whole = pl.BlockSpec(memory_space=pltpu.VMEM)
    there = pl.BlockSpec(memory_space=pl.ANY)
    scalars = pl.BlockSpec(memory_space=pltpu.SMEM)

    def pack(raw, other):
        return pl.pallas_call(
            pack_kernel,
            out_shape=[jax.ShapeDtypeStruct((rows, 512), F32) for rows in (PACK, PART)],
            in_specs=[scalars, there, there],
            out_specs=[whole] * 2,
            scratch_shapes=[pltpu.VMEM(raw.shape, F32)] * 2 + [pltpu.SemaphoreType.DMA((2,))],
            compiler_params=pltpu.CompilerParams(vmem_limit_bytes=8 * 1024 * 1024),
            name="pack",
        )(place, raw, other)

    book, coarse_book, after_book = pl.pallas_call(
        weights_kernel,
        out_shape=[jax.ShapeDtypeStruct((rows, 256), BF16) for _, rows in BOOKS],
        in_specs=[whole] * 3,
        out_specs=[whole] * 3,
        compiler_params=pltpu.CompilerParams(vmem_limit_bytes=8 * 1024 * 1024),
        name="weights",
    )(fine_stiffness, coarse_stiffness, cards())

    _, x_nodes, y_nodes, z_nodes = adjoint_load.shape
    room = [(0, whole_size - size) for whole_size, size in zip((x_nodes, y_nodes, z_nodes), levels.shape, strict=True)]
    raw = jnp.concatenate([adjoint_load, jnp.pad(levels, room).astype(F32)[None]], axis=0)
    own, half = pack(raw, swap(raw, "gz"))
    a, ax = sided(own, 1), sided(own, 1, True)
    half_x = swap(half, "gx")
    blocks = [own, a, ax, swap(lax.optimization_barrier((a, book))[0], "gz"), swap(ax, "gz"), half_x, swap(half_x, "gz")]

    def held(count, height=24):
        return pltpu.VMEM((count, height, LANES), F32)

    fine_scratch = [
        held(ROWS),
        held(ROWS),
        held(ROWS),
        pltpu.VMEM((ROWS + 1, 96, WIDE), BF16),
        pltpu.VMEM((32, LANES), F32),
    ]
    prods = [pltpu.VMEM((128, LANES), F32)] * (AHEAD + 1)
    limit = pltpu.CompilerParams(vmem_limit_bytes=24 * 1024 * 1024)
    load, moduli, inverse, smoothed, note = pl.pallas_call(
        before_kernel,
        out_shape=[
            jax.ShapeDtypeStruct(shape, F32)
            for shape in [(ROWS, 24, LANES), (ROWS, 8, LANES), (ROWS, 24, LANES), (OWN, 24, LANES), (NOTE, LANES)]
        ],
        in_specs=[scalars] + [there] * 8,
        out_specs=[there] * 5,
        scratch_shapes=[pltpu.VMEM(book.shape, BF16), *fine_scratch]
        + [
            held(ROWS),
            held(ROWS, 8),
            held(ROWS),
            pltpu.VMEM((NOTE, LANES), F32),
            pltpu.VMEM((7, 8, 512), F32),
            pltpu.VMEM((8, LANES), F32),
            pltpu.SemaphoreType.DMA((5 * (OWN + 1) + 7,)),
            pltpu.SemaphoreType.DMA((5,)),
            *prods,
        ],
        compiler_params=limit,
        name="before",
    )(place, *blocks, book)

    m1, m2 = sided(note, 1), sided(note, 2)
    s1 = sided(smoothed, 1)
    fix = pl.pallas_call(
        coarse_kernel,
        out_shape=jax.ShapeDtypeStruct((ROWS + 1, 16, WIDE), BF16),
        in_specs=[scalars] + [there] * 7,
        out_specs=there,
        scratch_shapes=[
            pltpu.VMEM(coarse_book.shape, BF16),
            held(C_ROWS, 8),
            pltpu.VMEM((5, NOTE, LANES), F32),
            held(C_ROWS, 8),
            held(C_ROWS + 1, 8),
            held(C_ROWS, 8),
            held(C_ROWS, 8),
            pltpu.VMEM((C_ROWS + 1, 16, WIDE), BF16),
            pltpu.VMEM((8, LANES), F32),
            pltpu.SemaphoreType.DMA((7,)),
            *prods,
        ],
        compiler_params=limit,
        cost_estimate=pl.CostEstimate(flops=4 * 10**9, bytes_accessed=4 * 10**7, transcendentals=0),
        name="coarse",
    )(place, note, m1, swap(m1, "gz"), m2, swap(m2, "gz"), moduli, coarse_book)
    return pl.pallas_call(
        after_kernel,
        out_shape=jax.ShapeDtypeStruct(adjoint_load.shape, F32),
        in_specs=[scalars] + [there] * 8,
        out_specs=whole,
        scratch_shapes=[
            pltpu.VMEM(after_book.shape, BF16),
            *fine_scratch,
            held(ROWS, 8),
            held(ROWS),
            pltpu.VMEM((ROWS + 1, 16, WIDE), BF16),
            pltpu.SemaphoreType.DMA((8,)),
            *prods,
        ],
        compiler_params=limit,
        name="after",
    )(place, fix, smoothed, s1, swap(s1, "gz"), load, moduli, inverse, after_book)


def solution(mesh):
    return jax.shard_map(
        per_device,
        mesh=mesh,
        in_specs=(P(None, "gx", "gy", "gz"), P("gx", "gy", "gz"), P(), P()),
        out_specs=P(None, "gx", "gy", "gz"),
        check_vma=False,
    )
```

```python
from typing import NamedTuple

import jax
import jax.numpy as jnp
import numpy as np
from jax import lax
from jax.experimental import pallas as pl
from jax.experimental.pallas import tpu as pltpu
from jax.sharding import PartitionSpec as P

DEG = 4
DENSITY_LEVELS = 16
MID = 1.125
HALF = 0.875

F32 = jnp.float32
BF16 = jnp.bfloat16

OWN = 4
SIDE = 4
FAR = 8
ROWS = OWN + 2 * SIDE
C_ROWS = OWN + 2 * FAR
LANES = 1024
WIDE = LANES + 128
AHEAD = 2
PART = 56
PACK = 104
NOTE = 24


def node_row(group, row):
    px, py = ((0, 0), (1, 0), (0, 1))[group]
    if row < 6:
        return row % 3, px, py, row // 3
    return group, 1, 1, row - 6


FINE_IN = [(g, sx, sy) for sx, sy, groups in ((0, 0, (0, 1, 2)), (1, 0, (0, 2)), (0, 1, (0, 1)), (1, 1, (0,))) for g in groups]
SHIFTS = [(0, 0), (1, 0), (0, 1), (1, 1)]


def fine_place(group, row, sx, sy, sz):
    p, px, py, pz = node_row(group, row)
    if (sx and px) or (sy and py) or (sz and pz):
        return None
    return 27 * p + 9 * (px + 2 * sx) + 3 * (py + 2 * sy) + pz + 2 * sz


def coarse_place(row, sx, sy, sz):
    return 8 * row + 4 * sx + 2 * sy + sz if row < 3 else None


def fine_selectors():
    out_rows = np.zeros((128, 81), np.float32)
    in_rows = np.zeros((256, 81), np.float32)
    at = 0
    for sz in (0, 1):
        for g, sx, sy in FINE_IN:
            for row in range(8):
                place = fine_place(g, row, sx, sy, sz)
                if place is not None:
                    out_rows[at + row, place] = 1.0
            at += 8
    at = 0
    for g, sx, sy in FINE_IN:
        for sz in (0, 1):
            for row in range(8):
                place = fine_place(g, row, sx, sy, sz)
                if place is not None:
                    in_rows[at + row, place] = 1.0
                    in_rows[at + 8 + row, place] = 1.0
            at += 16
    return out_rows, in_rows


def coarse_selectors():
    out_rows = np.zeros((32, 24), np.float32)
    in_rows = np.zeros((64, 24), np.float32)
    for at, (sx, sy) in enumerate(SHIFTS):
        for sz in (0, 1):
            for row in range(3):
                place = coarse_place(row, sx, sy, sz)
                out_rows[8 * at + 3 * sz + row, place] = 1.0
                in_rows[[16 * at + 3 * sz + row, 16 * at + 8 + 3 * sz + row], place] = 1.0
    return out_rows, in_rows


def weight_along(parity, shift):
    if parity == 0:
        return 1.0 if shift == 0 else 0.0
    return 0.5


def transfer_weights():
    prolong = np.zeros((24, 64), np.float32)
    restrict = np.zeros((32, 48), np.float32)
    for at, (sx, sy) in enumerate(SHIFTS):
        for sz in (0, 1):
            for g in range(3):
                for row in range(8):
                    p, px, py, pz = node_row(g, row)
                    w = weight_along(px, sx) * weight_along(py, sy) * weight_along(pz, sz)
                    prolong[8 * g + row, [16 * at + 3 * sz + p, 16 * at + 8 + 3 * sz + p]] = w
                    restrict[8 * at + 3 * sz + p, [16 * g + row, 16 * g + 8 + row]] = w
    return prolong, restrict


def row_shuffle():
    shuffle = np.zeros((96, 96), np.float32)
    for y in range(4):
        for g in range(3):
            for row in range(8):
                p, px, py, pz = node_row(g, row)
                shuffle[24 * y + 8 * g + row, pz * 48 + p * 16 + px * 8 + 2 * y + py] = 1.0
    return np.concatenate([shuffle, shuffle], axis=1)


def diag_selectors():
    fine_rows, fine_at = np.zeros((24, 81), np.float32), np.zeros((81, 16), np.float32)
    coarse_rows, coarse_at = np.zeros((8, 24), np.float32), np.zeros((24, 16), np.float32)
    for at in range(8):
        sy, sx, sz = at // 4, at // 2 % 2, at % 2
        for g in range(3):
            for row in range(8):
                place = fine_place(g, row, sx, sy, sz)
                if place is not None:
                    fine_rows[8 * g + row, place] = 1.0
                    fine_at[place, [at, at + 8]] = 1.0
        for row in range(3):
            place = coarse_place(row, sx, sy, sz)
            coarse_rows[row, place] = 1.0
            coarse_at[place, [at, at + 8]] = 1.0
    return fine_rows, fine_at, coarse_rows, coarse_at


def laid_out(parts):
    places, at = {}, 0
    for name, (rows, columns) in parts.items():
        places[name] = (at, rows, columns)
        at += -(-rows // 16) * 16
    return places, at


def constants():
    fine_out, fine_in = fine_selectors()
    coarse_out, coarse_in = coarse_selectors()
    fine_rows, fine_at, coarse_rows, coarse_at = diag_selectors()
    prolong, restrict = transfer_weights()
    return {
        "fine_out": fine_out, "fine_in": fine_in.T, "fine_rows": fine_rows, "fine_at": fine_at,
        "coarse_out": coarse_out, "coarse_in": coarse_in.T, "coarse_rows": coarse_rows, "coarse_at": coarse_at,
        "restrict": restrict, "prolong": prolong, "shuffle": row_shuffle(),
    }


CARDS, CARD_ROWS = laid_out({name: value.shape for name, value in constants().items()})
BOOKS = [
    laid_out({"fine": (256, 256), "fine_diag": (48, 16), "restrict": (32, 48)}),
    laid_out({"coarse": (64, 64), "coarse_diag": (16, 16)}),
    laid_out({"fine": (256, 256), "prolong": (24, 64), "shuffle": (96, 192)}),
]


def cards():
    sheet = np.zeros((CARD_ROWS, 256), np.float32)
    for name, value in constants().items():
        first, rows, columns = CARDS[name]
        sheet[first : first + rows, :columns] = value
    return jnp.asarray(sheet, dtype=BF16)


class Part:
    def __init__(self, ref, places, name):
        first, rows, columns = places[name]
        self.ref, self.at = ref, (slice(first, first + rows), slice(0, columns))

    def __getitem__(self, _):
        return self.ref[self.at]

    def __setitem__(self, _, values):
        self.ref[self.at] = values


def halves(values):
    high = values.astype(BF16).astype(F32)
    return high, (values - high).astype(BF16).astype(F32)


def fetched(copies, sems, first=0):
    started = [pltpu.make_async_copy(a, b, sems.at[first + i]) for i, (a, b) in enumerate(copies)]
    for copy in started:
        copy.start()
    return started


def wait_for(started):
    for copy in started:
        copy.wait()


def pack_kernel(place_ref, raw_sent, other_sent, out_ref, half_ref, raw, other, sems):
    gz = place_ref[2]
    copies = fetched([(raw_sent, raw), (other_sent, other)], sems)

    row = lax.broadcasted_iota(jnp.int32, (256, 256), 0)
    col = lax.broadcasted_iota(jnp.int32, (256, 256), 1)
    parter = jnp.where(2 * (col & 127) + (col >> 7) == ((row + 128 * gz) & 255), 1.0, 0.0).astype(BF16)
    row = lax.broadcasted_iota(jnp.int32, (256, 128), 0)
    col = lax.broadcasted_iota(jnp.int32, (256, 128), 1)
    half = jnp.where(row < 128, gz, 1 - gz)
    widen = jnp.where(((row & 127) < 64) & (col == (row & 127) + 64 * half), 1.0, 0.0).astype(BF16)

    row = lax.broadcasted_iota(jnp.int32, (96, 192), 0)
    col = lax.broadcasted_iota(jnp.int32, (96, 192), 1)
    y = sum(jnp.where(row >= 24 * i, 1, 0) for i in (1, 2, 3))
    group, at = (row >> 3) - 3 * y, row & 7
    back = jnp.where(at >= 3, 1, 0)
    corner = at >= 6
    component = jnp.where(corner, group, at - 3 * back)
    pz = jnp.where(corner, at - 6, back)
    px = jnp.where(corner | (group == 1), 1, 0)
    py = jnp.where(corner | (group == 2), 1, 0)
    source = 48 * pz + 16 * component + 8 * px + 2 * y + py
    shuffle = jnp.where(jnp.where(col >= 96, col - 96, col) == source, 1.0, 0.0).astype(BF16)

    wait_for(copies)
    high, low = halves(jnp.concatenate([raw[0:3].reshape(192, 128), other[0:3].reshape(192, 128)], axis=1))
    parted = jnp.dot(jnp.concatenate([high, low], axis=0).astype(BF16), parter, preferred_element_type=F32)
    parted = parted.reshape(2, 3, 8, 8, 256)
    pieces = []
    for x in range(4):
        near = parted[:, :, 2 * x : 2 * x + 2].reshape(2, 48, 256)
        pieces.append(
            jnp.concatenate([near[0, :, :128], near[0, :, 128:], near[1, :, :128], near[1, :, 128:]], axis=0)
        )
    stacked = jnp.concatenate(pieces, axis=1).astype(BF16)
    out_ref[0:96, :] = jnp.dot(shuffle, stacked, preferred_element_type=F32)

    levels = jnp.concatenate([raw[3, 0:4].reshape(32, 128), other[3, 0:4].reshape(32, 128)], axis=1)
    ratio = jnp.dot(levels.astype(BF16), widen, preferred_element_type=F32) / (DENSITY_LEVELS - 1)
    moduli = 0.05 + 0.95 * ratio * ratio * ratio
    for x in range(4):
        out_ref[96:104, 128 * x : 128 * x + 128] = moduli[8 * x : 8 * x + 8]
    half_ref[...] = out_ref[pl.ds(pl.multiple_of((PACK - PART) * gz, 8), PART), :]


def split(values):
    high = values.astype(BF16).astype(F32)
    return jnp.concatenate([high, values - high], axis=0).astype(BF16)


def roll_tiles(values, step):
    tiles = []
    for t in range(values.shape[1] // 128):
        tile = values[:, 128 * t : 128 * t + 128]
        lane = lax.broadcasted_iota(jnp.int32, tile.shape, 1)
        if step == 1:
            tiles.append(jnp.where(lane < 127, pltpu.roll(tile, 127, 1), 0.0))
        else:
            tiles.append(jnp.where(lane > 0, pltpu.roll(tile, 1, 1), 0.0))
    return tiles[0] if len(tiles) == 1 else jnp.concatenate(tiles, axis=1)


def hi_lo_weights(matrix, left, right):
    high, low = halves(matrix)
    col = lax.broadcasted_iota(jnp.int32, right.shape, 1)
    right_high = jnp.where(col % 16 < 8, right.astype(F32), 0.0).astype(BF16)
    rows = [
        jnp.dot(jnp.dot(left, part.astype(BF16), preferred_element_type=F32).astype(BF16), to, preferred_element_type=F32)
        for part, to in ((high, right), (low, right_high))
    ]
    return jnp.concatenate(rows, axis=0).astype(BF16)


def weights_kernel(fine_ref, coarse_ref, cards_ref, *book_refs):
    def card(name):
        return Part(cards_ref, CARDS, name)[...]

    matrices = {name: card(name) for name in ("restrict", "prolong", "shuffle")}
    for name, ref in (("fine", fine_ref), ("coarse", coarse_ref)):
        matrix = ref[...]
        row = lax.broadcasted_iota(jnp.int32, matrix.shape, 0)
        col = lax.broadcasted_iota(jnp.int32, matrix.shape, 1)
        diagonal = jnp.where(row == col, matrix, 0.0)
        matrices[name] = hi_lo_weights(matrix, card(name + "_out"), card(name + "_in"))
        matrices[name + "_diag"] = hi_lo_weights(diagonal, card(name + "_rows"), card(name + "_at"))
    for (places, _), book_ref in zip(BOOKS, book_refs, strict=True):
        for name in places:
            Part(book_ref, places, name)[...] = matrices[name]


def scaled(values, moduli):
    rows, lanes = values.shape
    return (values.reshape(rows // 8, 8, lanes) * moduli[None]).reshape(rows, lanes)


class Step(NamedTuple):
    row: int
    keep: float = 0.0
    gain: float = 0.0
    last: bool = False
    lead: bool = False
    tail: bool = False
    operand: bool = True
    residual: bool = True


def schedules():
    sigma = MID / HALF
    rhos = [1.0 / sigma]
    for _ in range(DEG - 1):
        rhos.append(1.0 / (2.0 * sigma - rhos[-1]))
    smooth = [(rhos[s + 1] * rhos[s], 2.0 * rhos[s + 1] / HALF) for s in range(DEG - 1)]
    o, c = SIDE, FAR

    def smoothing(sweeps, operand, residual):
        steps = []
        for at, (first, last, keep, gain) in enumerate(sweeps):
            final = at == len(sweeps) - 1
            reads = operand if final else range(sweeps[at + 1][0], sweeps[at + 1][1] + 1)
            sums = residual if final else range(sweeps[at + 1][0] + 1, sweeps[at + 1][1])
            for row in range(first, last):
                steps.append(Step(row, keep, gain, final, row == first, row == last - 1, row in reads, row in sums))
        return steps

    return {
        "start": [Step(row) for row in range(o - 3, o + 8)],
        "before": smoothing(
            [(o - 3 + s, o + 7 - s, *smooth[s]) for s in range(DEG - 1)], range(o, o + 5), range(o, o + 4)
        ),
        "leave": [Step(row) for row in range(o, o + 4)],
        "coarse_start": [Step(row) for row in range(c - 7, c + 11)],
        "coarse": smoothing(
            [(c - 7 + s, c + 10 - s, *smooth[s]) for s in range(DEG - 1)], range(c - 4, c + 8), range(0)
        ),
        "correct": [Step(row) for row in range(o - 4, o + 8)],
        "after": smoothing(
            [(o - 4, o + 7, 0.0, 1.0 / MID)] + [(o - 3 + s, o + 6 - s, *smooth[s]) for s in range(DEG - 1)],
            range(0),
            range(0),
        ),
    }


OWN_ROWS = range(SIDE, SIDE + OWN)


CHUNKS = [(256 * n, slice(256 * n, 256 * n + 256)) for n in range(4)]


def pushed(before, values):
    return jnp.concatenate([before, values[:, :128]], axis=1)


def store_fine(fine_x, y, lanes, values):
    for g in range(3):
        part = values[8 * g : 8 * g + 8]
        fine_x[y, 32 * g : 32 * g + 16, lanes] = split(part)
        fine_x[y, 32 * g + 16 : 32 * g + 32, lanes] = split(roll_tiles(part, 1))


def store_coarse(coarse_x, y, lanes, values):
    row = lax.broadcasted_iota(jnp.int32, values.shape, 0)
    further = pltpu.roll(roll_tiles(values, 1), 3, 0)
    coarse_x[y, :, lanes] = split(jnp.where(row < 3, values, jnp.where(row < 6, further, 0.0)))


def pipeline(prods, name, issue, finish):
    steps = schedules()[name]
    for t in range(len(steps) + AHEAD):
        if t < len(steps):
            issue(steps[t].row, prods[t % len(prods)], steps[t].lead)
        if t >= AHEAD:
            finish(steps[t - AHEAD], prods[(t - AHEAD) % len(prods)])


def fine_issue(fine_w, fine_x):
    def issue(y, prod, lead):
        for low, lanes in CHUNKS:
            there = slice(low + 128, low + 384)
            operand = jnp.concatenate(
                [
                    fine_x[y, :, lanes],
                    fine_x[y, 0:32, there],
                    fine_x[y, 64:96, there],
                    fine_x[y + 1, 0:64, lanes],
                    fine_x[y + 1, 0:32, there],
                ],
                axis=0,
            )
            if lead:
                weights = fine_w[...]
                weights = jnp.concatenate([weights[at : at + 32] for at in (32, 96, 160, 224)], axis=0)
                products = jnp.dot(weights, operand, preferred_element_type=F32)
                prod[32:64, lanes] = products[0:32] + products[64:96]
                prod[96:128, lanes] = products[32:64] + products[96:128]
                continue
            products = jnp.dot(fine_w[...], operand, preferred_element_type=F32)
            prod[:, lanes] = products[:128] + products[128:]

    return issue


def fine_finish(moduli, carry, use):
    def finish(now, prod):
        y = now.row
        before = [(jnp.zeros((16, 128), F32), jnp.zeros((8, 128), F32))] * 2
        for low, lanes in CHUNKS:
            m = moduli[y, :, lanes]
            sums = []
            for z in range(2):
                v = scaled(prod[64 * z + 32 * now.lead : 64 * z + 64, lanes], m)
                if now.lead:
                    v = jnp.concatenate([jnp.zeros((32, 256), F32), v], axis=0)
                if not now.lead:
                    old = carry[16 * z : 16 * z + 16, lanes]
                    along_x = pushed(before[z][0], v[24:40])
                    sums.append(
                        jnp.concatenate(
                            [v[0:8] + along_x[0:8] + old[0:8], v[8:16] + old[8:16], v[16:24] + along_x[8:16]], axis=0
                        )
                    )
                if not now.tail:
                    along_xy = pushed(before[z][1], v[56:64])
                    carry[16 * z : 16 * z + 16, lanes] = jnp.concatenate([v[40:48] + along_xy, v[48:56]], axis=0)
                before[z] = (v[24:40, 128:], v[56:64, 128:])
            if not now.lead:
                use(now, y, lanes, sums[0] + roll_tiles(sums[1], -1))

    return finish


def coarse_finish(moduli, carry, use):
    def finish(now, prod):
        y = now.row
        before = (jnp.zeros((8, 128), F32), jnp.zeros((8, 128), F32))
        for low, lanes in CHUNKS:
            v = prod[0:32, lanes]
            if moduli is not None:
                v = scaled(v, moduli[y, :, lanes])
            if not now.lead:
                sums = v[0:8] + pushed(before[0], v[8:16]) + carry[:, lanes]
            if not now.tail:
                carry[:, lanes] = v[16:24] + pushed(before[1], v[24:32])
            before = (v[8:16, 128:], v[24:32, 128:])
            if not now.lead:
                use(now, y, lanes, sums + roll_tiles(pltpu.roll(sums, 5, 0), -1))

    return finish


def smooth_fine(inverse, res, step, total, fine_x):
    def use(now, y, lanes, sums):
        if not (now.operand or now.residual or y in OWN_ROWS):
            return
        r = res[y, :, lanes] - sums
        d = now.gain * (inverse[y, :, lanes] * r)
        if now.keep:
            d = now.keep * step[y, :, lanes] + d
        if now.residual:
            res[y, :, lanes] = r
            step[y, :, lanes] = d
        if y in OWN_ROWS:
            total[y, :, lanes] = total[y, :, lanes] + d
        if now.operand:
            store_fine(fine_x, y, lanes, d)

    return use


def diag_issue(diag_w, moduli, count):
    def issue(y, prod, lead):
        spot = lax.broadcasted_iota(jnp.int32, (8, 256), 0)
        before = jnp.zeros((8, 128), F32)
        for low, lanes in CHUNKS:
            near = jnp.where(spot < 4, moduli[y, :, lanes], moduli[max(y - 1, 0), :, lanes])
            moved = pushed(before, near)
            before = near[:, 128:]
            around = jnp.where(spot % 4 < 2, near, moved)
            around = jnp.where(spot % 2 < 1, around, roll_tiles(around, -1))
            products = jnp.dot(diag_w[...], split(around), preferred_element_type=F32)
            prod[0:count, lanes] = products[:count] + products[count:]

    return issue


def clear_tail(ref, rows):
    def clear(y, _):
        ref[y, :, LANES:] = jnp.zeros((ref.shape[1], 128), BF16)
        return 0

    lax.fori_loop(0, rows, clear, 0)


def validity(place_ref, ahead):
    first, count = place_ref[1] * OWN - ahead, place_ref[3] * OWN

    def valid(y):
        return jnp.where((first + y >= 0) & (first + y < count), 1.0, 0.0).astype(F32)

    return valid


def before_kernel(place_ref, *refs):
    blocks = refs[:7]
    book_ref, outs = refs[7], refs[8:13]
    (book, res, step, total, fine_x, carry, load, moduli, inverse, note, moduli_rows, c_carry, sems, out_sems, *prods) = refs[13:]
    gx, gz = place_ref[0], place_ref[2]
    valid = validity(place_ref, SIDE)
    o = SIDE

    own, a, ax, za, zax, half, half_other = blocks
    lanes_of = [pl.ds(pl.multiple_of(x * 512, 512), 512) for x in (gx, 1 - gx)]
    side = 1 - 2 * gz
    spots = [(own, 0, 0), (a, -side, 0), (ax, -side, 1), (za, side, 0), (zax, side, 1)]
    fine_w, diag_w, restrict_w = [Part(book, BOOKS[0][0], name) for name in BOOKS[0][0]]
    copies = [(book_ref, book)]
    for i, (ref, offset, across) in enumerate(spots):
        copies.append((ref.at[96:104, :], moduli_rows.at[i]))
        for y in range(OWN):
            copies.append((ref.at[24 * y : 24 * y + 24, :], load.at[o + OWN * offset + y, :, lanes_of[across]]))
    for i, (ref, core) in enumerate([(half, gz), (half_other, 1 - gz)]):
        copies.append((ref.at[PART - 8 : PART, :], moduli_rows.at[5 + i]))
        for y in range(2):
            first = pl.multiple_of(24 * y + (PACK - PART - 48) * core, 8)
            copies.append((ref.at[pl.ds(first, 24), :], load.at[o + 2 * core + y, :, lanes_of[1]]))
    copies = fetched(copies, sems)
    clear_tail(fine_x, ROWS)
    carry[...] = jnp.zeros_like(carry)
    wait_for(copies)
    own_rows = jnp.where(jnp.full((8, 512), gz) == 1, moduli_rows[5], moduli_rows[6])
    for rows, offset, across in [(moduli_rows[i], *spot[1:]) for i, spot in enumerate(spots)] + [(own_rows, 0, 1)]:
        for y in range(OWN):
            moduli[o + OWN * offset + y, :, lanes_of[across]] = jnp.broadcast_to(rows[y : y + 1], (8, 512))
    leaving = fetched([(load, outs[0]), (moduli, outs[1])], out_sems)

    def start(now, prod):
        y = now.row
        ok = valid(y)
        for low, lanes in CHUNKS:
            inv = ok / (prod[0:24, lanes] + (1.0 - ok))
            r = load[y, :, lanes]
            d = inv * r * (1.0 / MID)
            inverse[y, :, lanes] = inv
            res[y, :, lanes] = r
            step[y, :, lanes] = d
            if y in OWN_ROWS:
                total[y, :, lanes] = d
            store_fine(fine_x, y, lanes, d)

    pipeline(prods, "start", diag_issue(diag_w, moduli, 24), start)
    leaving += fetched([(inverse, outs[2])], out_sems, len(leaving))
    issue = fine_issue(fine_w, fine_x)
    use = smooth_fine(inverse, res, step, total, fine_x)
    pipeline(prods, "before", issue, fine_finish(moduli, carry, use))
    leaving += fetched([(total.at[o : o + OWN], outs[3])], out_sems, len(leaving))

    carry[...] = jnp.zeros_like(carry)

    def store_left(y, lanes, left):
        for g in range(3):
            fine_x[y, 16 * g : 16 * g + 16, lanes] = split(left[8 * g : 8 * g + 8])

    def leave(now, y, lanes, sums):
        store_left(y, lanes, res[y, :, lanes] - sums)

    pipeline(prods, "leave", issue, fine_finish(moduli, carry, leave))
    for low, lanes in CHUNKS:
        last = carry[0:16, lanes] + roll_tiles(carry[16:32, lanes], -1)
        last = jnp.concatenate([last, jnp.zeros((8, 256), F32)], axis=0)
        store_left(o + OWN, lanes, -last * valid(o + OWN))

    c_carry[...] = jnp.zeros_like(c_carry)
    for j in range(OWN + 1):
        prod = prods[j % len(prods)]
        for low, lanes in CHUNKS:
            prod[0:32, lanes] = jnp.dot(restrict_w[...], fine_x[o + j, 0:48, lanes], preferred_element_type=F32)

        def keep(now, y, lanes, sums, j=j):
            note[3 * j : 3 * j + 3, lanes] = sums[0:3]

        coarse_finish(None, c_carry, keep)(Step(o + j), prod)
    for y in range(OWN):
        note[16 + y : 17 + y, :] = moduli[o + y, 0:1, :]
    leaving += fetched([(note, outs[4])], out_sems, len(leaving))
    wait_for(leaving)


def coarse_operand(coarse_x, y, low, lanes):
    there = slice(low + 128, low + 384)
    return jnp.concatenate(
        [coarse_x[y, :, lanes], coarse_x[y, :, there], coarse_x[y + 1, :, lanes], coarse_x[y + 1, :, there]], axis=0
    )


def coarse_kernel(place_ref, *refs):
    note, m1, zm1, m2, zm2, near_moduli, book_ref, fix = refs[:8]
    book, moduli, notes, c_inverse, c_res, c_step, c_total, coarse_x, c_carry, sems, *prods = refs[8:]
    gz = place_ref[2]
    o, c = SIDE, FAR
    valid = validity(place_ref, FAR)
    side = 1 - 2 * gz

    spots = [(note, 0), (m1, -side), (zm1, side), (m2, -2 * side), (zm2, 2 * side)]
    copies = [(ref, notes.at[i]) for i, (ref, _) in enumerate(spots)]
    copies.append((near_moduli, moduli.at[c - o : c - o + ROWS]))
    copies.append((book_ref, book))
    coarse_w, diag_w = [Part(book, BOOKS[1][0], name) for name in BOOKS[1][0]]
    copies = fetched(copies, sems)
    clear_tail(coarse_x, C_ROWS)
    c_carry[...] = jnp.zeros_like(c_carry)
    c_res[...] = jnp.zeros_like(c_res)
    wait_for(copies)
    for i, (_, offset) in enumerate(spots):
        at = c + OWN * offset
        if i >= 3:
            for y in range(OWN):
                moduli[at + y] = jnp.broadcast_to(notes[i, 16 + y : 17 + y, :], (8, LANES))
        for y in range(OWN + 1):
            c_res[at + y, 0:3, :] = c_res[at + y, 0:3, :] + notes[i, 3 * y : 3 * y + 3, :]

    def start(now, prod):
        y = now.row
        ok = valid(y)
        for low, lanes in CHUNKS:
            used = lax.broadcasted_iota(jnp.int32, (8, 256), 0) < 3
            inv = jnp.where(used, ok / (prod[0:8, lanes] + (1.0 - ok)), 0.0)
            d = inv * c_res[y, :, lanes] * (1.0 / MID)
            c_inverse[y, :, lanes] = inv
            c_step[y, :, lanes] = d
            c_total[y, :, lanes] = d
            store_coarse(coarse_x, y, lanes, d)

    pipeline(prods, "coarse_start", diag_issue(diag_w, moduli, 8), start)

    def issue(y, prod, lead):
        for low, lanes in CHUNKS:
            products = jnp.dot(coarse_w[...], coarse_operand(coarse_x, y, low, lanes), preferred_element_type=F32)
            prod[0:32, lanes] = products[:32] + products[32:]

    def smooth(now, y, lanes, sums):
        if not (now.operand or now.residual):
            return
        r = c_res[y, :, lanes] - sums
        d = now.keep * c_step[y, :, lanes] + now.gain * (c_inverse[y, :, lanes] * r)
        so_far = c_total[y, :, lanes] + d
        if now.residual:
            c_res[y, :, lanes] = r
            c_step[y, :, lanes] = d
            c_total[y, :, lanes] = so_far
        store_coarse(coarse_x, y, lanes, so_far if now.last else d)

    pipeline(prods, "coarse", issue, coarse_finish(moduli, c_carry, smooth))
    wait_for(fetched([(coarse_x.at[c - o : c - o + ROWS + 1], fix)], sems))


def after_kernel(place_ref, *refs):
    fix_sent, s0, s1, zs1, load_sent, moduli_sent, inverse_sent, book_ref, out_ref = refs[:9]
    (book, res, step, total, fine_x, carry, moduli, inverse, fix, sems, *prods) = refs[9:]
    gx, gz = place_ref[0], place_ref[2]
    o = SIDE
    side = 1 - 2 * gz

    fine_w, prolong_w, shuffle = [Part(book, BOOKS[2][0], name) for name in BOOKS[2][0]]
    copies = [(fix_sent, fix), (load_sent, res), (book_ref, book)]
    for ref, offset in [(s0, 0), (s1, -side), (zs1, side)]:
        copies.append((ref, total.at[pl.ds(o + OWN * offset, OWN)]))
    first = fetched(copies, sems)
    second = fetched([(inverse_sent, inverse), (moduli_sent, moduli)], sems, len(first))
    clear_tail(fine_x, ROWS)
    carry[...] = jnp.zeros_like(carry)
    wait_for(first)

    def correct_issue(y, prod, lead):
        for low, lanes in CHUNKS:
            prod[0:24, lanes] = jnp.dot(
                prolong_w[...], coarse_operand(fix, y, low, lanes), preferred_element_type=F32
            )

    def correct(now, prod):
        y = now.row
        for low, lanes in CHUNKS:
            corrected = total[y, :, lanes] + prod[0:24, lanes]
            if y in OWN_ROWS:
                total[y, :, lanes] = corrected
            store_fine(fine_x, y, lanes, corrected)

    pipeline(prods, "correct", correct_issue, correct)
    wait_for(second)
    use = smooth_fine(inverse, res, step, total, fine_x)
    pipeline(prods, "after", fine_issue(fine_w, fine_x), fine_finish(moduli, carry, use))

    row = lax.broadcasted_iota(jnp.int32, (256, 128), 0)
    col = lax.broadcasted_iota(jnp.int32, (256, 128), 1)
    weave = (row == 128 * (col % 2) + 64 * gz + col // 2).astype(F32).astype(BF16)
    lanes = pl.ds(pl.multiple_of(gx * 512, 512), 512)
    high, low = halves(total[o : o + OWN, :, lanes].reshape(96, 512))
    pieces = []
    for part in (high, low):
        back = lax.dot_general(
            shuffle[...][:, 0:96], part.astype(BF16), (((0,), (0,)), ((), ())), preferred_element_type=F32
        )
        for x in range(4):
            near = back[:, 128 * x : 128 * x + 128]
            pieces.append(jnp.concatenate([near[0:48], near[48:96]], axis=1))
    woven = jnp.dot(jnp.concatenate(pieces, axis=0).astype(BF16), weave, preferred_element_type=F32)
    woven = woven[:192] + woven[192:]
    for x in range(4):
        out_ref[:, 2 * x : 2 * x + 2] = woven[48 * x : 48 * x + 48].reshape(3, 2, 8, 128)


def per_device(adjoint_load, levels, fine_stiffness, coarse_stiffness):
    count = lax.axis_size("gy")
    place = jnp.stack(
        [lax.axis_index("gx"), lax.axis_index("gy"), lax.axis_index("gz"), jnp.int32(count)]
    ).astype(jnp.int32)

    def swap(value, axis):
        return lax.ppermute(value, axis, [(0, 1), (1, 0)])

    def sided(value, steps, across=False):
        pairs = []
        for gx in range(2):
            for i in range(count - steps):
                low, high = 2 * (gx * count + i), 2 * (gx * count + i + steps)
                other = 2 * count * (1 - 2 * gx) if across else 0
                pairs += [(low, high + other), (high + 1, low + other + 1)]
        return lax.ppermute(value, ("gx", "gy", "gz"), pairs)

    whole = pl.BlockSpec(memory_space=pltpu.VMEM)
    there = pl.BlockSpec(memory_space=pl.ANY)
    scalars = pl.BlockSpec(memory_space=pltpu.SMEM)

    def pack(raw, other):
        return pl.pallas_call(
            pack_kernel,
            out_shape=[jax.ShapeDtypeStruct((rows, 512), F32) for rows in (PACK, PART)],
            in_specs=[scalars, there, there],
            out_specs=[whole] * 2,
            scratch_shapes=[pltpu.VMEM(raw.shape, F32)] * 2 + [pltpu.SemaphoreType.DMA((2,))],
            compiler_params=pltpu.CompilerParams(vmem_limit_bytes=8 * 1024 * 1024),
            name="pack",
        )(place, raw, other)

    book, coarse_book, after_book = pl.pallas_call(
        weights_kernel,
        out_shape=[jax.ShapeDtypeStruct((rows, 256), BF16) for _, rows in BOOKS],
        in_specs=[whole] * 3,
        out_specs=[whole] * 3,
        compiler_params=pltpu.CompilerParams(vmem_limit_bytes=8 * 1024 * 1024),
        name="weights",
    )(fine_stiffness, coarse_stiffness, cards())

    _, x_nodes, y_nodes, z_nodes = adjoint_load.shape
    room = [(0, whole_size - size) for whole_size, size in zip((x_nodes, y_nodes, z_nodes), levels.shape, strict=True)]
    raw = jnp.concatenate([adjoint_load, jnp.pad(levels, room).astype(F32)[None]], axis=0)
    own, half = pack(raw, swap(raw, "gz"))
    a, ax = sided(own, 1), sided(own, 1, True)
    half_x = swap(half, "gx")
    blocks = [own, a, ax, swap(lax.optimization_barrier((a, book))[0], "gz"), swap(ax, "gz"), half_x, swap(half_x, "gz")]

    def held(count, height=24):
        return pltpu.VMEM((count, height, LANES), F32)

    fine_scratch = [
        held(ROWS),
        held(ROWS),
        held(ROWS),
        pltpu.VMEM((ROWS + 1, 96, WIDE), BF16),
        pltpu.VMEM((32, LANES), F32),
    ]
    prods = [pltpu.VMEM((128, LANES), F32)] * (AHEAD + 1)
    limit = pltpu.CompilerParams(vmem_limit_bytes=24 * 1024 * 1024)
    load, moduli, inverse, smoothed, note = pl.pallas_call(
        before_kernel,
        out_shape=[
            jax.ShapeDtypeStruct(shape, F32)
            for shape in [(ROWS, 24, LANES), (ROWS, 8, LANES), (ROWS, 24, LANES), (OWN, 24, LANES), (NOTE, LANES)]
        ],
        in_specs=[scalars] + [there] * 8,
        out_specs=[there] * 5,
        scratch_shapes=[pltpu.VMEM(book.shape, BF16), *fine_scratch]
        + [
            held(ROWS),
            held(ROWS, 8),
            held(ROWS),
            pltpu.VMEM((NOTE, LANES), F32),
            pltpu.VMEM((7, 8, 512), F32),
            pltpu.VMEM((8, LANES), F32),
            pltpu.SemaphoreType.DMA((5 * (OWN + 1) + 7,)),
            pltpu.SemaphoreType.DMA((5,)),
            *prods,
        ],
        compiler_params=limit,
        name="before",
    )(place, *blocks, book)

    m1, m2 = sided(note, 1), sided(note, 2)
    s1 = sided(smoothed, 1)
    fix = pl.pallas_call(
        coarse_kernel,
        out_shape=jax.ShapeDtypeStruct((ROWS + 1, 16, WIDE), BF16),
        in_specs=[scalars] + [there] * 7,
        out_specs=there,
        scratch_shapes=[
            pltpu.VMEM(coarse_book.shape, BF16),
            held(C_ROWS, 8),
            pltpu.VMEM((5, NOTE, LANES), F32),
            held(C_ROWS, 8),
            held(C_ROWS + 1, 8),
            held(C_ROWS, 8),
            held(C_ROWS, 8),
            pltpu.VMEM((C_ROWS + 1, 16, WIDE), BF16),
            pltpu.VMEM((8, LANES), F32),
            pltpu.SemaphoreType.DMA((7,)),
            *prods,
        ],
        compiler_params=limit,
        cost_estimate=pl.CostEstimate(flops=4 * 10**9, bytes_accessed=4 * 10**7, transcendentals=0),
        name="coarse",
    )(place, note, m1, swap(m1, "gz"), m2, swap(m2, "gz"), moduli, coarse_book)
    return pl.pallas_call(
        after_kernel,
        out_shape=jax.ShapeDtypeStruct(adjoint_load.shape, F32),
        in_specs=[scalars] + [there] * 8,
        out_specs=whole,
        scratch_shapes=[
            pltpu.VMEM(after_book.shape, BF16),
            *fine_scratch,
            held(ROWS, 8),
            held(ROWS),
            pltpu.VMEM((ROWS + 1, 16, WIDE), BF16),
            pltpu.SemaphoreType.DMA((8,)),
            *prods,
        ],
        compiler_params=limit,
        name="after",
    )(place, fix, smoothed, s1, swap(s1, "gz"), load, moduli, inverse, after_book)


def solution(mesh):
    return jax.shard_map(
        per_device,
        mesh=mesh,
        in_specs=(P(None, "gx", "gy", "gz"), P("gx", "gy", "gz"), P(), P()),
        out_specs=P(None, "gx", "gy", "gz"),
        check_vma=False,
    )
```
